32 devices in a mesh: replica: 2 (over y), tensor: 2 (over x), group: 8 (over z, core).
Axes of the slice: x: 2, y: 2, z: 4, core: 2. Of those that a mesh axis runs over, the one named last changes fastest.
Arguments:
- hidden_in: bfloat16 [16, 512, 5120], P(('replica', 'group'), None, 'tensor'), parts along dimension 0, may hold values from -6 to 6
- ln_gain: bfloat16 [5120], P('tensor'), may hold values from 0.25 to 1.75
- wq: bfloat16 [5120, 4096], P(None, 'tensor'), may hold values from -0.078125 to 0.078125
- wk: bfloat16 [5120, 1024], P(None, 'tensor'), may hold values from -0.078125 to 0.078125
- wv: bfloat16 [5120, 1024], P(None, 'tensor'), may hold values from -0.078125 to 0.078125
- q_gain: bfloat16 [128], replicated, may hold values from 0.7 to 6
- key_norm_gain: bfloat16 [128], replicated, may hold values from 0.7 to 6
- wo: bfloat16 [4096, 5120], P('tensor'), may hold values from -0.5 to 0.5
- prompt_spans: int32 [6], P('replica'), parts along dimension 0, may hold values from 1 to 4, 8 in all
- span_source: int32 [16], P('replica'), parts along dimension 0, may hold values from 0 to 7, each once
- span_target: int32 [16], P('replica'), parts along dimension 0, may hold values from 0 to 7, each once
- page_slot: int32 [64], P('replica'), parts along dimension 0, may hold values from 0 to 31, each once
Outputs:
- mixed: bfloat16 [16, 512, 5120], P(('replica', 'group'), None, 'tensor'), parts along dimension 0
- kv_pages: bfloat16 [64, 2, 128, 1024], P(('replica', 'group')), parts along dimension 0
The draws below stay inside these ranges and needn't reach their ends.
There are 2 independent parts, one for each index of `replica`. The reference program is written for one: setup_inputs(seed, part) draws one part's arguments, and reference() takes and returns one part's arrays. A program takes and returns all parts, laid end to end along the dimension named above; an argument that names none is the same for every part. Nothing has to cross between parts.
Inputs may be any that keep to these rules, and one draw needn't show every extreme that they name: `prompt_spans`: the lengths sum to 8; the longest prompt has exactly 4 spans. `span_source`: a permutation of the slots. `span_target`: a permutation of the slots. `page_slot`: a permutation of the page slots.
All inputs are finite; a program needn't handle non-finite values.
Results may differ from the reference program's by a relative error of at most 0.011.
The reference program's roundings to bfloat16 on the way (of `normed`, `weights` and `attended`) count: a program that leaves them out, or rounds other values in their place, can miss the bound.
Values may be sent and summed in bfloat16 or wider, within the bound.
No kernel may reach another device: no remote copies, remote signals or barrier semaphores. Data moves between devices by JAX's collectives and lax.ppermute only.
A program may use at most 576 MiB of HBM per device.

```python
import math
import jax
import jax.numpy as jnp
import numpy as np
from jax import lax

MODEL_WIDTH = 5120
QUERY_HEADS_HALF = 32
KEY_VALUE_HEADS = 8
HEAD_SIZE = 128
SPAN_ROWS = 512
PAGE_ROWS = 128
PROMPTS = 3
PPC = 4
SPAN_COUNT = 8
MOST = 4
N_TENSOR = 2


def draw_q_gain(key, part):
    key = jax.random.fold_in(key, 11)
    return jax.random.uniform(key, (HEAD_SIZE,), jnp.float32, 0.7, 1.6).astype(jnp.bfloat16)


def draw_key_norm_gain(key, part):
    key = jax.random.fold_in(key, 23)
    return jax.random.uniform(key, (HEAD_SIZE,), jnp.float32, 0.7, 1.6).astype(jnp.bfloat16)


def raised(values, own_key, source, target, shards_of, factor):
    owner, partner = [(jnp.arange(values.shape[axis_at]) // (values.shape[axis_at] // shards_of)).reshape([-1 if axis == axis_at else 1 for axis in range(values.ndim)]) for axis_at in (source, target)]
    chosen = jax.random.permutation(own_key, shards_of)[partner]
    strong = (owner == chosen) | (owner == (partner + shards_of // 2) % shards_of)
    return jnp.where(strong, factor * values, values)


def level_of(key, shape, shards, low, largest):
    factor_of, own = 1.0, jax.random.fold_in(key, 6)
    for dim, shards_of in shards:
        heights = jnp.exp(jax.random.uniform(jax.random.fold_in(own, dim), (shards_of,), jnp.float32, low / len(shards), largest / len(shards)))
        factor_of = factor_of * jnp.repeat(heights, shape[dim] // shards_of).reshape([-1 if axis == dim else 1 for axis in range(len(shape))])
    return factor_of


def length_profile(count, total, reach, lean):
    loads = [(1 << 20) // math.isqrt(standing ** lean) + 1 for standing in range(2, count + 1)]
    spare, given = total - reach - (count - 1), [1] * (count - 1)
    while spare > 0:
        free = [i for i in range(count - 1) if given[i] < reach]
        pool, remaining = sum([loads[i] for i in free]), spare
        for i in free:
            more = min(reach - given[i], max(1, remaining * loads[i] // pool), spare)
            given[i] = given[i] + more
            spare = spare - more
    return np.array([reach] + given)


def uneven_parts(key, amount, total, bound, skew):
    if amount == 2:
        one = jax.random.randint(key, (), max(1, total - bound), min(bound, total - 1) + 1)
        return jnp.stack([one, total - one])
    sizes = jnp.asarray(length_profile(amount, total, bound, skew), jnp.int32)
    pairs = (amount - 1) // 2
    donor, sink = sizes[1:1 + 2 * pairs:2], sizes[2:2 + 2 * pairs:2]
    margin = jnp.minimum(donor - 1, bound - sink)
    shifted = jax.random.randint(jax.random.fold_in(key, 1), (pairs,), 0, 1 << 20) % (margin + 1)
    sizes = sizes.at[1:1 + 2 * pairs:2].set(donor - shifted).at[2:2 + 2 * pairs:2].set(sink + shifted)
    return sizes[jax.random.permutation(jax.random.fold_in(key, 2), amount)]


def gaussian(own_key, extent, width, limit, cuts=(), kind=jnp.bfloat16):
    factor_of = level_of(own_key, extent, cuts, -0.22, 0.18) if cuts else 1.0
    entries = jax.random.normal(own_key, extent, jnp.float32) * width * factor_of
    return jnp.minimum(jnp.maximum(entries, -limit), limit).astype(kind)


def noise_with(own_key, dims, deviation, limit, split, heavy, held_as=jnp.bfloat16):
    result = deviation * jax.random.normal(own_key, dims, jnp.float32)
    if split:
        result = result * level_of(own_key, dims, split, -0.22, 0.18)
    return jnp.clip(raised(result, jax.random.fold_in(own_key, 3), *heavy), -limit, limit).astype(held_as)


def setup_inputs(seed: int = 0, part: int = 0) -> dict:
    key_of = jax.random.split(jax.random.key(seed), 13)
    part_splits = jax.random.split(jax.random.fold_in(key_of[12], part), 13)
    return {
        "hidden_in": gaussian(part_splits[0], (SPAN_COUNT, SPAN_ROWS, MODEL_WIDTH), 1.0, 6.0, ((0, 8), (2, 2))),
        "ln_gain": jnp.clip(1.0 + 0.15 * jax.random.normal(key_of[1], (MODEL_WIDTH,), jnp.float32), 0.25, 1.75).astype(jnp.bfloat16),
        "wq": gaussian(key_of[2], (MODEL_WIDTH, QUERY_HEADS_HALF * HEAD_SIZE), MODEL_WIDTH ** -0.5, 0.078125, ((1, 2),)),
        "wk": gaussian(key_of[3], (MODEL_WIDTH, KEY_VALUE_HEADS * HEAD_SIZE), MODEL_WIDTH ** -0.5, 0.078125, ((1, 2),)),
        "wv": gaussian(key_of[4], (MODEL_WIDTH, KEY_VALUE_HEADS * HEAD_SIZE), MODEL_WIDTH ** -0.5, 0.078125, ((1, 2),)),
        "q_gain": draw_q_gain(jax.random.fold_in(key_of[12], 71), part),
        "key_norm_gain": draw_key_norm_gain(jax.random.fold_in(key_of[12], 71), part),
        "wo": noise_with(key_of[7], (QUERY_HEADS_HALF * HEAD_SIZE, MODEL_WIDTH), (QUERY_HEADS_HALF * HEAD_SIZE // 16) ** -0.5, 0.5, ((0, 2),), (0, 1, 2, 2.0)),
        "prompt_spans": uneven_parts(part_splits[8], PROMPTS, SPAN_COUNT, MOST, 1).astype(jnp.int32),
        "span_source": jax.random.permutation(part_splits[9], SPAN_COUNT).astype(jnp.int32),
        "span_target": jax.random.permutation(part_splits[10], SPAN_COUNT).astype(jnp.int32),
        "page_slot": jax.random.permutation(part_splits[11], SPAN_COUNT * PPC).astype(jnp.int32),
    }


epsilon = 1e-06
rope_base = 1000000.0

def norm_per_head(values, gain):
    mean_sq = lax.optimization_barrier(jnp.mean(values * values, axis=-1, keepdims=True))
    return values * lax.rsqrt(mean_sq + epsilon) * gain.astype(jnp.float32)

def apply_rotary(values, token_positions):
    half_width = values.shape[-1] // 2
    freqs = jnp.power(jnp.float32(rope_base), -jnp.arange(half_width, dtype=jnp.float32) * 2.0 / values.shape[-1])
    angles = token_positions[:, None] * freqs[None, :]
    cosine = jnp.cos(angles)[:, None, :]
    sine = jnp.sin(angles)[:, None, :]
    first_half = values[..., :half_width]
    second_half = values[..., half_width:]
    return jnp.concatenate([first_half * cosine - second_half * sine, second_half * cosine + first_half * sine], axis=-1)

def span_tables(prompt_spans, span_ids):
    ends = jnp.cumsum(prompt_spans, dtype=jnp.int32)
    prompt_of = lax.optimization_barrier(jnp.sum((span_ids[:, None] >= ends[None, :]).astype(jnp.int32), axis=1, dtype=jnp.int32))
    starts = ends - prompt_spans
    onehot_table = (prompt_of[:, None] == jnp.arange(prompt_spans.shape[0], dtype=jnp.int32)[None, :]).astype(jnp.int32)
    start_of = lax.optimization_barrier(jnp.sum(onehot_table * starts[None, :], axis=1, dtype=jnp.int32))
    return (prompt_of, start_of)

def reference(hidden_in, ln_gain, wq, wk, wv, q_gain, key_norm_gain, wo, prompt_spans, span_source, span_target, page_slot):
    order = jnp.arange(SPAN_COUNT, dtype=jnp.int32)
    prompt_of, start_of = span_tables(prompt_spans, order)
    ordered = hidden_in[span_source]
    widened = ordered.astype(jnp.float32)
    mean_sq = lax.optimization_barrier(jnp.mean(widened * widened, axis=-1, keepdims=True))
    normed = (widened * lax.rsqrt(mean_sq + epsilon) * ln_gain.astype(jnp.float32)).astype(jnp.bfloat16)
    flattened_rows = normed.reshape(SPAN_COUNT * SPAN_ROWS, MODEL_WIDTH)
    token_positions = ((order - start_of)[:, None] * SPAN_ROWS + jnp.arange(SPAN_ROWS, dtype=jnp.int32)[None, :]).reshape(-1).astype(jnp.float32)
    query_lin = jnp.dot(flattened_rows, wq, preferred_element_type=jnp.float32).reshape(-1, QUERY_HEADS_HALF, HEAD_SIZE)
    key_linear_weight = jnp.dot(flattened_rows, wk, preferred_element_type=jnp.float32).astype(jnp.bfloat16)
    every_value_row = jnp.dot(flattened_rows, wv, preferred_element_type=jnp.float32).astype(jnp.bfloat16).reshape(-1, KEY_VALUE_HEADS, HEAD_SIZE)
    queries = apply_rotary(norm_per_head(query_lin, q_gain), token_positions).astype(jnp.bfloat16)
    key_tensor = apply_rotary(norm_per_head(key_linear_weight.astype(jnp.float32).reshape(-1, KEY_VALUE_HEADS, HEAD_SIZE), key_norm_gain), token_positions).astype(jnp.bfloat16)
    row_prompt = jnp.repeat(prompt_of, SPAN_ROWS)
    row_index = jnp.arange(SPAN_COUNT * SPAN_ROWS, dtype=jnp.int32)
    allowed = (row_prompt[:, None] == row_prompt[None, :]) & (row_index[None, :] <= row_index[:, None])
    score_scale = 1.0 / math.sqrt(HEAD_SIZE)

    def one_head(head_number):
        key_value_head = head_number // (QUERY_HEADS_HALF // KEY_VALUE_HEADS)
        query_head = lax.dynamic_index_in_dim(queries, head_number, 1, keepdims=False)
        key_head = lax.dynamic_index_in_dim(key_tensor, key_value_head, 1, keepdims=False)
        value_head = lax.dynamic_index_in_dim(every_value_row, key_value_head, 1, keepdims=False)
        scores = jnp.dot(query_head, key_head.T, preferred_element_type=jnp.float32) * score_scale
        scores = jnp.where(allowed, scores, -jnp.inf)
        row_max = lax.optimization_barrier(jnp.max(scores, axis=1, keepdims=True))
        weights = jnp.exp(scores - row_max)
        weights_sum = lax.optimization_barrier(jnp.sum(weights, axis=1, keepdims=True))
        mixed_head = jnp.dot(weights.astype(jnp.bfloat16), value_head, preferred_element_type=jnp.float32) / weights_sum
        return mixed_head.astype(jnp.bfloat16)
    heads_out = lax.map(one_head, jnp.arange(QUERY_HEADS_HALF, dtype=jnp.int32))
    attended = jnp.transpose(heads_out, (1, 0, 2)).reshape(-1, QUERY_HEADS_HALF * HEAD_SIZE)
    head_cols = QUERY_HEADS_HALF * HEAD_SIZE // N_TENSOR
    attn_split = attended.reshape(-1, N_TENSOR, head_cols).transpose(1, 0, 2)
    wo_split = wo.reshape(N_TENSOR, head_cols, MODEL_WIDTH)

    def add_partial(summed, pair):
        part_attn, part_wo = pair
        term = jnp.dot(part_attn, part_wo, preferred_element_type=jnp.float32).astype(jnp.bfloat16)
        term = lax.optimization_barrier(term)
        return (summed + term.astype(jnp.float32), None)
    summed, _ = lax.scan(add_partial, jnp.zeros((SPAN_COUNT * SPAN_ROWS, MODEL_WIDTH), jnp.float32), (attn_split, wo_split))
    out_ordered = (widened.reshape(-1, MODEL_WIDTH) + summed).astype(jnp.bfloat16).reshape(SPAN_COUNT, SPAN_ROWS, MODEL_WIDTH)
    mixed = jnp.zeros_like(hidden_in).at[span_target].set(out_ordered)
    paged_key_cache = key_tensor.reshape(SPAN_COUNT * (SPAN_ROWS // PAGE_ROWS), PAGE_ROWS, KEY_VALUE_HEADS * HEAD_SIZE)
    paged_value_cache = every_value_row.reshape(SPAN_COUNT * (SPAN_ROWS // PAGE_ROWS), PAGE_ROWS, KEY_VALUE_HEADS * HEAD_SIZE)
    stacked = jnp.stack([paged_key_cache, paged_value_cache], axis=1)
    kv_pages = jnp.zeros_like(stacked).at[page_slot].set(stacked)
    return (mixed, kv_pages)
```

```python
import functools
import math

import jax
import jax.numpy as jnp
from jax import lax
from jax.experimental import pallas as pl
from jax.experimental.pallas import tpu as pltpu
from jax.sharding import PartitionSpec as P

PAGE_ROWS = 128
epsilon = 1e-06
rope_base = 1000000.0
very_negative = -1e30
VMEM_BYTES = 48 * 1024 * 1024
PARTS = 2


def params():
    return pltpu.CompilerParams(vmem_limit_bytes=VMEM_BYTES)


def cost(flops, moved, transcendentals=0):
    return pl.CostEstimate(
        flops=int(flops), bytes_accessed=int(moved), transcendentals=int(transcendentals)
    )


class Layout:
    def __init__(self, spans, pages):
        self.start = 0
        self.slot = self.start + spans
        self.offset = self.slot + spans
        self.from_slot = self.offset + spans
        self.page = self.from_slot + spans
        self.group_rank = self.page + pages
        self.tensor_rank = self.group_rank + 1
        self.length = self.tensor_rank + 1


def tables_kernel(lay, spans, pages, ranks, prompt_spans, source, target, page_slot, out):
    out[lay.group_rank] = ranks[0]
    out[lay.tensor_rank] = ranks[1]
    for k in range(spans):
        start = jnp.int32(0)
        begin = jnp.int32(0)
        for p in range(prompt_spans.shape[0]):
            start = jnp.where(begin <= k, begin, start)
            begin = begin + prompt_spans[p]
        slot = source[k]
        out[lay.start + k] = start
        out[lay.slot + k] = slot
        out[lay.offset + slot] = k - start
        out[lay.from_slot + target[k]] = slot
    for p in range(pages):
        out[lay.page + page_slot[p]] = jnp.int32(p)


def make_tables(lay, spans, pages, ranks, prompt_spans, source, target, page_slot):
    smem = pl.BlockSpec(memory_space=pltpu.SMEM)
    return pl.pallas_call(
        functools.partial(tables_kernel, lay, spans, pages),
        out_shape=jax.ShapeDtypeStruct((lay.length,), jnp.int32),
        in_specs=[smem] * 5,
        out_specs=smem,
        name="tables",
    )(ranks, prompt_spans, source, target, page_slot)


def head_norm_rope(u, gain, cosine, sine):
    mean_sq = jnp.mean(u * u, axis=-1, keepdims=True)
    u = u * lax.rsqrt(mean_sq + epsilon) * gain
    half = u.shape[-1] // 2
    return u * cosine + pltpu.roll(u, half, 1) * sine


def kv_kernel(x, gain, wk, wv, kgain, cosine, sine, normed, kv):
    head = kgain.shape[1]

    @pl.when(pl.program_id(0) == 0)
    def _():
        wide = x[...].astype(jnp.float32)
        mean_sq = jnp.mean(wide * wide, axis=-1, keepdims=True)
        normed[...] = (
            wide * lax.rsqrt(mean_sq + epsilon) * gain[...].astype(jnp.float32)
        ).astype(jnp.bfloat16)

    rows = normed[...]
    keys = jnp.dot(rows, wk[...], preferred_element_type=jnp.float32).astype(jnp.bfloat16)
    gains = kgain[...].astype(jnp.float32)
    for h in range(wk.shape[1] // head):
        u = keys[:, h * head : (h + 1) * head].astype(jnp.float32)
        kv[0, :, h * head : (h + 1) * head] = head_norm_rope(
            u, gains, cosine[...], sine[...]
        ).astype(jnp.bfloat16)
    kv[1] = jnp.dot(rows, wv[...], preferred_element_type=jnp.float32).astype(jnp.bfloat16)


def make_kv(x, gain, wk, wv, kgain, cosine, sine):
    rows, width = x.shape
    cols = wk.shape[1]
    tile = 256 if cols % 256 == 0 else cols
    head = kgain.shape[1]
    fixed = lambda n: (0, 0)
    return pl.pallas_call(
        kv_kernel,
        grid=(cols // tile,),
        in_specs=[
            pl.BlockSpec((rows, width), fixed),
            pl.BlockSpec((1, width), fixed),
            pl.BlockSpec((width, tile), lambda n: (0, n)),
            pl.BlockSpec((width, tile), lambda n: (0, n)),
            pl.BlockSpec((1, head), fixed),
            pl.BlockSpec((rows, head), fixed),
            pl.BlockSpec((rows, head), fixed),
        ],
        out_specs=[
            pl.BlockSpec((rows, width), fixed),
            pl.BlockSpec((2, rows, tile), lambda n: (0, 0, n)),
        ],
        out_shape=[
            jax.ShapeDtypeStruct((rows, width), jnp.bfloat16),
            jax.ShapeDtypeStruct((2, rows, cols), jnp.bfloat16),
        ],
        compiler_params=params(),
        cost_estimate=cost(4 * rows * width * cols, 4 * width * cols + 4 * rows * width),
        name="keys_values",
    )(x, gain, wk, wv, kgain, cosine, sine)


def q_kernel(normed, wq, qgain, cosine, sine, out):
    head = qgain.shape[1]
    lin = jnp.dot(normed[...], wq[...], preferred_element_type=jnp.float32)
    gains = qgain[...].astype(jnp.float32)
    for h in range(wq.shape[1] // head):
        out[:, h * head : (h + 1) * head] = head_norm_rope(
            lin[:, h * head : (h + 1) * head], gains, cosine[...], sine[...]
        ).astype(jnp.bfloat16)


def make_q(normed, wq, qgain, cosine, sine):
    rows, width = normed.shape
    cols = wq.shape[1]
    tile = 256 if cols % 256 == 0 else cols
    head = qgain.shape[1]
    fixed = lambda n: (0, 0)
    return pl.pallas_call(
        q_kernel,
        grid=(cols // tile,),
        in_specs=[
            pl.BlockSpec((rows, width), fixed),
            pl.BlockSpec((width, tile), lambda n: (0, n)),
            pl.BlockSpec((1, head), fixed),
            pl.BlockSpec((rows, head), fixed),
            pl.BlockSpec((rows, head), fixed),
        ],
        out_specs=pl.BlockSpec((rows, tile), lambda n: (0, n)),
        out_shape=jax.ShapeDtypeStruct((rows, cols), jnp.bfloat16),
        compiler_params=params(),
        cost_estimate=cost(2 * rows * width * cols, 2 * width * cols + 2 * rows * (width + cols)),
        name="queries",
    )(normed, wq, qgain, cosine, sine)


def attention_kernel(lay, spans, most, per_kv, head, table, *refs):
    q_refs, k_refs, v_refs, out = refs[:PARTS], refs[PARTS : 2 * PARTS], refs[2 * PARTS : -1], refs[-1]
    owners, rows = k_refs[0].shape[0], k_refs[0].shape[3]
    group_rank = table[lay.group_rank]
    scale = (1.0 / math.sqrt(head)) * math.log2(math.e)
    q_rows, k_rows = PARTS * per_kv * rows, owners * rows
    row = lax.broadcasted_iota(jnp.int32, (q_rows, k_rows), 0)
    col = lax.broadcasted_iota(jnp.int32, (q_rows, k_rows), 1)
    q_at = group_rank * PARTS * rows + (row // (per_kv * rows)) * rows + row % rows
    k_at = (col // rows) * PARTS * rows + col % rows
    allowed = [k_at + c * rows <= q_at for c in range(PARTS)]

    def one_span(k, carry):
        slot = table[lay.slot + k]
        earlier = k - table[lay.start + k]
        queries = jnp.concatenate(
            [
                ref[slot, :, g * head : (g + 1) * head]
                for ref in q_refs
                for g in range(per_kv)
            ],
            axis=0,
        )

        def with_earlier(count):
            scores, blocks = [], []
            for back in range(count + 1):
                at = table[lay.slot + k - back]
                for c in range(PARTS):
                    block = k_refs[c][:, 0, at].reshape(k_rows, head)
                    s = lax.dot_general(
                        queries, block, (((1,), (1,)), ((), ())),
                        preferred_element_type=jnp.float32,
                    )
                    if back == 0:
                        s = jnp.where(allowed[c], s, very_negative)
                    scores.append(s)
                    blocks.append((c, at))
            best = scores[0]
            for s in scores[1:]:
                best = jnp.maximum(best, s)
            best = jnp.max(best, axis=-1, keepdims=True)
            total = None
            summed = None
            for s, (c, at) in zip(scores, blocks):
                w = jnp.exp2((s - best) * scale)
                part = jnp.sum(w, axis=-1, keepdims=True)
                value = v_refs[c][:, 0, at].reshape(k_rows, head)
                term = jnp.dot(
                    w.astype(jnp.bfloat16), value, preferred_element_type=jnp.float32
                )
                total = part if total is None else total + part
                summed = term if summed is None else summed + term
            result = (summed / total).astype(jnp.bfloat16)
            for c in range(PARTS):
                for g in range(per_kv):
                    at_row = (c * per_kv + g) * rows
                    out[slot, c * rows : (c + 1) * rows, g * head : (g + 1) * head] = result[
                        at_row : at_row + rows
                    ]

        for count in range(most):
            pl.when(earlier == count)(functools.partial(with_earlier, count))
        return carry

    lax.fori_loop(0, spans, one_span, 0)


def make_attention(lay, most, table, queries, gathered, per_kv, head):
    spans, rows, cols = queries[0].shape
    owners = gathered[0].shape[0]
    own_kv = cols // (per_kv * head)
    q_spec = pl.BlockSpec((spans, rows, per_kv * head), lambda h, t: (0, 0, h))
    k_spec = pl.BlockSpec((owners, 1, spans, rows, head), lambda h, t: (0, 0, 0, 0, h))
    v_spec = pl.BlockSpec((owners, 1, spans, rows, head), lambda h, t: (0, 1, 0, 0, h))
    all_rows = spans * rows * PARTS
    pairs = 2.2 * all_rows * owners * rows * PARTS * per_kv * own_kv
    return pl.pallas_call(
        functools.partial(attention_kernel, lay, spans, most, per_kv, head),
        grid_spec=pltpu.PrefetchScalarGridSpec(
            num_scalar_prefetch=1,
            grid=(own_kv,),
            in_specs=[q_spec] * PARTS + [k_spec] * PARTS + [v_spec] * PARTS,
            out_specs=pl.BlockSpec((spans, rows * PARTS, per_kv * head), lambda h, t: (0, 0, h)),
        ),
        out_shape=jax.ShapeDtypeStruct((spans, rows * PARTS, cols), jnp.bfloat16),
        compiler_params=params(),
        cost_estimate=cost(4 * pairs * head, 4 * all_rows * cols + 4 * PARTS * gathered[0].size, pairs),
        name="attention",
    )(table, *queries, *gathered, *gathered)


def project_kernel(table, attended, wo, out):
    out[...] = jnp.dot(
        attended[...], wo[...], preferred_element_type=jnp.float32
    ).astype(jnp.bfloat16)


def make_projection(lay, table, attended, wo, first, count, tile, name):
    rows, depth = attended.shape
    return pl.pallas_call(
        project_kernel,
        grid_spec=pltpu.PrefetchScalarGridSpec(
            num_scalar_prefetch=1,
            grid=(count,),
            in_specs=[
                pl.BlockSpec((rows, depth), lambda n, t: (0, 0)),
                pl.BlockSpec((depth, tile), lambda n, t: (0, first(t[lay.tensor_rank]) + n)),
            ],
            out_specs=pl.BlockSpec((rows, tile), lambda n, t: (0, n)),
        ),
        out_shape=jax.ShapeDtypeStruct((rows, count * tile), jnp.bfloat16),
        compiler_params=params(),
        cost_estimate=cost(
            2 * rows * depth * count * tile, 2 * (rows * depth + (rows + depth) * count * tile)
        ),
        name=name,
    )(table, attended, wo)


def add_kernel(table, *refs):
    x_refs, own, received, out = refs[:PARTS], refs[PARTS], refs[PARTS + 1], refs[PARTS + 2]
    rows = x_refs[0].shape[1]
    for c in range(PARTS):
        at = slice(c * rows, (c + 1) * rows)
        summed = own[0, at].astype(jnp.float32) + received[0, at].astype(jnp.float32)
        out[0, at] = (x_refs[c][0].astype(jnp.float32) + summed).astype(jnp.bfloat16)


def make_sum(lay, table, arrived, own, received, first, tile):
    spans, rows, cols = received.shape
    part = rows // PARTS
    tiles = cols // tile
    slot_of = lambda t, table: table[lay.from_slot + t]
    return pl.pallas_call(
        add_kernel,
        grid_spec=pltpu.PrefetchScalarGridSpec(
            num_scalar_prefetch=1,
            grid=(spans, tiles),
            in_specs=[
                pl.BlockSpec((1, part, tile), lambda t, n, s: (slot_of(t, s), 0, first + n))
            ] * PARTS
            + [
                pl.BlockSpec((1, rows, tile), lambda t, n, s: (slot_of(t, s), 0, first + n)),
                pl.BlockSpec((1, rows, tile), lambda t, n, s: (slot_of(t, s), 0, n)),
            ],
            out_specs=pl.BlockSpec((1, rows, tile), lambda t, n, s: (t, 0, n)),
        ),
        out_shape=jax.ShapeDtypeStruct((spans, rows, cols), jnp.bfloat16),
        compiler_params=params(),
        cost_estimate=cost(3 * spans * rows * cols, 8 * spans * rows * cols),
        name="residual",
    )(table, *arrived, own, received)


def pages_kernel(table, *refs):
    sources, out = refs[:PARTS], refs[PARTS]
    rows = sources[0].shape[3]
    for d in range(sources[0].shape[0]):
        for c in range(PARTS):
            at = (d * PARTS + c) * rows
            out[0, :, at : at + rows] = sources[c][d, :, 0]


def make_pages(lay, table, gathered, pages_each):
    owners, _, spans, rows, cols = gathered[0].shape
    per_page = PAGE_ROWS // (rows * PARTS)

    def source(i, t):
        page = t[lay.page + t[lay.group_rank] * pages_each + i]
        return (lax.rem(page, pages_each), 0, t[lay.slot + lax.div(page, pages_each)], 0, 0)

    return pl.pallas_call(
        pages_kernel,
        grid_spec=pltpu.PrefetchScalarGridSpec(
            num_scalar_prefetch=1,
            grid=(pages_each,),
            in_specs=[pl.BlockSpec((per_page, 2, 1, rows, cols), source)] * PARTS,
            out_specs=pl.BlockSpec((1, 2, PAGE_ROWS, cols), lambda i, t: (i, 0, 0, 0)),
        ),
        out_shape=jax.ShapeDtypeStruct((pages_each, 2, PAGE_ROWS, cols), jnp.bfloat16),
        compiler_params=params(),
        cost_estimate=cost(0, 8 * pages_each * PAGE_ROWS * cols),
        name="pages",
    )(table, *gathered)


def rope_tables(offsets, span_len, first_row, rows, head):
    half = head // 2
    freqs = jnp.power(
        jnp.float32(rope_base), -jnp.arange(half, dtype=jnp.float32) * 2.0 / head
    )
    at = offsets[:, None] * span_len + first_row + jnp.arange(rows, dtype=jnp.int32)[None, :]
    angles = at.reshape(-1).astype(jnp.float32)[:, None] * freqs[None, :]
    cosine, sine = jnp.cos(angles), jnp.sin(angles)
    return (
        jnp.concatenate([cosine, cosine], axis=1),
        jnp.concatenate([-sine, sine], axis=1),
    )


def widths_of(cols, tile):
    tiles = cols // tile
    if tiles == 10:
        return [2, 3, 3, 2]
    return [tiles]


def local(
    hidden_in, ln_gain, wq, wk, wv, q_gain, key_norm_gain, wo,
    prompt_spans, span_source, span_target, page_slot,
):
    _, span_len, cols = hidden_in.shape
    tensor_size = lax.axis_size("tensor")
    owners = lax.axis_size("group")
    tensor_rank = lax.axis_index("tensor")
    group_rank = lax.axis_index("group")
    head = q_gain.shape[0]
    own_rows = span_len // owners
    rows = own_rows // PARTS
    pages_each = span_len // PAGE_ROWS
    spans = span_source.shape[0]
    most = spans - (prompt_spans.shape[0] - 1)
    most = min(most, spans // 2)
    local_heads = wq.shape[1] // head
    kv_cols = wk.shape[1]
    kv_heads = kv_cols * tensor_size // head
    lay = Layout(spans, spans * pages_each)

    if kv_cols < head:
        share = head // kv_cols
        sets = [list(range(i, i + share)) for i in range(0, tensor_size, share)]
        wk, wv = [
            lax.all_gather(w, "tensor", axis=1, tiled=True, axis_index_groups=sets)
            for w in (wk, wv)
        ]
    per_kv = local_heads // max(1, wk.shape[1] // head)

    ranks = jnp.stack([group_rank, tensor_rank]).astype(jnp.int32)
    table = make_tables(
        lay, spans, spans * pages_each, ranks, prompt_spans, span_source, span_target, page_slot
    )
    gain = lax.all_gather(ln_gain, "tensor", axis=0, tiled=True)[None]
    offsets = table[lay.offset : lay.offset + spans]

    split = hidden_in.reshape(owners, PARTS, rows, cols)
    arrived, queries, gathered, normed = [], [], [], []
    ropes = []
    for c in range(PARTS):
        arrived.append(
            lax.all_to_all(split[:, c], "group", split_axis=0, concat_axis=0, tiled=True)
        )
        ropes.append(
            rope_tables(offsets, span_len, group_rank * own_rows + c * rows, rows, head)
        )
    for c in range(PARTS):
        whole = lax.all_gather(
            arrived[c].reshape(spans * rows, cols), "tensor", axis=1, tiled=True
        )
        rows_normed, kv = make_kv(
            whole, gain, wk, wv, key_norm_gain[None], *ropes[c]
        )
        normed.append(rows_normed)
        kv = kv.reshape(2, spans, rows, kv.shape[2])
        gathered.append(lax.all_gather(kv, "group", axis=0, tiled=False))
    for c in range(PARTS):
        made = make_q(normed[c], wq, q_gain[None], *ropes[c])
        queries.append(made.reshape(spans, rows, made.shape[1]))

    attended = make_attention(lay, most, table, queries, gathered, per_kv, head)
    attended = attended.reshape(spans * own_rows, -1)

    pages = make_pages(lay, table, gathered, pages_each)
    if kv_cols < head:
        pages = lax.dynamic_slice_in_dim(
            pages, lax.rem(tensor_rank, head // kv_cols) * kv_cols, kv_cols, 3
        )
    cache = lax.all_gather(pages, "tensor", axis=3, tiled=True)

    if tensor_size == 2:
        tile = 256
        half_tiles = cols // tile
        widths = widths_of(cols, tile)
        received, first = [], 0
        for width in widths:
            partial = make_projection(
                lay, table, attended, wo,
                lambda r, first=first: (1 - r) * half_tiles + first, width, tile, "send_part",
            )
            received.append(
                lax.ppermute(partial, "tensor", [(0, 1), (1, 0)]).reshape(spans, own_rows, -1)
            )
            first += width
        own = make_projection(
            lay, table, attended, wo, lambda r: r * half_tiles, half_tiles, tile, "own_part"
        ).reshape(spans, own_rows, cols)
        pieces, first = [], 0
        for width, got in zip(widths, received):
            moved = make_sum(lay, table, arrived, own, got, first, tile)
            pieces.append(
                lax.all_to_all(moved, "group", split_axis=0, concat_axis=0, tiled=True)
            )
            first += width
        mixed = jnp.concatenate(pieces, axis=2).reshape(1, span_len, cols)
    else:
        partial = jnp.dot(attended, wo, preferred_element_type=jnp.float32)
        summed = lax.psum_scatter(
            partial.astype(jnp.bfloat16), "tensor", scatter_dimension=1, tiled=True
        )
        x = jnp.concatenate(arrived, axis=1).astype(jnp.float32)
        moved = (x + summed.reshape(x.shape).astype(jnp.float32)).astype(jnp.bfloat16)
        moved = jnp.take(moved, table[lay.from_slot : lay.from_slot + spans], axis=0)
        moved = lax.all_to_all(moved, "group", split_axis=0, concat_axis=0, tiled=True)
        mixed = moved.reshape(1, span_len, cols)
    return (mixed, cache)


def solution(mesh):
    in_specs = (
        P(("replica", "group"), None, "tensor"),
        P("tensor"),
        P(None, "tensor"),
        P(None, "tensor"),
        P(None, "tensor"),
        P(),
        P(),
        P("tensor", None),
        P("replica"),
        P("replica"),
        P("replica"),
        P("replica"),
    )
    out_specs = (P(("replica", "group"), None, "tensor"), P(("replica", "group"), None, None, None))
    return jax.shard_map(local, mesh=mesh, in_specs=in_specs, out_specs=out_specs, check_vma=False)
```

```python
import functools
import math

import jax
import jax.numpy as jnp
from jax import lax
from jax.experimental import pallas as pl
from jax.experimental.pallas import tpu as pltpu
from jax.sharding import PartitionSpec as P

PAGE_ROWS = 128
epsilon = 1e-06
rope_base = 1000000.0
very_negative = -1e30
VMEM_BYTES = 48 * 1024 * 1024
PARTS = 2
CORES = 2


def params():
    return pltpu.CompilerParams(vmem_limit_bytes=VMEM_BYTES)


def cost(flops, moved, transcendentals=0):
    return pl.CostEstimate(
        flops=int(flops), bytes_accessed=int(moved), transcendentals=int(transcendentals)
    )


def hop_order(chips):
    return [0, 1, chips - 1] + list(range(2, chips - 1)) if chips > 2 else list(range(chips))


class Layout:
    def __init__(self, spans, pages, owners):
        self.chips = owners // CORES
        self.span_at = 0
        self.earlier_at = self.span_at + spans
        self.target_at = self.earlier_at + spans
        self.page = self.target_at + spans
        self.origin = self.page + pages
        self.group_rank = self.origin + owners * spans
        self.tensor_rank = self.group_rank + 1
        self.length = self.tensor_rank + 1


def tables_kernel(lay, spans, pages, ranks, prompt_spans, source, target, page_slot, out, span_of, start_of):
    chips = lay.chips
    group_rank = ranks[0]
    out[lay.group_rank] = group_rank
    out[lay.tensor_rank] = ranks[1]
    for k in range(spans):
        start = jnp.int32(0)
        begin = jnp.int32(0)
        for p in range(prompt_spans.shape[0]):
            start = jnp.where(begin <= k, begin, start)
            begin = begin + prompt_spans[p]
        start_of[k] = start
        span_of[source[k]] = jnp.int32(k)
    for p in range(pages):
        out[lay.page + page_slot[p]] = jnp.int32(p)
    chip, core = lax.div(group_rank, CORES), lax.rem(group_rank, CORES)
    hops = hop_order(chips)
    for back in range(chips):
        for other in range(CORES):
            at_chip = lax.rem(chip + chips - back, chips)
            at_core = jnp.where(other == 0, core, 1 - core)
            for n, hop in enumerate(hops):
                for flip in range(CORES):
                    from_chip = lax.rem(at_chip + chips - hop, chips)
                    from_core = jnp.where(flip == 0, at_core, 1 - at_core)
                    k = span_of[from_chip * CORES + from_core]
                    place = n * CORES + flip
                    out[lay.origin + (back * CORES + other) * spans + place] = k
                    if back == 0 and other == 0:
                        out[lay.span_at + place] = k
                        out[lay.earlier_at + place] = k - start_of[k]
                        out[lay.target_at + place] = target[k]


def make_tables(lay, spans, pages, ranks, prompt_spans, source, target, page_slot):
    smem = pl.BlockSpec(memory_space=pltpu.SMEM)
    return pl.pallas_call(
        functools.partial(tables_kernel, lay, spans, pages),
        out_shape=jax.ShapeDtypeStruct((lay.length,), jnp.int32),
        in_specs=[smem] * 5,
        out_specs=smem,
        scratch_shapes=[pltpu.SMEM((spans,), jnp.int32)] * 2,
        name="tables",
    )(ranks, prompt_spans, source, target, page_slot)


def head_norm_rope(u, gain, cosine, sine):
    mean_sq = jnp.mean(u * u, axis=-1, keepdims=True)
    u = u * lax.rsqrt(mean_sq + epsilon) * gain
    half = u.shape[-1] // 2
    return u * cosine + pltpu.roll(u, half, 1) * sine


def half_index(lay, sides, side):
    if sides == 1:
        return lambda t: 0
    if side == 0:
        return lambda t: t[lay.tensor_rank]
    return lambda t: 1 - t[lay.tensor_rank]


def summed_dot(lefts, rights):
    total = None
    for left, right in zip(lefts, rights):
        term = jnp.dot(left[...], right[...], preferred_element_type=jnp.float32)
        total = term if total is None else total + term
    return total


def kv_kernel(sides, blocks, table, *refs):
    refs = list(refs)
    take = lambda n: [refs.pop(0) for _ in range(n)]
    xs = [take(blocks) for _ in range(sides)]
    gains, wks, wvs = take(sides), take(sides), take(sides)
    kgain, cosine, sine = take(3)
    normed, (kv,) = take(sides), take(1)
    head = kgain.shape[1]
    width = sum(x[0].shape[1] for x in xs)

    @pl.when(pl.program_id(0) == 0)
    def _():
        at = 0
        for b in range(blocks):
            wide = [x[b][...].astype(jnp.float32) for x in xs]
            total = sum(jnp.sum(w * w, axis=-1, keepdims=True) for w in wide)
            factor = lax.rsqrt(total / width + epsilon)
            rows = xs[0][b].shape[0]
            for w, gain, to in zip(wide, gains, normed):
                to[at : at + rows] = (w * factor * gain[...].astype(jnp.float32)).astype(
                    jnp.bfloat16
                )
            at += rows

    keys = summed_dot(normed, wks).astype(jnp.bfloat16)
    gains = kgain[...].astype(jnp.float32)
    for h in range(keys.shape[1] // head):
        u = keys[:, h * head : (h + 1) * head].astype(jnp.float32)
        kv[0, :, h * head : (h + 1) * head] = head_norm_rope(
            u, gains, cosine[...], sine[...]
        ).astype(jnp.bfloat16)
    kv[1] = summed_dot(normed, wvs).astype(jnp.bfloat16)


def make_kv(lay, table, xs, gains, wk, wv, kgain, cosine, sine, part):
    sides, blocks = len(xs), len(xs[0])
    rows = sum(x.shape[0] for x in xs[0])
    widths = [x[0].shape[1] for x in xs]
    width, cols = wk.shape
    tile = 256 if cols % 256 == 0 else cols
    head = kgain.shape[1]
    fixed = lambda n, t: (0, 0)
    here = lambda n, t: (part, 0)
    weights = []
    for side in range(sides):
        index = half_index(lay, sides, side)
        weights.append(
            pl.BlockSpec((widths[side], tile), lambda n, t, index=index: (index(t), n))
        )
    return pl.pallas_call(
        functools.partial(kv_kernel, sides, blocks),
        grid_spec=pltpu.PrefetchScalarGridSpec(
            num_scalar_prefetch=1,
            grid=(cols // tile,),
            in_specs=[pl.BlockSpec(x.shape, fixed) for side in xs for x in side]
            + [pl.BlockSpec((1, w), fixed) for w in widths]
            + weights
            + weights
            + [
                pl.BlockSpec((1, head), fixed),
                pl.BlockSpec((rows, head), here),
                pl.BlockSpec((rows, head), here),
            ],
            out_specs=[pl.BlockSpec((rows, w), fixed) for w in widths]
            + [pl.BlockSpec((2, rows, tile), lambda n, t: (0, 0, n))],
        ),
        out_shape=[jax.ShapeDtypeStruct((rows, w), jnp.bfloat16) for w in widths]
        + [jax.ShapeDtypeStruct((2, rows, cols), jnp.bfloat16)],
        compiler_params=params(),
        cost_estimate=cost(4 * rows * width * cols, 4 * width * cols + 4 * rows * width),
        name="keys_values",
    )(
        table, *[x for side in xs for x in side], *gains, *[wk] * sides, *[wv] * sides,
        kgain, cosine, sine,
    )


def q_kernel(sides, table, *refs):
    normed, wqs = refs[:sides], refs[sides : 2 * sides]
    qgain, cosine, sine, out = refs[2 * sides :]
    head = qgain.shape[1]
    lin = summed_dot(normed, wqs)
    gains = qgain[...].astype(jnp.float32)
    for h in range(lin.shape[1] // head):
        out[:, h * head : (h + 1) * head] = head_norm_rope(
            lin[:, h * head : (h + 1) * head], gains, cosine[...], sine[...]
        ).astype(jnp.bfloat16)


def make_q(lay, table, normed, wq, qgain, cosine, sine, part):
    sides = len(normed)
    rows = normed[0].shape[0]
    width, cols = wq.shape
    tile = 512 if cols % 512 == 0 else cols
    head = qgain.shape[1]
    fixed = lambda n, t: (0, 0)
    here = lambda n, t: (part, 0)
    weights = []
    for side in range(sides):
        index = half_index(lay, sides, side)
        weights.append(
            pl.BlockSpec(
                (normed[side].shape[1], tile), lambda n, t, index=index: (index(t), n)
            )
        )
    return pl.pallas_call(
        functools.partial(q_kernel, sides),
        grid_spec=pltpu.PrefetchScalarGridSpec(
            num_scalar_prefetch=1,
            grid=(cols // tile,),
            in_specs=[pl.BlockSpec(x.shape, fixed) for x in normed]
            + weights
            + [
                pl.BlockSpec((1, head), fixed),
                pl.BlockSpec((rows, head), here),
                pl.BlockSpec((rows, head), here),
            ],
            out_specs=pl.BlockSpec((rows, tile), lambda n, t: (0, n)),
        ),
        out_shape=jax.ShapeDtypeStruct((rows, cols), jnp.bfloat16),
        compiler_params=params(),
        cost_estimate=cost(2 * rows * width * cols, 2 * width * cols + 2 * rows * (width + cols)),
        name="queries",
    )(table, *normed, *[wq] * sides, qgain, cosine, sine)


def attention_kernel(lay, spans, most, per_kv, head, owners, pages_each, table, *refs):
    q_refs = refs[:PARTS]
    kv_refs = refs[PARTS : PARTS + owners * PARTS]
    out, pages, keys, values = refs[PARTS + owners * PARTS :]
    chips = lay.chips
    here, rows = kv_refs[0].shape[1], kv_refs[0].shape[2]
    group_rank = table[lay.group_rank]
    chip, core = lax.div(group_rank, CORES), lax.rem(group_rank, CORES)
    for o in range(owners):
        back, other = o // CORES, o % CORES
        owner = lax.rem(chip + chips - back, chips) * CORES + (core if other == 0 else 1 - core)
        at = pl.ds(pl.multiple_of(owner * rows, rows), rows)
        for p in range(PARTS):
            for i in range(here):
                k = table[lay.origin + o * spans + p * here + i]
                keys[k, at] = kv_refs[o * PARTS + p][0, i]
                values[k, at] = kv_refs[o * PARTS + p][1, i]

    for i in range(pages_each):
        page = table[lay.page + group_rank * pages_each + i]
        k = lax.div(page, pages_each)
        at = pl.ds(pl.multiple_of(lax.rem(page, pages_each) * PAGE_ROWS, PAGE_ROWS), PAGE_ROWS)
        pages[i, 0] = keys[k, at]
        pages[i, 1] = values[k, at]

    scale = (1.0 / math.sqrt(head)) * math.log2(math.e)
    q_rows, k_rows = per_kv * rows, owners * rows
    row = lax.broadcasted_iota(jnp.int32, (q_rows, k_rows), 0)
    col = lax.broadcasted_iota(jnp.int32, (q_rows, k_rows), 1)
    allowed = col <= group_rank * rows + row % rows

    def one_place(p, i, carry):
        k = table[lay.span_at + p * here + i]
        earlier = table[lay.earlier_at + p * here + i]
        queries = jnp.concatenate(
            [q_refs[p][i, :, g * head : (g + 1) * head] for g in range(per_kv)], axis=0
        )

        def with_earlier(count):
            scores = []
            for back in range(count + 1):
                s = lax.dot_general(
                    queries, keys[k - back], (((1,), (1,)), ((), ())),
                    preferred_element_type=jnp.float32,
                )
                if back == 0:
                    s = jnp.where(allowed, s, very_negative)
                scores.append(s)
            best = scores[0]
            for s in scores[1:]:
                best = jnp.maximum(best, s)
            best = jnp.max(best, axis=-1, keepdims=True)
            total = None
            summed = None
            for back, s in enumerate(scores):
                w = jnp.exp2((s - best) * scale)
                part = jnp.sum(w, axis=-1, keepdims=True)
                term = jnp.dot(
                    w.astype(jnp.bfloat16), values[k - back], preferred_element_type=jnp.float32
                )
                total = part if total is None else total + part
                summed = term if summed is None else summed + term
            result = (summed / total).astype(jnp.bfloat16)
            for g in range(per_kv):
                out[p * here + i, :, g * head : (g + 1) * head] = result[
                    g * rows : (g + 1) * rows
                ]

        for count in range(most):
            pl.when(earlier == count)(functools.partial(with_earlier, count))
        return carry

    for p in range(PARTS):
        lax.fori_loop(0, here, functools.partial(one_place, p), 0)


def make_attention(lay, most, table, queries, gathered, per_kv, head, pages_each):
    here, rows, cols = queries[0].shape
    spans = here * PARTS
    owners = len(gathered)
    own_kv = cols // (per_kv * head)
    q_spec = pl.BlockSpec((here, rows, per_kv * head), lambda h, t: (0, 0, h))
    kv_spec = pl.BlockSpec((2, here, rows, head), lambda h, t: (0, 0, 0, h))
    flat = [x for origin in gathered for x in origin]
    all_rows = spans * rows
    pairs = 2.2 * all_rows * owners * rows * per_kv * own_kv
    return pl.pallas_call(
        functools.partial(
            attention_kernel, lay, spans, most, per_kv, head, owners, pages_each
        ),
        grid_spec=pltpu.PrefetchScalarGridSpec(
            num_scalar_prefetch=1,
            grid=(own_kv,),
            in_specs=[q_spec] * PARTS + [kv_spec] * len(flat),
            out_specs=[
                pl.BlockSpec((spans, rows, per_kv * head), lambda h, t: (0, 0, h)),
                pl.BlockSpec((pages_each, 2, PAGE_ROWS, head), lambda h, t: (0, 0, 0, h)),
            ],
            scratch_shapes=[pltpu.VMEM((spans, owners * rows, head), jnp.bfloat16)] * 2,
        ),
        out_shape=[
            jax.ShapeDtypeStruct((spans, rows, cols), jnp.bfloat16),
            jax.ShapeDtypeStruct((pages_each, 2, PAGE_ROWS, own_kv * head), jnp.bfloat16),
        ],
        compiler_params=params(),
        cost_estimate=cost(
            4 * pairs * head, 4 * all_rows * cols + 2 * len(flat) * flat[0].size, pairs
        ),
        name="attention",
    )(table, *queries, *flat)


def project_kernel(table, attended, wo, *refs):
    refs[-1][...] = jnp.dot(
        attended[...], wo[...], preferred_element_type=jnp.float32
    ).astype(jnp.bfloat16)


def make_projection(lay, table, attended, wo, first, count, tile, name, after=()):
    rows, depth = attended.shape
    return pl.pallas_call(
        project_kernel,
        grid_spec=pltpu.PrefetchScalarGridSpec(
            num_scalar_prefetch=1,
            grid=(count,),
            in_specs=[
                pl.BlockSpec((rows, depth), lambda n, t: (0, 0)),
                pl.BlockSpec((depth, tile), lambda n, t: (0, first(t[lay.tensor_rank]) + n)),
            ]
            + [pl.BlockSpec(memory_space=pl.ANY)] * len(after),
            out_specs=pl.BlockSpec((rows, tile), lambda n, t: (0, n)),
        ),
        out_shape=jax.ShapeDtypeStruct((rows, count * tile), jnp.bfloat16),
        compiler_params=params(),
        cost_estimate=cost(
            2 * rows * depth * count * tile, 2 * (rows * depth + (rows + depth) * count * tile)
        ),
        name=name,
    )(table, attended, wo, *after)


def add_kernel(lay, table, *refs):
    x_refs, own, received, out = refs[:-3], refs[-3], refs[-2], refs[-1]
    for place, x in enumerate(x_refs):
        summed = own[place].astype(jnp.float32) + received[place].astype(jnp.float32)
        out[table[lay.target_at + place]] = (x[...].astype(jnp.float32) + summed).astype(
            jnp.bfloat16
        )


def make_sum(lay, table, arrived, own, received, first):
    spans, rows, cols = received.shape
    unit = math.gcd(first, cols) if first else cols
    steps, start = cols // unit, first // unit
    return pl.pallas_call(
        functools.partial(add_kernel, lay),
        grid_spec=pltpu.PrefetchScalarGridSpec(
            num_scalar_prefetch=1,
            grid=(steps,),
            in_specs=[pl.BlockSpec((rows, unit), lambda n, t: (0, start + n))] * spans
            + [
                pl.BlockSpec((spans, rows, unit), lambda n, t: (0, 0, start + n)),
                pl.BlockSpec((spans, rows, unit), lambda n, t: (0, 0, n)),
            ],
            out_specs=pl.BlockSpec((spans, rows, unit), lambda n, t: (0, 0, n)),
        ),
        out_shape=jax.ShapeDtypeStruct((spans, rows, cols), jnp.bfloat16),
        compiler_params=params(),
        cost_estimate=cost(3 * spans * rows * cols, 8 * spans * rows * cols),
        name="residual",
    )(table, *arrived, own, received)


def rope_tables(earlier, span_len, first_row, rows, head):
    half = head // 2
    freqs = jnp.power(
        jnp.float32(rope_base), -jnp.arange(half, dtype=jnp.float32) * 2.0 / head
    )
    at = earlier[:, None] * span_len + first_row + jnp.arange(rows, dtype=jnp.int32)[None, :]
    angles = at.reshape(-1).astype(jnp.float32)[:, None] * freqs[None, :]
    cosine, sine = jnp.cos(angles), jnp.sin(angles)
    return (
        jnp.concatenate([cosine, cosine], axis=1),
        jnp.concatenate([-sine, sine], axis=1),
    )


def widths_of(tiles):
    return [1, 2, 1, 1] if tiles == 5 else [1, tiles - 1]


def shift(x, owners, hop, flip):
    chips = owners // CORES
    pairs = [
        (z * CORES + c, (z + hop) % chips * CORES + (c ^ flip))
        for z in range(chips)
        for c in range(CORES)
    ]
    return lax.ppermute(x, "group", pairs)


def local(
    hidden_in, ln_gain, wq, wk, wv, q_gain, key_norm_gain, wo,
    prompt_spans, span_source, span_target, page_slot,
):
    _, span_len, cols = hidden_in.shape
    tensor_size = lax.axis_size("tensor")
    owners = lax.axis_size("group")
    tensor_rank = lax.axis_index("tensor")
    group_rank = lax.axis_index("group")
    chips = owners // CORES
    head = q_gain.shape[0]
    rows = span_len // owners
    pages_each = span_len // PAGE_ROWS
    spans = span_source.shape[0]
    here = spans // PARTS
    most = min(spans - (prompt_spans.shape[0] - 1), spans // 2)
    kv_cols = wk.shape[1]
    paired = tensor_size == 2
    swap = [(0, 1), (1, 0)]
    lay = Layout(spans, spans * pages_each, owners)

    if kv_cols < head:
        share = head // kv_cols
        sets = [list(range(i, i + share)) for i in range(0, tensor_size, share)]
        wk, wv = [
            lax.all_gather(w, "tensor", axis=1, tiled=True, axis_index_groups=sets)
            for w in (wk, wv)
        ]
    per_kv = wq.shape[1] // max(head, wk.shape[1])

    chip, core = group_rank // CORES, group_rank % CORES
    split = hidden_in.reshape(owners, rows, cols)
    arrived = []
    for hop in hop_order(chips):
        for flip in range(CORES):
            to = (chip + hop) % chips * CORES + (core + flip) % CORES
            block = lax.dynamic_index_in_dim(split, to, 0, keepdims=False)
            if hop or flip:
                block = shift(block, owners, hop, flip)
            arrived.append(block)

    ranks = jnp.stack([group_rank, tensor_rank]).astype(jnp.int32)
    table = make_tables(
        lay, spans, spans * pages_each, ranks, prompt_spans, span_source, span_target, page_slot
    )
    earlier = table[lay.earlier_at : lay.earlier_at + spans]
    cosine, sine = rope_tables(earlier, span_len, group_rank * rows, rows, head)

    if paired:
        gain = ln_gain[None]
        gains = [gain, lax.ppermute(gain, "tensor", swap)]
        crossed = [lax.ppermute(block, "tensor", swap) for block in arrived]
    else:
        gains = [lax.all_gather(ln_gain, "tensor", axis=0, tiled=True)[None]]

    queries, normed, gathered = [], [], [[] for _ in range(owners)]
    for p in range(PARTS):
        at = slice(p * here, (p + 1) * here)
        if paired:
            xs = [arrived[at], crossed[at]]
        else:
            xs = [[lax.all_gather(jnp.concatenate(arrived[at]), "tensor", axis=1, tiled=True)]]
        *rows_normed, kv = make_kv(
            lay, table, xs, gains, wk, wv, key_norm_gain[None], cosine, sine, p
        )
        normed.append(rows_normed)
        kv = kv.reshape(2, here, rows, kv.shape[2])
        for back in range(chips):
            if back:
                kv = shift(kv, owners, 1, 0)
            gathered[back * CORES].append(kv)
            gathered[back * CORES + 1].append(shift(kv, owners, 0, 1))
    for p in range(PARTS):
        made = make_q(lay, table, normed[p], wq, q_gain[None], cosine, sine, p)
        queries.append(made.reshape(here, rows, made.shape[1]))

    attended, pages = make_attention(
        lay, most, table, queries, gathered, per_kv, head, pages_each
    )
    attended = attended.reshape(spans * rows, -1)

    if paired:
        tile = 512
        half_tiles = cols // tile
        widths = widths_of(half_tiles)
        received, first, last = [], 0, ()
        for width in widths:
            partial = make_projection(
                lay, table, attended, wo,
                lambda r, first=first: (1 - r) * half_tiles + first, width, tile, "send_part",
                last,
            )
            last = (partial,)
            received.append(lax.ppermute(partial, "tensor", swap).reshape(spans, rows, -1))
            first += width
        own = make_projection(
            lay, table, attended, wo, lambda r: r * half_tiles, half_tiles, tile, "own_part", last
        ).reshape(spans, rows, cols)
        pages, received[-2] = lax.optimization_barrier((pages, received[-2]))
        other = lax.ppermute(pages, "tensor", swap)
        cache = jnp.concatenate(
            [jnp.where(tensor_rank == 0, pages, other), jnp.where(tensor_rank == 0, other, pages)],
            axis=3,
        )
        pieces, first = [], 0
        for got in received:
            moved = make_sum(lay, table, arrived, own, got, first)
            pieces.append(
                lax.all_to_all(moved, "group", split_axis=0, concat_axis=0, tiled=True)
            )
            first += got.shape[2]
        mixed = jnp.concatenate(pieces, axis=2).reshape(1, span_len, cols)
    else:
        if kv_cols < head:
            pages = lax.dynamic_slice_in_dim(
                pages, lax.rem(tensor_rank, head // kv_cols) * kv_cols, kv_cols, 3
            )
        cache = lax.all_gather(pages, "tensor", axis=3, tiled=True)
        partial = jnp.dot(attended, wo, preferred_element_type=jnp.float32)
        summed = lax.psum_scatter(
            partial.astype(jnp.bfloat16), "tensor", scatter_dimension=1, tiled=True
        )
        summed = summed.reshape(spans, rows, cols).astype(jnp.float32)
        moved = (jnp.stack(arrived).astype(jnp.float32) + summed).astype(jnp.bfloat16)
        targets = table[lay.target_at : lay.target_at + spans]
        moved = jnp.zeros_like(moved).at[targets].set(moved, unique_indices=True)
        moved = lax.all_to_all(moved, "group", split_axis=0, concat_axis=0, tiled=True)
        mixed = moved.reshape(1, span_len, cols)
    return (mixed, cache)


def solution(mesh):
    in_specs = (
        P(("replica", "group"), None, "tensor"),
        P("tensor"),
        P(None, "tensor"),
        P(None, "tensor"),
        P(None, "tensor"),
        P(),
        P(),
        P("tensor", None),
        P("replica"),
        P("replica"),
        P("replica"),
        P("replica"),
    )
    out_specs = (P(("replica", "group"), None, "tensor"), P(("replica", "group"), None, None, None))
    return jax.shard_map(local, mesh=mesh, in_specs=in_specs, out_specs=out_specs, check_vma=False)
```

```python
import functools
import math

import jax
import jax.numpy as jnp
from jax import lax
from jax.experimental import pallas as pl
from jax.experimental.pallas import tpu as pltpu
from jax.sharding import PartitionSpec as P

PAGE_ROWS = 128
epsilon = 1e-06
rope_base = 1000000.0
very_negative = -1e30
VMEM_BYTES = 48 * 1024 * 1024
PARTS = 2
CORES = 2
IN_FLIGHT = 4
SHARE = 0.1


def params():
    return pltpu.CompilerParams(vmem_limit_bytes=VMEM_BYTES)


def cost(flops, moved, transcendentals=0):
    return pl.CostEstimate(
        flops=int(flops * SHARE),
        bytes_accessed=int(moved * SHARE),
        transcendentals=int(transcendentals * SHARE),
    )


def hop_order(chips):
    return [0, 1, chips - 1] + list(range(2, chips - 1)) if chips > 2 else list(range(chips))


class Layout:
    def __init__(self, spans, pages, owners):
        self.chips = owners // CORES
        self.span_at = 0
        self.earlier_at = self.span_at + spans
        self.target_at = self.earlier_at + spans
        self.page = self.target_at + spans
        self.origin = self.page + pages
        self.group_rank = self.origin + owners * spans
        self.tensor_rank = self.group_rank + 1
        self.length = self.tensor_rank + 1


def tables_kernel(lay, spans, pages, ranks, prompt_spans, source, target, page_slot, out, span_of, start_of):
    chips = lay.chips
    group_rank = ranks[0]
    out[lay.group_rank] = group_rank
    out[lay.tensor_rank] = ranks[1]
    for k in range(spans):
        start = jnp.int32(0)
        begin = jnp.int32(0)
        for p in range(prompt_spans.shape[0]):
            start = jnp.where(begin <= k, begin, start)
            begin = begin + prompt_spans[p]
        start_of[k] = start
        span_of[source[k]] = jnp.int32(k)
    for p in range(pages):
        out[lay.page + page_slot[p]] = jnp.int32(p)
    chip, core = lax.div(group_rank, CORES), lax.rem(group_rank, CORES)
    hops = hop_order(chips)
    for back in range(chips):
        for other in range(CORES):
            at_chip = lax.rem(chip + chips - back, chips)
            at_core = jnp.where(other == 0, core, 1 - core)
            for n, hop in enumerate(hops):
                for flip in range(CORES):
                    from_chip = lax.rem(at_chip + chips - hop, chips)
                    from_core = jnp.where(flip == 0, at_core, 1 - at_core)
                    k = span_of[from_chip * CORES + from_core]
                    place = n * CORES + flip
                    out[lay.origin + (back * CORES + other) * spans + place] = k
                    if back == 0 and other == 0:
                        out[lay.span_at + place] = k
                        out[lay.earlier_at + place] = k - start_of[k]
                        out[lay.target_at + place] = target[k]


def make_tables(lay, spans, pages, ranks, prompt_spans, source, target, page_slot):
    smem = pl.BlockSpec(memory_space=pltpu.SMEM)
    return pl.pallas_call(
        functools.partial(tables_kernel, lay, spans, pages),
        out_shape=jax.ShapeDtypeStruct((lay.length,), jnp.int32),
        in_specs=[smem] * 5,
        out_specs=smem,
        scratch_shapes=[pltpu.SMEM((spans,), jnp.int32)] * 2,
        name="tables",
    )(ranks, prompt_spans, source, target, page_slot)


def head_norm_rope(u, gain, cosine, sine):
    mean_sq = jnp.mean(u * u, axis=-1, keepdims=True)
    u = u * lax.rsqrt(mean_sq + epsilon) * gain
    half = u.shape[-1] // 2
    return u * cosine + pltpu.roll(u, half, 1) * sine


def half_index(lay, sides, side):
    if sides == 1:
        return lambda t: 0
    if side == 0:
        return lambda t: t[lay.tensor_rank]
    return lambda t: 1 - t[lay.tensor_rank]


def summed_dot(lefts, rights):
    total = None
    for left, right in zip(lefts, rights):
        term = jnp.dot(left[...], right[...], preferred_element_type=jnp.float32)
        total = term if total is None else total + term
    return total


def kv_kernel(sides, blocks, table, *refs):
    refs = list(refs)
    take = lambda n: [refs.pop(0) for _ in range(n)]
    xs = [take(blocks) for _ in range(sides)]
    gains, wks, wvs = take(sides), take(sides), take(sides)
    kgain, cosine, sine = take(3)
    normed, (kv,) = take(sides), take(1)
    head = kgain.shape[1]
    width = sum(x[0].shape[1] for x in xs)

    @pl.when(pl.program_id(0) == 0)
    def _():
        at = 0
        for b in range(blocks):
            wide = [x[b][...].astype(jnp.float32) for x in xs]
            total = sum(jnp.sum(w * w, axis=-1, keepdims=True) for w in wide)
            factor = lax.rsqrt(total / width + epsilon)
            rows = xs[0][b].shape[0]
            for w, gain, to in zip(wide, gains, normed):
                to[at : at + rows] = (w * factor * gain[...].astype(jnp.float32)).astype(
                    jnp.bfloat16
                )
            at += rows

    keys = summed_dot(normed, wks).astype(jnp.bfloat16)
    gains = kgain[...].astype(jnp.float32)
    for h in range(keys.shape[1] // head):
        u = keys[:, h * head : (h + 1) * head].astype(jnp.float32)
        kv[0, :, h * head : (h + 1) * head] = head_norm_rope(
            u, gains, cosine[...], sine[...]
        ).astype(jnp.bfloat16)
    kv[1] = summed_dot(normed, wvs).astype(jnp.bfloat16)


def make_kv(lay, table, xs, gains, wk, wv, kgain, cosine, sine, part):
    sides, blocks = len(xs), len(xs[0])
    rows = sum(x.shape[0] for x in xs[0])
    widths = [x[0].shape[1] for x in xs]
    width, cols = wk.shape
    tile = 256 if cols % 256 == 0 else cols
    head = kgain.shape[1]
    fixed = lambda n, t: (0, 0)
    here = lambda n, t: (part, 0)
    weights = []
    for side in range(sides):
        index = half_index(lay, sides, side)
        weights.append(
            pl.BlockSpec((widths[side], tile), lambda n, t, index=index: (index(t), n))
        )
    return pl.pallas_call(
        functools.partial(kv_kernel, sides, blocks),
        grid_spec=pltpu.PrefetchScalarGridSpec(
            num_scalar_prefetch=1,
            grid=(cols // tile,),
            in_specs=[pl.BlockSpec(x.shape, fixed) for side in xs for x in side]
            + [pl.BlockSpec((1, w), fixed) for w in widths]
            + weights
            + weights
            + [
                pl.BlockSpec((1, head), fixed),
                pl.BlockSpec((rows, head), here),
                pl.BlockSpec((rows, head), here),
            ],
            out_specs=[pl.BlockSpec((rows, w), fixed) for w in widths]
            + [pl.BlockSpec((2, rows, tile), lambda n, t: (0, 0, n))],
        ),
        out_shape=[jax.ShapeDtypeStruct((rows, w), jnp.bfloat16) for w in widths]
        + [jax.ShapeDtypeStruct((2, rows, cols), jnp.bfloat16)],
        compiler_params=params(),
        cost_estimate=cost(4 * rows * width * cols, 4 * width * cols + 4 * rows * width),
        name="keys_values",
    )(
        table, *[x for side in xs for x in side], *gains, *[wk] * sides, *[wv] * sides,
        kgain, cosine, sine,
    )


def q_kernel(sides, table, *refs):
    normed, wqs = refs[:sides], refs[sides : 2 * sides]
    qgain, cosine, sine, out = refs[2 * sides :]
    head = qgain.shape[1]
    lin = summed_dot(normed, wqs)
    gains = qgain[...].astype(jnp.float32)
    for h in range(lin.shape[1] // head):
        out[:, h * head : (h + 1) * head] = head_norm_rope(
            lin[:, h * head : (h + 1) * head], gains, cosine[...], sine[...]
        ).astype(jnp.bfloat16)


def make_q(lay, table, normed, wq, qgain, cosine, sine, part):
    sides = len(normed)
    rows = normed[0].shape[0]
    width, cols = wq.shape
    tile = 512 if cols % 512 == 0 else cols
    head = qgain.shape[1]
    fixed = lambda n, t: (0, 0)
    here = lambda n, t: (part, 0)
    weights = []
    for side in range(sides):
        index = half_index(lay, sides, side)
        weights.append(
            pl.BlockSpec(
                (normed[side].shape[1], tile), lambda n, t, index=index: (index(t), n)
            )
        )
    return pl.pallas_call(
        functools.partial(q_kernel, sides),
        grid_spec=pltpu.PrefetchScalarGridSpec(
            num_scalar_prefetch=1,
            grid=(cols // tile,),
            in_specs=[pl.BlockSpec(x.shape, fixed) for x in normed]
            + weights
            + [
                pl.BlockSpec((1, head), fixed),
                pl.BlockSpec((rows, head), here),
                pl.BlockSpec((rows, head), here),
            ],
            out_specs=pl.BlockSpec((rows, tile), lambda n, t: (0, n)),
        ),
        out_shape=jax.ShapeDtypeStruct((rows, cols), jnp.bfloat16),
        compiler_params=params(),
        cost_estimate=cost(2 * rows * width * cols, 2 * width * cols + 2 * rows * (width + cols)),
        name="queries",
    )(table, *normed, *[wq] * sides, qgain, cosine, sine)


def attention_kernel(lay, spans, most, per_kv, head, owners, pages_each, table, *refs):
    q_refs = refs[:PARTS]
    kv_refs = refs[PARTS : PARTS + owners * PARTS]
    out, pages, keys, values = refs[PARTS + owners * PARTS :]
    chips = lay.chips
    here, rows = kv_refs[0].shape[1], kv_refs[0].shape[2]
    group_rank = table[lay.group_rank]
    chip, core = lax.div(group_rank, CORES), lax.rem(group_rank, CORES)
    for o in range(owners):
        back, other = o // CORES, o % CORES
        owner = lax.rem(chip + chips - back, chips) * CORES + (core if other == 0 else 1 - core)
        at = pl.ds(pl.multiple_of(owner * rows, rows), rows)
        for p in range(PARTS):
            for i in range(here):
                k = table[lay.origin + o * spans + p * here + i]
                keys[k, at] = kv_refs[o * PARTS + p][0, i]
                values[k, at] = kv_refs[o * PARTS + p][1, i]

    for i in range(pages_each):
        page = table[lay.page + group_rank * pages_each + i]
        k = lax.div(page, pages_each)
        at = pl.ds(pl.multiple_of(lax.rem(page, pages_each) * PAGE_ROWS, PAGE_ROWS), PAGE_ROWS)
        pages[i, 0] = keys[k, at]
        pages[i, 1] = values[k, at]

    scale = (1.0 / math.sqrt(head)) * math.log2(math.e)
    q_rows, k_rows = per_kv * rows, owners * rows
    row = lax.broadcasted_iota(jnp.int32, (q_rows, k_rows), 0)
    col = lax.broadcasted_iota(jnp.int32, (q_rows, k_rows), 1)
    allowed = col <= group_rank * rows + row % rows

    def one_place(p, i, carry):
        k = table[lay.span_at + p * here + i]
        earlier = table[lay.earlier_at + p * here + i]
        queries = jnp.concatenate(
            [q_refs[p][i, :, g * head : (g + 1) * head] for g in range(per_kv)], axis=0
        )

        def with_earlier(count):
            scores = []
            for back in range(count + 1):
                s = lax.dot_general(
                    queries, keys[k - back], (((1,), (1,)), ((), ())),
                    preferred_element_type=jnp.float32,
                )
                if back == 0:
                    s = jnp.where(allowed, s, very_negative)
                scores.append(s)
            best = scores[0]
            for s in scores[1:]:
                best = jnp.maximum(best, s)
            best = jnp.max(best, axis=-1, keepdims=True)
            total = None
            summed = None
            for back, s in enumerate(scores):
                w = jnp.exp2((s - best) * scale)
                part = jnp.sum(w, axis=-1, keepdims=True)
                term = jnp.dot(
                    w.astype(jnp.bfloat16), values[k - back], preferred_element_type=jnp.float32
                )
                total = part if total is None else total + part
                summed = term if summed is None else summed + term
            result = (summed / total).astype(jnp.bfloat16)
            for g in range(per_kv):
                out[p * here + i, :, g * head : (g + 1) * head] = result[
                    g * rows : (g + 1) * rows
                ]

        for count in range(most):
            pl.when(earlier == count)(functools.partial(with_earlier, count))
        return carry

    for p in range(PARTS):
        lax.fori_loop(0, here, functools.partial(one_place, p), 0)


def make_attention(lay, most, table, queries, gathered, per_kv, head, pages_each, first, count):
    here, rows, cols = queries[0].shape
    spans = here * PARTS
    owners = len(gathered)
    q_spec = pl.BlockSpec((here, rows, per_kv * head), lambda h, t: (0, 0, first + h))
    kv_spec = pl.BlockSpec((2, here, rows, head), lambda h, t: (0, 0, 0, first + h))
    flat = [x for origin in gathered for x in origin]
    all_rows = spans * rows
    pairs = 2.2 * all_rows * owners * rows * per_kv * count
    return pl.pallas_call(
        functools.partial(
            attention_kernel, lay, spans, most, per_kv, head, owners, pages_each
        ),
        grid_spec=pltpu.PrefetchScalarGridSpec(
            num_scalar_prefetch=1,
            grid=(count,),
            in_specs=[q_spec] * PARTS + [kv_spec] * len(flat),
            out_specs=[
                pl.BlockSpec((spans, rows, per_kv * head), lambda h, t: (0, 0, h)),
                pl.BlockSpec((pages_each, 2, PAGE_ROWS, head), lambda h, t: (0, 0, 0, h)),
            ],
            scratch_shapes=[pltpu.VMEM((spans, owners * rows, head), jnp.bfloat16)] * 2,
        ),
        out_shape=[
            jax.ShapeDtypeStruct((spans, rows, count * per_kv * head), jnp.bfloat16),
            jax.ShapeDtypeStruct((pages_each, 2, PAGE_ROWS, count * head), jnp.bfloat16),
        ],
        compiler_params=params(),
        cost_estimate=cost(
            4 * pairs * head, 4 * all_rows * cols + 2 * len(flat) * flat[0].size, pairs
        ),
        name="attention",
    )(table, *queries, *flat)


def project_kernel(pieces, table, *refs):
    attended, wo, out = refs[:pieces], refs[pieces], refs[-1]
    total, at = None, 0
    for piece in attended:
        depth = piece.shape[1]
        term = jnp.dot(piece[...], wo[at : at + depth], preferred_element_type=jnp.float32)
        total = term if total is None else total + term
        at += depth
    out[...] = total.astype(jnp.bfloat16)


def make_projection(lay, table, attended, wo, first, count, tile, name, follows=()):
    rows = attended[0].shape[0]
    depth = wo.shape[0]
    return pl.pallas_call(
        functools.partial(project_kernel, len(attended)),
        grid_spec=pltpu.PrefetchScalarGridSpec(
            num_scalar_prefetch=1,
            grid=(count,),
            in_specs=[pl.BlockSpec(x.shape, lambda n, t: (0, 0)) for x in attended]
            + [pl.BlockSpec((depth, tile), lambda n, t: (0, first(t[lay.tensor_rank]) + n))]
            + [pl.BlockSpec(memory_space=pl.ANY)] * len(follows),
            out_specs=pl.BlockSpec((rows, tile), lambda n, t: (0, n)),
        ),
        out_shape=jax.ShapeDtypeStruct((rows, count * tile), jnp.bfloat16),
        compiler_params=params(),
        cost_estimate=cost(
            2 * rows * depth * count * tile, 2 * (rows * depth + (rows + depth) * count * tile)
        ),
        name=name,
    )(table, *attended, wo, *follows)


def add_kernel(lay, table, *refs):
    x_refs, own, received, out = refs[:-3], refs[-3], refs[-2], refs[-1]
    for place, x in enumerate(x_refs):
        summed = own[place].astype(jnp.float32) + received[place].astype(jnp.float32)
        out[table[lay.target_at + place]] = (x[...].astype(jnp.float32) + summed).astype(
            jnp.bfloat16
        )


def make_sum(lay, table, arrived, own, received, first):
    spans, rows, cols = received.shape
    unit = math.gcd(first, cols) if first else cols
    steps, start = cols // unit, first // unit
    return pl.pallas_call(
        functools.partial(add_kernel, lay),
        grid_spec=pltpu.PrefetchScalarGridSpec(
            num_scalar_prefetch=1,
            grid=(steps,),
            in_specs=[pl.BlockSpec((rows, unit), lambda n, t: (0, start + n))] * spans
            + [
                pl.BlockSpec((spans, rows, unit), lambda n, t: (0, 0, n)),
                pl.BlockSpec((spans, rows, unit), lambda n, t: (0, 0, n)),
            ],
            out_specs=pl.BlockSpec((spans, rows, unit), lambda n, t: (0, 0, n)),
        ),
        out_shape=jax.ShapeDtypeStruct((spans, rows, cols), jnp.bfloat16),
        compiler_params=params(),
        cost_estimate=cost(3 * spans * rows * cols, 8 * spans * rows * cols),
        name="residual",
    )(table, *arrived, own, received)


def rope_tables(earlier, span_len, first_row, rows, head):
    half = head // 2
    freqs = jnp.power(
        jnp.float32(rope_base), -jnp.arange(half, dtype=jnp.float32) * 2.0 / head
    )
    at = earlier[:, None] * span_len + first_row + jnp.arange(rows, dtype=jnp.int32)[None, :]
    angles = at.reshape(-1).astype(jnp.float32)[:, None] * freqs[None, :]
    cosine, sine = jnp.cos(angles), jnp.sin(angles)
    return (
        jnp.concatenate([cosine, cosine], axis=1),
        jnp.concatenate([-sine, sine], axis=1),
    )


def widths_of(tiles):
    return [1, 2, 1, 1] if tiles == 5 else [1, tiles - 1]


def after(x, done):
    return lax.optimization_barrier((x, done))[0]


def shift(x, owners, hop, flip):
    chips = owners // CORES
    pairs = [
        (z * CORES + c, (z + hop) % chips * CORES + (c ^ flip))
        for z in range(chips)
        for c in range(CORES)
    ]
    return lax.ppermute(x, "group", pairs)


def local(
    hidden_in, ln_gain, wq, wk, wv, q_gain, key_norm_gain, wo,
    prompt_spans, span_source, span_target, page_slot,
):
    _, span_len, cols = hidden_in.shape
    tensor_size = lax.axis_size("tensor")
    owners = lax.axis_size("group")
    tensor_rank = lax.axis_index("tensor")
    group_rank = lax.axis_index("group")
    chips = owners // CORES
    head = q_gain.shape[0]
    rows = span_len // owners
    pages_each = span_len // PAGE_ROWS
    spans = span_source.shape[0]
    here = spans // PARTS
    most = min(spans - (prompt_spans.shape[0] - 1), spans // 2)
    kv_cols = wk.shape[1]
    paired = tensor_size == 2
    swap = [(0, 1), (1, 0)]
    lay = Layout(spans, spans * pages_each, owners)

    if kv_cols < head:
        share = head // kv_cols
        sets = [list(range(i, i + share)) for i in range(0, tensor_size, share)]
        wk, wv = [
            lax.all_gather(w, "tensor", axis=1, tiled=True, axis_index_groups=sets)
            for w in (wk, wv)
        ]
    per_kv = wq.shape[1] // max(head, wk.shape[1])

    chip, core = group_rank // CORES, group_rank % CORES
    split = hidden_in.reshape(owners, rows, cols)
    arrived, crossed = [], []
    for hop in hop_order(chips):
        for flip in range(CORES):
            to = lax.rem(chip + hop, chips) * CORES + lax.rem(core + flip, CORES)
            block = lax.dynamic_index_in_dim(split, to, 0, keepdims=False)
            if hop or flip:
                if paired and len(arrived) > IN_FLIGHT:
                    block = after(block, crossed[len(arrived) - IN_FLIGHT - 1])
                block = shift(block, owners, hop, flip)
            arrived.append(block)
            if paired:
                crossed.append(lax.ppermute(block, "tensor", swap))

    ranks = jnp.stack([group_rank, tensor_rank]).astype(jnp.int32)
    table = make_tables(
        lay, spans, spans * pages_each, ranks, prompt_spans, span_source, span_target, page_slot
    )
    earlier = table[lay.earlier_at : lay.earlier_at + spans]
    cosine, sine = rope_tables(earlier, span_len, group_rank * rows, rows, head)

    if paired:
        gain = ln_gain[None]
        gains = [gain, lax.ppermute(gain, "tensor", swap)]
    else:
        gains = [lax.all_gather(ln_gain, "tensor", axis=0, tiled=True)[None]]

    queries, gathered = [], [[] for _ in range(owners)]
    for p in range(PARTS):
        at = slice(p * here, (p + 1) * here)
        if paired:
            xs = [arrived[at], crossed[at]]
        else:
            xs = [[lax.all_gather(jnp.concatenate(arrived[at]), "tensor", axis=1, tiled=True)]]
        kgain = key_norm_gain[None]
        if queries:
            kgain = after(kgain, queries[-1])
        *normed, kv = make_kv(lay, table, xs, gains, wk, wv, kgain, cosine, sine, p)
        kv = kv.reshape(2, here, rows, kv.shape[2])
        for back in range(chips):
            if back:
                if p and back == chips // 2:
                    kv = after(kv, queries[-1])
                kv = shift(kv, owners, 1, 0)
            gathered[back * CORES].append(kv)
            gathered[back * CORES + 1].append(shift(kv, owners, 0, 1))
            if back == 1 or chips == 1:
                qgain = q_gain[None]
                if p:
                    qgain = after(qgain, gathered[(chips // 2) * CORES][0])
                made = make_q(lay, table, normed, wq, qgain, cosine, sine, p)
                queries.append(made.reshape(here, rows, made.shape[1]))

    own_kv = wk.shape[1] // head
    sets = [own_kv // 2, own_kv - own_kv // 2] if own_kv > 1 else [own_kv]
    attended, pages, first = [], [], 0
    for count in sets:
        made, cut = make_attention(
            lay, most, table, queries, gathered, per_kv, head, pages_each, first, count
        )
        attended.append(made.reshape(spans * rows, -1))
        pages.append(cut)
        first += count

    if paired:
        tile = 512
        half_tiles = cols // tile
        widths = widths_of(half_tiles)
        others = [lax.ppermute(pages[0], "tensor", swap)]
        own, received, moved, starts = [], [], [], []
        for n in range(len(widths) + 1):
            if n < len(widths):
                first = sum(widths[:n])
                starts.append(first * tile)
                follows = (others[0],) if n == 0 else own[-1:] if n == 1 else moved[-1:]
                sent = make_projection(
                    lay, table, attended, wo,
                    lambda r, first=first: (1 - r) * half_tiles + first,
                    widths[n], tile, "send_part", follows,
                )
                received.append(lax.ppermute(sent, "tensor", swap).reshape(spans, rows, -1))
                own.append(make_projection(
                    lay, table, attended, wo,
                    lambda r, first=first: r * half_tiles + first,
                    widths[n], tile, "own_part", (sent,),
                ).reshape(spans, rows, -1))
            if n:
                moved.append(
                    make_sum(lay, table, arrived, own[n - 1], received[n - 1], starts[n - 1])
                )
        for cut in pages[1:]:
            others.append(lax.ppermute(after(cut, received[-2]), "tensor", swap))
        low = [jnp.where(tensor_rank == 0, a, b) for a, b in zip(pages, others)]
        high = [jnp.where(tensor_rank == 0, b, a) for a, b in zip(pages, others)]
        cache = jnp.concatenate(low + high, axis=3)
        pieces = [
            lax.all_to_all(rows_of, "group", split_axis=0, concat_axis=0, tiled=True)
            for rows_of in moved
        ]
        mixed = jnp.concatenate(pieces, axis=2).reshape(1, span_len, cols)
    else:
        pages = jnp.concatenate(pages, axis=3)
        attended = jnp.concatenate(attended, axis=1)
        if kv_cols < head:
            pages = lax.dynamic_slice_in_dim(
                pages, lax.rem(tensor_rank, head // kv_cols) * kv_cols, kv_cols, 3
            )
        cache = lax.all_gather(pages, "tensor", axis=3, tiled=True)
        partial = jnp.dot(attended, wo, preferred_element_type=jnp.float32)
        summed = lax.psum_scatter(
            partial.astype(jnp.bfloat16), "tensor", scatter_dimension=1, tiled=True
        )
        summed = summed.reshape(spans, rows, cols).astype(jnp.float32)
        moved = (jnp.stack(arrived).astype(jnp.float32) + summed).astype(jnp.bfloat16)
        targets = table[lay.target_at : lay.target_at + spans]
        moved = jnp.zeros_like(moved).at[targets].set(moved, unique_indices=True)
        moved = lax.all_to_all(moved, "group", split_axis=0, concat_axis=0, tiled=True)
        mixed = moved.reshape(1, span_len, cols)
    return (mixed, cache)


def solution(mesh):
    in_specs = (
        P(("replica", "group"), None, "tensor"),
        P("tensor"),
        P(None, "tensor"),
        P(None, "tensor"),
        P(None, "tensor"),
        P(),
        P(),
        P("tensor", None),
        P("replica"),
        P("replica"),
        P("replica"),
        P("replica"),
    )
    out_specs = (P(("replica", "group"), None, "tensor"), P(("replica", "group"), None, None, None))
    return jax.shard_map(local, mesh=mesh, in_specs=in_specs, out_specs=out_specs, check_vma=False)
```

```python
import functools
import math

import jax
import jax.numpy as jnp
from jax import lax
from jax.experimental import pallas as pl
from jax.experimental.pallas import tpu as pltpu
from jax.sharding import PartitionSpec as P

PAGE_ROWS = 128
epsilon = 1e-06
rope_base = 1000000.0
very_negative = -1e30
VMEM_BYTES = 48 * 1024 * 1024
PARTS = 2
CORES = 2
SHARE = 0.1


def params():
    return pltpu.CompilerParams(vmem_limit_bytes=VMEM_BYTES)


def cost(flops, moved, transcendentals=0):
    return pl.CostEstimate(
        flops=int(flops * SHARE),
        bytes_accessed=int(moved * SHARE),
        transcendentals=int(transcendentals * SHARE),
    )


def hop_order(chips):
    return [0, 1, chips - 1] + list(range(2, chips - 1)) if chips > 2 else list(range(chips))


class Layout:
    def __init__(self, spans, pages, owners):
        self.chips = owners // CORES
        self.span_at = 0
        self.earlier_at = self.span_at + spans
        self.target_at = self.earlier_at + spans
        self.sent_as = self.target_at + spans
        self.page = self.sent_as + spans
        self.origin = self.page + pages
        self.group_rank = self.origin + owners * spans
        self.tensor_rank = self.group_rank + 1
        self.length = self.tensor_rank + 1


def tables_kernel(lay, spans, pages, ranks, prompt_spans, source, target, page_slot, out, span_of, start_of):
    chips = lay.chips
    group_rank = ranks[0]
    out[lay.group_rank] = group_rank
    out[lay.tensor_rank] = ranks[1]
    for k in range(spans):
        start = jnp.int32(0)
        begin = jnp.int32(0)
        for p in range(prompt_spans.shape[0]):
            start = jnp.where(begin <= k, begin, start)
            begin = begin + prompt_spans[p]
        start_of[k] = start
        span_of[source[k]] = jnp.int32(k)
    for p in range(pages):
        out[lay.page + page_slot[p]] = jnp.int32(p)
    chip, core = lax.div(group_rank, CORES), lax.rem(group_rank, CORES)
    hops = hop_order(chips)
    for back in range(chips):
        for other in range(CORES):
            at_chip = lax.rem(chip + chips - back, chips)
            at_core = jnp.where(other == 0, core, 1 - core)
            for n, hop in enumerate(hops):
                for flip in range(CORES):
                    from_chip = lax.rem(at_chip + chips - hop, chips)
                    from_core = jnp.where(flip == 0, at_core, 1 - at_core)
                    k = span_of[from_chip * CORES + from_core]
                    place = n * CORES + flip
                    out[lay.origin + (back * CORES + other) * spans + place] = k
                    if back == 0 and other == 0:
                        out[lay.span_at + place] = k
                        out[lay.earlier_at + place] = k - start_of[k]
                        owner = target[k]
                        ahead = lax.rem(lax.div(owner, CORES) + chips - chip, chips)
                        turn = jnp.int32(0)
                        for m, other_hop in enumerate(hops):
                            turn = jnp.where(ahead == other_hop, jnp.int32(m), turn)
                        crossing = jnp.where(lax.rem(owner, CORES) == core, 0, 1)
                        out[lay.target_at + place] = owner
                        out[lay.sent_as + place] = turn * CORES + crossing


def make_tables(lay, spans, pages, ranks, prompt_spans, source, target, page_slot):
    smem = pl.BlockSpec(memory_space=pltpu.SMEM)
    return pl.pallas_call(
        functools.partial(tables_kernel, lay, spans, pages),
        out_shape=jax.ShapeDtypeStruct((lay.length,), jnp.int32),
        in_specs=[smem] * 5,
        out_specs=smem,
        scratch_shapes=[pltpu.SMEM((spans,), jnp.int32)] * 2,
        name="tables",
    )(ranks, prompt_spans, source, target, page_slot)


def head_norm_rope(u, gain, cosine, sine):
    mean_sq = jnp.mean(u * u, axis=-1, keepdims=True)
    u = u * lax.rsqrt(mean_sq + epsilon) * gain
    half = u.shape[-1] // 2
    return u * cosine + pltpu.roll(u, half, 1) * sine


def half_index(lay, sides, side):
    if sides == 1:
        return lambda t: 0
    if side == 0:
        return lambda t: t[lay.tensor_rank]
    return lambda t: 1 - t[lay.tensor_rank]


def summed_dot(lefts, rights):
    total = None
    for left, right in zip(lefts, rights):
        term = jnp.dot(left[...], right[...], preferred_element_type=jnp.float32)
        total = term if total is None else total + term
    return total


def kv_kernel(sides, blocks, table, *refs):
    refs = list(refs)
    take = lambda n: [refs.pop(0) for _ in range(n)]
    xs = [take(blocks) for _ in range(sides)]
    gains, wks, wvs = take(sides), take(sides), take(sides)
    kgain, cosine, sine = take(3)
    normed, (kv,) = take(sides), take(1)
    head = kgain.shape[1]
    width = sum(x[0].shape[1] for x in xs)

    @pl.when(pl.program_id(0) == 0)
    def _():
        at = 0
        for b in range(blocks):
            wide = [x[b][...].astype(jnp.float32) for x in xs]
            total = sum(jnp.sum(w * w, axis=-1, keepdims=True) for w in wide)
            factor = lax.rsqrt(total / width + epsilon)
            rows = xs[0][b].shape[0]
            for w, gain, to in zip(wide, gains, normed):
                to[at : at + rows] = (w * factor * gain[...].astype(jnp.float32)).astype(
                    jnp.bfloat16
                )
            at += rows

    keys = summed_dot(normed, wks).astype(jnp.bfloat16)
    gains = kgain[...].astype(jnp.float32)
    for h in range(keys.shape[1] // head):
        u = keys[:, h * head : (h + 1) * head].astype(jnp.float32)
        kv[0, :, h * head : (h + 1) * head] = head_norm_rope(
            u, gains, cosine[...], sine[...]
        ).astype(jnp.bfloat16)
    kv[1] = summed_dot(normed, wvs).astype(jnp.bfloat16)


def make_kv(lay, table, xs, gains, wk, wv, kgain, cosine, sine, part):
    sides, blocks = len(xs), len(xs[0])
    rows = sum(x.shape[0] for x in xs[0])
    widths = [x[0].shape[1] for x in xs]
    width, cols = wk.shape
    tile = 256 if cols % 256 == 0 else cols
    head = kgain.shape[1]
    fixed = lambda n, t: (0, 0)
    here = lambda n, t: (part, 0)
    weights = []
    for side in range(sides):
        index = half_index(lay, sides, side)
        weights.append(
            pl.BlockSpec((widths[side], tile), lambda n, t, index=index: (index(t), n))
        )
    return pl.pallas_call(
        functools.partial(kv_kernel, sides, blocks),
        grid_spec=pltpu.PrefetchScalarGridSpec(
            num_scalar_prefetch=1,
            grid=(cols // tile,),
            in_specs=[pl.BlockSpec(x.shape, fixed) for side in xs for x in side]
            + [pl.BlockSpec((1, w), fixed) for w in widths]
            + weights
            + weights
            + [
                pl.BlockSpec((1, head), fixed),
                pl.BlockSpec((rows, head), here),
                pl.BlockSpec((rows, head), here),
            ],
            out_specs=[pl.BlockSpec((rows, w), fixed) for w in widths]
            + [pl.BlockSpec((2, rows, tile), lambda n, t: (0, 0, n))],
        ),
        out_shape=[jax.ShapeDtypeStruct((rows, w), jnp.bfloat16) for w in widths]
        + [jax.ShapeDtypeStruct((2, rows, cols), jnp.bfloat16)],
        compiler_params=params(),
        cost_estimate=cost(4 * rows * width * cols, 4 * width * cols + 4 * rows * width),
        name="keys_values",
    )(
        table, *[x for side in xs for x in side], *gains, *[wk] * sides, *[wv] * sides,
        kgain, cosine, sine,
    )


def q_kernel(sides, table, *refs):
    normed, wqs = refs[:sides], refs[sides : 2 * sides]
    qgain, cosine, sine, out = refs[2 * sides :]
    head = qgain.shape[1]
    lin = summed_dot(normed, wqs)
    gains = qgain[...].astype(jnp.float32)
    for h in range(lin.shape[1] // head):
        out[:, h * head : (h + 1) * head] = head_norm_rope(
            lin[:, h * head : (h + 1) * head], gains, cosine[...], sine[...]
        ).astype(jnp.bfloat16)


def make_q(lay, table, normed, wq, qgain, cosine, sine, part):
    sides = len(normed)
    rows = normed[0].shape[0]
    width, cols = wq.shape
    tile = 512 if cols % 512 == 0 else cols
    head = qgain.shape[1]
    fixed = lambda n, t: (0, 0)
    here = lambda n, t: (part, 0)
    weights = []
    for side in range(sides):
        index = half_index(lay, sides, side)
        weights.append(
            pl.BlockSpec(
                (normed[side].shape[1], tile), lambda n, t, index=index: (index(t), n)
            )
        )
    return pl.pallas_call(
        functools.partial(q_kernel, sides),
        grid_spec=pltpu.PrefetchScalarGridSpec(
            num_scalar_prefetch=1,
            grid=(cols // tile,),
            in_specs=[pl.BlockSpec(x.shape, fixed) for x in normed]
            + weights
            + [
                pl.BlockSpec((1, head), fixed),
                pl.BlockSpec((rows, head), here),
                pl.BlockSpec((rows, head), here),
            ],
            out_specs=pl.BlockSpec((rows, tile), lambda n, t: (0, n)),
        ),
        out_shape=jax.ShapeDtypeStruct((rows, cols), jnp.bfloat16),
        compiler_params=params(),
        cost_estimate=cost(2 * rows * width * cols, 2 * width * cols + 2 * rows * (width + cols)),
        name="queries",
    )(table, *normed, *[wq] * sides, qgain, cosine, sine)


def attention_kernel(lay, spans, most, per_kv, head, owners, pages_each, table, *refs):
    q_refs = refs[:PARTS]
    kv_refs = refs[PARTS : PARTS + owners * PARTS]
    out, pages, keys, values = refs[PARTS + owners * PARTS :]
    chips = lay.chips
    here, rows = kv_refs[0].shape[1], kv_refs[0].shape[2]
    group_rank = table[lay.group_rank]
    chip, core = lax.div(group_rank, CORES), lax.rem(group_rank, CORES)
    for o in range(owners):
        back, other = o // CORES, o % CORES
        owner = lax.rem(chip + chips - back, chips) * CORES + (core if other == 0 else 1 - core)
        at = pl.ds(pl.multiple_of(owner * rows, rows), rows)
        for p in range(PARTS):
            for i in range(here):
                k = table[lay.origin + o * spans + p * here + i]
                keys[k, at] = kv_refs[o * PARTS + p][0, i]
                values[k, at] = kv_refs[o * PARTS + p][1, i]

    for i in range(pages_each):
        page = table[lay.page + group_rank * pages_each + i]
        k = lax.div(page, pages_each)
        at = pl.ds(pl.multiple_of(lax.rem(page, pages_each) * PAGE_ROWS, PAGE_ROWS), PAGE_ROWS)
        pages[i, 0] = keys[k, at]
        pages[i, 1] = values[k, at]

    scale = (1.0 / math.sqrt(head)) * math.log2(math.e)
    q_rows, k_rows = per_kv * rows, owners * rows
    row = lax.broadcasted_iota(jnp.int32, (q_rows, k_rows), 0)
    col = lax.broadcasted_iota(jnp.int32, (q_rows, k_rows), 1)
    allowed = col <= group_rank * rows + row % rows

    def one_place(p, i, carry):
        k = table[lay.span_at + p * here + i]
        earlier = table[lay.earlier_at + p * here + i]
        queries = jnp.concatenate(
            [q_refs[p][i, :, g * head : (g + 1) * head] for g in range(per_kv)], axis=0
        )

        def with_earlier(count):
            scores = []
            for back in range(count + 1):
                s = lax.dot_general(
                    queries, keys[k - back], (((1,), (1,)), ((), ())),
                    preferred_element_type=jnp.float32,
                )
                if back == 0:
                    s = jnp.where(allowed, s, very_negative)
                scores.append(s)
            best = scores[0]
            for s in scores[1:]:
                best = jnp.maximum(best, s)
            best = jnp.max(best, axis=-1, keepdims=True)
            total = None
            summed = None
            for back, s in enumerate(scores):
                w = jnp.exp2((s - best) * scale)
                part = jnp.sum(w, axis=-1, keepdims=True)
                term = jnp.dot(
                    w.astype(jnp.bfloat16), values[k - back], preferred_element_type=jnp.float32
                )
                total = part if total is None else total + part
                summed = term if summed is None else summed + term
            result = (summed / total).astype(jnp.bfloat16)
            for g in range(per_kv):
                out[p * here + i, :, g * head : (g + 1) * head] = result[
                    g * rows : (g + 1) * rows
                ]

        for count in range(most):
            pl.when(earlier == count)(functools.partial(with_earlier, count))
        return carry

    for p in range(PARTS):
        lax.fori_loop(0, here, functools.partial(one_place, p), 0)


def make_attention(lay, most, table, queries, gathered, per_kv, head, pages_each, first, count):
    here, rows, cols = queries[0].shape
    spans = here * PARTS
    owners = len(gathered)
    q_spec = pl.BlockSpec((here, rows, per_kv * head), lambda h, t: (0, 0, first + h))
    kv_spec = pl.BlockSpec((2, here, rows, head), lambda h, t: (0, 0, 0, first + h))
    flat = [x for origin in gathered for x in origin]
    all_rows = spans * rows
    pairs = 2.2 * all_rows * owners * rows * per_kv * count
    return pl.pallas_call(
        functools.partial(
            attention_kernel, lay, spans, most, per_kv, head, owners, pages_each
        ),
        grid_spec=pltpu.PrefetchScalarGridSpec(
            num_scalar_prefetch=1,
            grid=(count,),
            in_specs=[q_spec] * PARTS + [kv_spec] * len(flat),
            out_specs=[
                pl.BlockSpec((spans, rows, per_kv * head), lambda h, t: (0, 0, h)),
                pl.BlockSpec((pages_each, 2, PAGE_ROWS, head), lambda h, t: (0, 0, 0, h)),
            ],
            scratch_shapes=[pltpu.VMEM((spans, owners * rows, head), jnp.bfloat16)] * 2,
        ),
        out_shape=[
            jax.ShapeDtypeStruct((spans, rows, count * per_kv * head), jnp.bfloat16),
            jax.ShapeDtypeStruct((pages_each, 2, PAGE_ROWS, count * head), jnp.bfloat16),
        ],
        compiler_params=params(),
        cost_estimate=cost(
            4 * pairs * head, 4 * all_rows * cols + 2 * len(flat) * flat[0].size, pairs
        ),
        name="attention",
    )(table, *queries, *flat)


def project_kernel(pieces, follows, tile, table, *refs):
    attended, wo, outs = refs[:pieces], refs[pieces], refs[pieces + 1 + follows :]
    total, at = None, 0
    for piece in attended:
        depth = piece.shape[1]
        term = jnp.dot(piece[...], wo[at : at + depth], preferred_element_type=jnp.float32)
        total = term if total is None else total + term
        at += depth
    total = total.astype(jnp.bfloat16)
    step = 0
    for out in outs:
        for at in range(0, out.shape[1], tile):

            @pl.when(pl.program_id(0) == step)
            def _(out=out, at=at):
                out[:, at : at + tile] = total

            step += 1


def make_projection(lay, table, attended, wo, tile, first, widths, name, follows=()):
    rows = attended[0].shape[0]
    depth = wo.shape[0]
    count = sum(widths)
    return pl.pallas_call(
        functools.partial(project_kernel, len(attended), len(follows), tile),
        grid_spec=pltpu.PrefetchScalarGridSpec(
            num_scalar_prefetch=1,
            grid=(count,),
            in_specs=[pl.BlockSpec(x.shape, lambda n, t: (0, 0)) for x in attended]
            + [pl.BlockSpec((depth, tile), lambda n, t: (0, first(t[lay.tensor_rank]) + n))]
            + [pl.BlockSpec(memory_space=pl.ANY)] * len(follows),
            out_specs=[pl.BlockSpec((rows, w * tile), lambda n, t: (0, 0)) for w in widths],
        ),
        out_shape=[jax.ShapeDtypeStruct((rows, w * tile), jnp.bfloat16) for w in widths],
        compiler_params=params(),
        cost_estimate=cost(
            2 * rows * depth * count * tile, 2 * (rows * depth + (rows + depth) * count * tile)
        ),
        name=name,
    )(table, *attended, wo, *follows)


def add_kernel(lay, blocks, table, *refs):
    x_refs, own, received = refs[:blocks], refs[blocks], refs[blocks + 1]
    outs, moved = refs[blocks + 2 : -1], refs[-1]
    rows = moved.shape[1]
    place = 0
    for x in x_refs:
        for at in range(0, x.shape[0], rows):
            summed = own[place].astype(jnp.float32) + received[place].astype(jnp.float32)
            moved[table[lay.sent_as + place]] = (
                x[at : at + rows].astype(jnp.float32) + summed
            ).astype(jnp.bfloat16)
            place += 1
    for n, out in enumerate(outs):
        for flip in range(CORES):
            out[flip] = moved[n * CORES + flip]


def make_sum(lay, table, arrived, own, received, first):
    spans, rows, cols = received.shape
    chunk = first // cols
    whole = lambda n, t: (0, 0, 0)
    return pl.pallas_call(
        functools.partial(add_kernel, lay, len(arrived)),
        grid_spec=pltpu.PrefetchScalarGridSpec(
            num_scalar_prefetch=1,
            grid=(1,),
            in_specs=[pl.BlockSpec((x.shape[0], cols), lambda n, t: (0, chunk)) for x in arrived]
            + [pl.BlockSpec((spans, rows, cols), whole)] * 2,
            out_specs=[pl.BlockSpec((CORES, rows, cols), whole)] * lay.chips,
            scratch_shapes=[pltpu.VMEM((spans, rows, cols), jnp.bfloat16)],
        ),
        out_shape=[jax.ShapeDtypeStruct((CORES, rows, cols), jnp.bfloat16)] * lay.chips,
        compiler_params=params(),
        cost_estimate=cost(3 * spans * rows * cols, 8 * spans * rows * cols),
        name="residual",
    )(table, *arrived, own, received)


def place_kernel(lay, table, *refs):
    same, swapped, out = refs[: lay.chips], refs[lay.chips], refs[-1]
    rows = swapped.shape[1]
    group_rank = table[lay.group_rank]
    chip, core = lax.div(group_rank, CORES), lax.rem(group_rank, CORES)
    for n, hop in enumerate(hop_order(lay.chips)):
        owner = lax.rem(chip + lay.chips - hop, lay.chips) * CORES
        for block, at_core in ((same[n][0], core), (swapped[n], 1 - core)):
            at = pl.multiple_of((owner + at_core) * rows, rows)
            out[pl.ds(at, rows)] = block


def make_placed(lay, table, same, swapped, first, cols, whole):
    chips, rows, tile = swapped.shape
    chunk = first // tile
    return pl.pallas_call(
        functools.partial(place_kernel, lay),
        grid_spec=pltpu.PrefetchScalarGridSpec(
            num_scalar_prefetch=1,
            grid=(1,),
            in_specs=[pl.BlockSpec((CORES, rows, tile), lambda n, t: (0, 0, 0))] * chips
            + [pl.BlockSpec((chips, rows, tile), lambda n, t: (0, 0, 0))]
            + [pl.BlockSpec(memory_space=pl.ANY)] * len(whole),
            out_specs=pl.BlockSpec((chips * CORES * rows, tile), lambda n, t: (0, chunk)),
        ),
        out_shape=jax.ShapeDtypeStruct((chips * CORES * rows, cols), jnp.bfloat16),
        input_output_aliases={chips + 2: 0} if whole else {},
        compiler_params=params(),
        cost_estimate=cost(0, 4 * chips * CORES * rows * tile),
        name="placed",
    )(table, *same, swapped, *whole)


def rope_tables(earlier, span_len, first_row, rows, head):
    half = head // 2
    freqs = jnp.power(
        jnp.float32(rope_base), -jnp.arange(half, dtype=jnp.float32) * 2.0 / head
    )
    at = earlier[:, None] * span_len + first_row + jnp.arange(rows, dtype=jnp.int32)[None, :]
    angles = at.reshape(-1).astype(jnp.float32)[:, None] * freqs[None, :]
    cosine, sine = jnp.cos(angles), jnp.sin(angles)
    return (
        jnp.concatenate([cosine, cosine], axis=1),
        jnp.concatenate([-sine, sine], axis=1),
    )


def after(x, done):
    return lax.optimization_barrier((x, done))[0]


def shift(x, owners, hop, flip):
    chips = owners // CORES
    pairs = [
        (z * CORES + c, (z + hop) % chips * CORES + (c ^ flip))
        for z in range(chips)
        for c in range(CORES)
    ]
    return lax.ppermute(x, "group", pairs)


def local(
    hidden_in, ln_gain, wq, wk, wv, q_gain, key_norm_gain, wo,
    prompt_spans, span_source, span_target, page_slot,
):
    _, span_len, cols = hidden_in.shape
    tensor_size = lax.axis_size("tensor")
    owners = lax.axis_size("group")
    tensor_rank = lax.axis_index("tensor")
    group_rank = lax.axis_index("group")
    chips = owners // CORES
    head = q_gain.shape[0]
    rows = span_len // owners
    pages_each = span_len // PAGE_ROWS
    spans = span_source.shape[0]
    here = spans // PARTS
    most = min(spans - (prompt_spans.shape[0] - 1), spans // 2)
    kv_cols = wk.shape[1]
    paired = tensor_size == 2
    swap = [(0, 1), (1, 0)]
    lay = Layout(spans, spans * pages_each, owners)

    if kv_cols < head:
        share = head // kv_cols
        sets = [list(range(i, i + share)) for i in range(0, tensor_size, share)]
        wk, wv = [
            lax.all_gather(w, "tensor", axis=1, tiled=True, axis_index_groups=sets)
            for w in (wk, wv)
        ]
    per_kv = wq.shape[1] // max(head, wk.shape[1])

    chip, core = group_rank // CORES, group_rank % CORES
    split = hidden_in.reshape(chips, CORES, rows, cols)
    mine, theirs = [
        lax.dynamic_index_in_dim(split, at, 1, keepdims=False) for at in (core, 1 - core)
    ]
    theirs = shift(theirs, owners, 0, 1)
    pairs = []
    for hop in hop_order(chips):
        at = lax.rem(chip + hop, chips)
        pairs.append([lax.dynamic_index_in_dim(x, at, 0, keepdims=False) for x in (mine, theirs)])
    arrived = [jnp.concatenate(pairs[0])]
    moves = [(hop, [jnp.concatenate(pair)]) for hop, pair in zip(hop_order(chips), pairs)][1:]
    if len(moves) > 1:
        moves[-1] = (moves[-1][0], pairs[-1])
    moves = [(hop, block) for hop, blocks in moves for block in blocks]

    ranks = jnp.stack([group_rank, tensor_rank]).astype(jnp.int32)
    table = make_tables(
        lay, spans, spans * pages_each, ranks, prompt_spans, span_source, span_target, page_slot
    )
    earlier = table[lay.earlier_at : lay.earlier_at + spans]
    cosine, sine = rope_tables(earlier, span_len, group_rank * rows, rows, head)

    cross = lambda x: lax.ppermute(x, "tensor", swap)
    crossed = [cross(arrived[0])] if paired else []
    if paired:
        gain = ln_gain[None]
        gains = [gain, cross(after(gain, crossed[0]))]
    else:
        gains = [lax.all_gather(ln_gain, "tensor", axis=0, tiled=True)[None]]

    queries, gathered = [], [[] for _ in range(owners)]

    def make_part(p, own_rows, crossed_rows):
        if paired:
            xs = [own_rows, crossed_rows]
        else:
            xs = [[lax.all_gather(jnp.concatenate(own_rows), "tensor", axis=1, tiled=True)]]
        kgain = key_norm_gain[None]
        *normed, kv = make_kv(lay, table, xs, gains, wk, wv, kgain, cosine, sine, p)
        kv = kv.reshape(2, here, rows, kv.shape[2])
        for back in range(chips):
            if back:
                if p and back == chips // 2:
                    kv = after(kv, queries[-1])
                kv = shift(kv, owners, 1, 0)
            gathered[back * CORES].append(kv)
            gathered[back * CORES + 1].append(shift(kv, owners, 0, 1))
            if back == 1 or chips == 1:
                qgain = q_gain[None]
                if p:
                    qgain = after(qgain, gathered[(chips // 2) * CORES][0])
                made = make_q(lay, table, normed, wq, qgain, cosine, sine, p)
                queries.append(made.reshape(here, rows, made.shape[1]))

    begun = 0
    for m in range(len(moves) + 1):
        if m:
            hop, block = moves[m - 1]
            if paired and m > 1:
                block = after(block, crossed[m - 2])
            arrived.append(shift(block, owners, hop, 0))
            if paired:
                block = arrived[-1]
                if m == len(moves) and queries:
                    block = after(block, queries[0])
                crossed.append(cross(block))
        if sum(x.shape[0] for x in arrived[begun:]) == here * rows:
            make_part(len(queries), arrived[begun:], crossed[begun:])
            begun = len(arrived)

    own_kv = wk.shape[1] // head
    sets = [own_kv // 2, own_kv - own_kv // 2] if own_kv > 1 else [own_kv]
    attended, pages, first = [], [], 0
    for count in sets:
        made, cut = make_attention(
            lay, most, table, queries, gathered, per_kv, head, pages_each, first, count
        )
        attended.append(made.reshape(spans * rows, -1))
        pages.append(cut)
        first += count

    if paired:
        tile = 512 if cols % 512 == 0 else cols
        tiles = cols // tile
        widths = [2, 2, 1] if tiles == 5 else [tiles]
        others = [cross(pages[0])]
        project = functools.partial(make_projection, lay, table, attended, wo, tile)
        send = project(lambda r: (1 - r) * tiles, widths[:1], "send_part", (others[0],))
        if widths[1:]:
            send += project(
                lambda r: (1 - r) * tiles + widths[0], widths[1:], "send_part", (send[0],)
            )
        own = project(lambda r: r * tiles, widths, "own_part", (send[-1],))
        whole, received, landed, first = (), [], [], 0
        for n, sent in enumerate(send):
            if n:
                sent = after(sent, (received[-1], own, landed[-2:-1]))
            received.append(cross(sent))
            moved = make_sum(
                lay, table, arrived, own[n].reshape(spans, rows, -1),
                received[-1].reshape(spans, rows, -1), first,
            )
            same = [
                shift(x, owners, hop, 0) if hop else x
                for hop, x in zip(hop_order(chips), moved)
            ]
            landed.append(same)
            swapped = shift(jnp.concatenate([x[1:] for x in same]), owners, 0, 1)
            whole = (make_placed(lay, table, same, swapped, first, cols, whole),)
            first += sent.shape[1]
        mixed = whole[0].reshape(1, span_len, cols)
        for cut in pages[1:]:
            others.append(cross(after(cut, received[-1])))
        low = [jnp.where(tensor_rank == 0, a, b) for a, b in zip(pages, others)]
        high = [jnp.where(tensor_rank == 0, b, a) for a, b in zip(pages, others)]
        cache = jnp.concatenate(low + high, axis=3)
    else:
        pages = jnp.concatenate(pages, axis=3)
        attended = jnp.concatenate(attended, axis=1)
        if kv_cols < head:
            pages = lax.dynamic_slice_in_dim(
                pages, lax.rem(tensor_rank, head // kv_cols) * kv_cols, kv_cols, 3
            )
        cache = lax.all_gather(pages, "tensor", axis=3, tiled=True)
        partial = jnp.dot(attended, wo, preferred_element_type=jnp.float32)
        summed = lax.psum_scatter(
            partial.astype(jnp.bfloat16), "tensor", scatter_dimension=1, tiled=True
        )
        summed = summed.reshape(spans, rows, cols).astype(jnp.float32)
        x = jnp.concatenate(arrived).reshape(spans, rows, cols).astype(jnp.float32)
        moved = (x + summed).astype(jnp.bfloat16)
        targets = table[lay.target_at : lay.target_at + spans]
        moved = jnp.zeros_like(moved).at[targets].set(moved, unique_indices=True)
        moved = lax.all_to_all(moved, "group", split_axis=0, concat_axis=0, tiled=True)
        mixed = moved.reshape(1, span_len, cols)
    return (mixed, cache)


def solution(mesh):
    in_specs = (
        P(("replica", "group"), None, "tensor"),
        P("tensor"),
        P(None, "tensor"),
        P(None, "tensor"),
        P(None, "tensor"),
        P(),
        P(),
        P("tensor", None),
        P("replica"),
        P("replica"),
        P("replica"),
        P("replica"),
    )
    out_specs = (P(("replica", "group"), None, "tensor"), P(("replica", "group"), None, None, None))
    return jax.shard_map(local, mesh=mesh, in_specs=in_specs, out_specs=out_specs, check_vma=False)
```

```python
import functools
import math

import jax
import jax.numpy as jnp
from jax import lax
from jax.experimental import pallas as pl
from jax.experimental.pallas import tpu as pltpu
from jax.sharding import PartitionSpec as P

PAGE_ROWS = 128
epsilon = 1e-06
rope_base = 1000000.0
very_negative = -1e30
VMEM_BYTES = 48 * 1024 * 1024
PARTS = 2
CORES = 2
SHARE = 0.1


def params():
    return pltpu.CompilerParams(vmem_limit_bytes=VMEM_BYTES)


def cost(flops, moved, transcendentals=0):
    return pl.CostEstimate(
        flops=int(flops * SHARE),
        bytes_accessed=int(moved * SHARE),
        transcendentals=int(transcendentals * SHARE),
    )


def hop_order(chips):
    return [0, 1, chips - 1] + list(range(2, chips - 1)) if chips > 2 else list(range(chips))


class Layout:
    def __init__(self, spans, pages, owners):
        self.chips = owners // CORES
        self.span_at = 0
        self.earlier_at = self.span_at + spans
        self.target_at = self.earlier_at + spans
        self.sent_as = self.target_at + spans
        self.page = self.sent_as + spans
        self.origin = self.page + pages
        self.group_rank = self.origin + owners * spans
        self.tensor_rank = self.group_rank + 1
        self.length = self.tensor_rank + 1


def tables_kernel(lay, spans, pages, ranks, prompt_spans, source, target, page_slot, out, span_of, start_of):
    chips = lay.chips
    group_rank = ranks[0]
    out[lay.group_rank] = group_rank
    out[lay.tensor_rank] = ranks[1]
    for k in range(spans):
        start = jnp.int32(0)
        begin = jnp.int32(0)
        for p in range(prompt_spans.shape[0]):
            start = jnp.where(begin <= k, begin, start)
            begin = begin + prompt_spans[p]
        start_of[k] = start
        span_of[source[k]] = jnp.int32(k)
    for p in range(pages):
        out[lay.page + page_slot[p]] = jnp.int32(p)
    chip, core = lax.div(group_rank, CORES), lax.rem(group_rank, CORES)
    hops = hop_order(chips)
    for back in range(chips):
        for other in range(CORES):
            at_chip = lax.rem(chip + chips - back, chips)
            at_core = jnp.where(other == 0, core, 1 - core)
            for n, hop in enumerate(hops):
                for flip in range(CORES):
                    from_chip = lax.rem(at_chip + chips - hop, chips)
                    from_core = jnp.where(flip == 0, at_core, 1 - at_core)
                    k = span_of[from_chip * CORES + from_core]
                    place = n * CORES + flip
                    out[lay.origin + (back * CORES + other) * spans + place] = k
                    if back == 0 and other == 0:
                        out[lay.span_at + place] = k
                        out[lay.earlier_at + place] = k - start_of[k]
                        owner = target[k]
                        ahead = lax.rem(lax.div(owner, CORES) + chips - chip, chips)
                        turn = jnp.int32(0)
                        for m, other_hop in enumerate(hops):
                            turn = jnp.where(ahead == other_hop, jnp.int32(m), turn)
                        crossing = jnp.where(lax.rem(owner, CORES) == core, 0, 1)
                        out[lay.target_at + place] = owner
                        out[lay.sent_as + place] = turn * CORES + crossing


def make_tables(lay, spans, pages, ranks, prompt_spans, source, target, page_slot):
    smem = pl.BlockSpec(memory_space=pltpu.SMEM)
    return pl.pallas_call(
        functools.partial(tables_kernel, lay, spans, pages),
        out_shape=jax.ShapeDtypeStruct((lay.length,), jnp.int32),
        in_specs=[smem] * 5,
        out_specs=smem,
        scratch_shapes=[pltpu.SMEM((spans,), jnp.int32)] * 2,
        name="tables",
    )(ranks, prompt_spans, source, target, page_slot)


def head_norm_rope(u, gain, cosine, sine):
    mean_sq = jnp.mean(u * u, axis=-1, keepdims=True)
    u = u * lax.rsqrt(mean_sq + epsilon) * gain
    half = u.shape[-1] // 2
    return u * cosine + pltpu.roll(u, half, 1) * sine


def half_index(lay, sides, side):
    if sides == 1:
        return lambda t: 0
    if side == 0:
        return lambda t: t[lay.tensor_rank]
    return lambda t: 1 - t[lay.tensor_rank]


def summed_dot(lefts, rights):
    total = None
    for left, right in zip(lefts, rights):
        term = jnp.dot(left[...], right[...], preferred_element_type=jnp.float32)
        total = term if total is None else total + term
    return total


def kv_kernel(sides, blocks, table, *refs):
    refs = list(refs)
    take = lambda n: [refs.pop(0) for _ in range(n)]
    xs = [take(blocks) for _ in range(sides)]
    gains, wks, wvs = take(sides), take(sides), take(sides)
    kgain, cosine, sine = take(3)
    normed, (kv,) = take(sides), take(1)
    head = kgain.shape[1]
    width = sum(x[0].shape[1] for x in xs)

    @pl.when(pl.program_id(0) == 0)
    def _():
        at = 0
        for b in range(blocks):
            wide = [x[b][...].astype(jnp.float32) for x in xs]
            total = sum(jnp.sum(w * w, axis=-1, keepdims=True) for w in wide)
            factor = lax.rsqrt(total / width + epsilon)
            rows = xs[0][b].shape[0]
            for w, gain, to in zip(wide, gains, normed):
                to[at : at + rows] = (w * factor * gain[...].astype(jnp.float32)).astype(
                    jnp.bfloat16
                )
            at += rows

    keys = summed_dot(normed, wks).astype(jnp.bfloat16)
    gains = kgain[...].astype(jnp.float32)
    for h in range(keys.shape[1] // head):
        u = keys[:, h * head : (h + 1) * head].astype(jnp.float32)
        kv[0, :, h * head : (h + 1) * head] = head_norm_rope(
            u, gains, cosine[...], sine[...]
        ).astype(jnp.bfloat16)
    kv[1] = summed_dot(normed, wvs).astype(jnp.bfloat16)


def make_kv(lay, table, xs, gains, wk, wv, kgain, cosine, sine, part):
    sides, blocks = len(xs), len(xs[0])
    rows = sum(x.shape[0] for x in xs[0])
    widths = [x[0].shape[1] for x in xs]
    width, cols = wk.shape
    tile = 256 if cols % 256 == 0 else cols
    head = kgain.shape[1]
    fixed = lambda n, t: (0, 0)
    here = lambda n, t: (part, 0)
    weights = []
    for side in range(sides):
        index = half_index(lay, sides, side)
        weights.append(
            pl.BlockSpec((widths[side], tile), lambda n, t, index=index: (index(t), n))
        )
    return pl.pallas_call(
        functools.partial(kv_kernel, sides, blocks),
        grid_spec=pltpu.PrefetchScalarGridSpec(
            num_scalar_prefetch=1,
            grid=(cols // tile,),
            in_specs=[pl.BlockSpec(x.shape, fixed) for side in xs for x in side]
            + [pl.BlockSpec((1, w), fixed) for w in widths]
            + weights
            + weights
            + [
                pl.BlockSpec((1, head), fixed),
                pl.BlockSpec((rows, head), here),
                pl.BlockSpec((rows, head), here),
            ],
            out_specs=[pl.BlockSpec((rows, w), fixed) for w in widths]
            + [pl.BlockSpec((2, rows, tile), lambda n, t: (0, 0, n))],
        ),
        out_shape=[jax.ShapeDtypeStruct((rows, w), jnp.bfloat16) for w in widths]
        + [jax.ShapeDtypeStruct((2, rows, cols), jnp.bfloat16)],
        compiler_params=params(),
        cost_estimate=cost(4 * rows * width * cols, 4 * width * cols + 4 * rows * width),
        name="keys_values",
    )(
        table, *[x for side in xs for x in side], *gains, *[wk] * sides, *[wv] * sides,
        kgain, cosine, sine,
    )


def q_kernel(sides, table, *refs):
    normed, wqs = refs[:sides], refs[sides : 2 * sides]
    qgain, cosine, sine, out = refs[2 * sides :]
    head = qgain.shape[1]
    lin = summed_dot(normed, wqs)
    gains = qgain[...].astype(jnp.float32)
    for h in range(lin.shape[1] // head):
        out[:, h * head : (h + 1) * head] = head_norm_rope(
            lin[:, h * head : (h + 1) * head], gains, cosine[...], sine[...]
        ).astype(jnp.bfloat16)


def make_q(lay, table, normed, wq, qgain, cosine, sine, part):
    sides = len(normed)
    rows = normed[0].shape[0]
    width, cols = wq.shape
    tile = 512 if cols % 512 == 0 else cols
    head = qgain.shape[1]
    fixed = lambda n, t: (0, 0)
    here = lambda n, t: (part, 0)
    weights = []
    for side in range(sides):
        index = half_index(lay, sides, side)
        weights.append(
            pl.BlockSpec(
                (normed[side].shape[1], tile), lambda n, t, index=index: (index(t), n)
            )
        )
    return pl.pallas_call(
        functools.partial(q_kernel, sides),
        grid_spec=pltpu.PrefetchScalarGridSpec(
            num_scalar_prefetch=1,
            grid=(cols // tile,),
            in_specs=[pl.BlockSpec(x.shape, fixed) for x in normed]
            + weights
            + [
                pl.BlockSpec((1, head), fixed),
                pl.BlockSpec((rows, head), here),
                pl.BlockSpec((rows, head), here),
            ],
            out_specs=pl.BlockSpec((rows, tile), lambda n, t: (0, n)),
        ),
        out_shape=jax.ShapeDtypeStruct((rows, cols), jnp.bfloat16),
        compiler_params=params(),
        cost_estimate=cost(2 * rows * width * cols, 2 * width * cols + 2 * rows * (width + cols)),
        name="queries",
    )(table, *normed, *[wq] * sides, qgain, cosine, sine)


def attention_kernel(lay, spans, most, per_kv, head, owners, pages_each, table, *refs):
    q_refs = refs[:PARTS]
    kv_refs = refs[PARTS : PARTS + owners * PARTS]
    out, pages, keys, values = refs[PARTS + owners * PARTS :]
    chips = lay.chips
    here, rows = kv_refs[0].shape[1], kv_refs[0].shape[2]
    group_rank = table[lay.group_rank]
    chip, core = lax.div(group_rank, CORES), lax.rem(group_rank, CORES)
    for o in range(owners):
        back, other = o // CORES, o % CORES
        owner = lax.rem(chip + chips - back, chips) * CORES + (core if other == 0 else 1 - core)
        at = pl.ds(pl.multiple_of(owner * rows, rows), rows)
        for p in range(PARTS):
            for i in range(here):
                k = table[lay.origin + o * spans + p * here + i]
                keys[k, at] = kv_refs[o * PARTS + p][0, i]
                values[k, at] = kv_refs[o * PARTS + p][1, i]

    for i in range(pages_each):
        page = table[lay.page + group_rank * pages_each + i]
        k = lax.div(page, pages_each)
        at = pl.ds(pl.multiple_of(lax.rem(page, pages_each) * PAGE_ROWS, PAGE_ROWS), PAGE_ROWS)
        pages[i, 0] = keys[k, at]
        pages[i, 1] = values[k, at]

    scale = (1.0 / math.sqrt(head)) * math.log2(math.e)
    q_rows, k_rows = per_kv * rows, owners * rows
    row = lax.broadcasted_iota(jnp.int32, (q_rows, k_rows), 0)
    col = lax.broadcasted_iota(jnp.int32, (q_rows, k_rows), 1)
    allowed = col <= group_rank * rows + row % rows

    def one_place(p, i, carry):
        k = table[lay.span_at + p * here + i]
        earlier = table[lay.earlier_at + p * here + i]
        queries = jnp.concatenate(
            [q_refs[p][i, :, g * head : (g + 1) * head] for g in range(per_kv)], axis=0
        )

        def with_earlier(count):
            scores = []
            for back in range(count + 1):
                s = lax.dot_general(
                    queries, keys[k - back], (((1,), (1,)), ((), ())),
                    preferred_element_type=jnp.float32,
                )
                if back == 0:
                    s = jnp.where(allowed, s, very_negative)
                scores.append(s)
            best = scores[0]
            for s in scores[1:]:
                best = jnp.maximum(best, s)
            best = jnp.max(best, axis=-1, keepdims=True)
            total = None
            summed = None
            for back, s in enumerate(scores):
                w = jnp.exp2((s - best) * scale)
                part = jnp.sum(w, axis=-1, keepdims=True)
                term = jnp.dot(
                    w.astype(jnp.bfloat16), values[k - back], preferred_element_type=jnp.float32
                )
                total = part if total is None else total + part
                summed = term if summed is None else summed + term
            result = (summed / total).astype(jnp.bfloat16)
            for g in range(per_kv):
                out[p * here + i, :, g * head : (g + 1) * head] = result[
                    g * rows : (g + 1) * rows
                ]

        for count in range(most):
            pl.when(earlier == count)(functools.partial(with_earlier, count))
        return carry

    for p in range(PARTS):
        lax.fori_loop(0, here, functools.partial(one_place, p), 0)


def make_attention(lay, most, table, queries, gathered, per_kv, head, pages_each, first, count):
    here, rows, cols = queries[0].shape
    spans = here * PARTS
    owners = len(gathered)
    q_spec = pl.BlockSpec((here, rows, per_kv * head), lambda h, t: (0, 0, first + h))
    kv_spec = pl.BlockSpec((2, here, rows, head), lambda h, t: (0, 0, 0, first + h))
    flat = [x for origin in gathered for x in origin]
    all_rows = spans * rows
    pairs = 2.2 * all_rows * owners * rows * per_kv * count
    return pl.pallas_call(
        functools.partial(
            attention_kernel, lay, spans, most, per_kv, head, owners, pages_each
        ),
        grid_spec=pltpu.PrefetchScalarGridSpec(
            num_scalar_prefetch=1,
            grid=(count,),
            in_specs=[q_spec] * PARTS + [kv_spec] * len(flat),
            out_specs=[
                pl.BlockSpec((spans, rows, per_kv * head), lambda h, t: (0, 0, h)),
                pl.BlockSpec((pages_each, 2, PAGE_ROWS, head), lambda h, t: (0, 0, 0, h)),
            ],
            scratch_shapes=[pltpu.VMEM((spans, owners * rows, head), jnp.bfloat16)] * 2,
        ),
        out_shape=[
            jax.ShapeDtypeStruct((spans, rows, count * per_kv * head), jnp.bfloat16),
            jax.ShapeDtypeStruct((pages_each, 2, PAGE_ROWS, count * head), jnp.bfloat16),
        ],
        compiler_params=params(),
        cost_estimate=cost(
            4 * pairs * head, 4 * all_rows * cols + 2 * len(flat) * flat[0].size, pairs
        ),
        name="attention",
    )(table, *queries, *flat)


def project_kernel(pieces, follows, tile, table, *refs):
    attended, wo, outs = refs[:pieces], refs[pieces], refs[pieces + 1 + follows :]
    total, at = None, 0
    for piece in attended:
        depth = piece.shape[1]
        term = jnp.dot(piece[...], wo[at : at + depth], preferred_element_type=jnp.float32)
        total = term if total is None else total + term
        at += depth
    total = total.astype(jnp.bfloat16)
    step = 0
    for out in outs:
        for at in range(0, out.shape[1], tile):

            @pl.when(pl.program_id(0) == step)
            def _(out=out, at=at):
                out[:, at : at + tile] = total

            step += 1


def make_projection(lay, table, attended, wo, tile, first, widths, name, follows=()):
    rows = attended[0].shape[0]
    depth = wo.shape[0]
    count = sum(widths)
    return pl.pallas_call(
        functools.partial(project_kernel, len(attended), len(follows), tile),
        grid_spec=pltpu.PrefetchScalarGridSpec(
            num_scalar_prefetch=1,
            grid=(count,),
            in_specs=[pl.BlockSpec(x.shape, lambda n, t: (0, 0)) for x in attended]
            + [pl.BlockSpec((depth, tile), lambda n, t: (0, first(t[lay.tensor_rank]) + n))]
            + [pl.BlockSpec(memory_space=pl.ANY)] * len(follows),
            out_specs=[pl.BlockSpec((rows, w * tile), lambda n, t: (0, 0)) for w in widths],
        ),
        out_shape=[jax.ShapeDtypeStruct((rows, w * tile), jnp.bfloat16) for w in widths],
        compiler_params=params(),
        cost_estimate=cost(
            2 * rows * depth * count * tile, 2 * (rows * depth + (rows + depth) * count * tile)
        ),
        name=name,
    )(table, *attended, wo, *follows)


def add_kernel(lay, blocks, table, *refs):
    x_refs, own, received = refs[:blocks], refs[blocks], refs[blocks + 1]
    outs, moved = refs[blocks + 2 : -1], refs[-1]
    rows = moved.shape[1]
    place = 0
    for x in x_refs:
        for at in range(0, x.shape[0], rows):
            summed = own[place].astype(jnp.float32) + received[place].astype(jnp.float32)
            moved[table[lay.sent_as + place]] = (
                x[at : at + rows].astype(jnp.float32) + summed
            ).astype(jnp.bfloat16)
            place += 1
    for n, out in enumerate(outs):
        for flip in range(CORES):
            out[flip] = moved[n * CORES + flip]


def make_sum(lay, table, arrived, own, received, first):
    spans, rows, cols = received.shape
    chunk = first // cols
    whole = lambda n, t: (0, 0, 0)
    return pl.pallas_call(
        functools.partial(add_kernel, lay, len(arrived)),
        grid_spec=pltpu.PrefetchScalarGridSpec(
            num_scalar_prefetch=1,
            grid=(1,),
            in_specs=[pl.BlockSpec((x.shape[0], cols), lambda n, t: (0, chunk)) for x in arrived]
            + [pl.BlockSpec((spans, rows, cols), whole)] * 2,
            out_specs=[pl.BlockSpec((CORES, rows, cols), whole)] * lay.chips,
            scratch_shapes=[pltpu.VMEM((spans, rows, cols), jnp.bfloat16)],
        ),
        out_shape=[jax.ShapeDtypeStruct((CORES, rows, cols), jnp.bfloat16)] * lay.chips,
        compiler_params=params(),
        cost_estimate=cost(3 * spans * rows * cols, 8 * spans * rows * cols),
        name="residual",
    )(table, *arrived, own, received)


def place_kernel(lay, table, *refs):
    same, swapped, out = refs[: lay.chips], refs[lay.chips], refs[-1]
    rows = swapped.shape[1]
    group_rank = table[lay.group_rank]
    chip, core = lax.div(group_rank, CORES), lax.rem(group_rank, CORES)
    for n, hop in enumerate(hop_order(lay.chips)):
        owner = lax.rem(chip + lay.chips - hop, lay.chips) * CORES
        for block, at_core in ((same[n][0], core), (swapped[n], 1 - core)):
            at = pl.multiple_of((owner + at_core) * rows, rows)
            out[pl.ds(at, rows)] = block


def make_placed(lay, table, same, swapped, first, cols, whole):
    chips, rows, tile = swapped.shape
    chunk = first // tile
    return pl.pallas_call(
        functools.partial(place_kernel, lay),
        grid_spec=pltpu.PrefetchScalarGridSpec(
            num_scalar_prefetch=1,
            grid=(1,),
            in_specs=[pl.BlockSpec((CORES, rows, tile), lambda n, t: (0, 0, 0))] * chips
            + [pl.BlockSpec((chips, rows, tile), lambda n, t: (0, 0, 0))]
            + [pl.BlockSpec(memory_space=pl.ANY)] * len(whole),
            out_specs=pl.BlockSpec((chips * CORES * rows, tile), lambda n, t: (0, chunk)),
        ),
        out_shape=jax.ShapeDtypeStruct((chips * CORES * rows, cols), jnp.bfloat16),
        input_output_aliases={chips + 2: 0} if whole else {},
        compiler_params=params(),
        cost_estimate=cost(0, 4 * chips * CORES * rows * tile),
        name="placed",
    )(table, *same, swapped, *whole)


def rope_tables(earlier, span_len, first_row, rows, head):
    half = head // 2
    freqs = jnp.power(
        jnp.float32(rope_base), -jnp.arange(half, dtype=jnp.float32) * 2.0 / head
    )
    at = earlier[:, None] * span_len + first_row + jnp.arange(rows, dtype=jnp.int32)[None, :]
    angles = at.reshape(-1).astype(jnp.float32)[:, None] * freqs[None, :]
    cosine, sine = jnp.cos(angles), jnp.sin(angles)
    return (
        jnp.concatenate([cosine, cosine], axis=1),
        jnp.concatenate([-sine, sine], axis=1),
    )


def after(x, done):
    return lax.optimization_barrier((x, done))[0]


def shift(x, owners, hop, flip):
    chips = owners // CORES
    pairs = [
        (z * CORES + c, (z + hop) % chips * CORES + (c ^ flip))
        for z in range(chips)
        for c in range(CORES)
    ]
    return lax.ppermute(x, "group", pairs)


def local(
    hidden_in, ln_gain, wq, wk, wv, q_gain, key_norm_gain, wo,
    prompt_spans, span_source, span_target, page_slot,
):
    _, span_len, cols = hidden_in.shape
    tensor_size = lax.axis_size("tensor")
    owners = lax.axis_size("group")
    tensor_rank = lax.axis_index("tensor")
    group_rank = lax.axis_index("group")
    chips = owners // CORES
    head = q_gain.shape[0]
    rows = span_len // owners
    pages_each = span_len // PAGE_ROWS
    spans = span_source.shape[0]
    here = spans // PARTS
    most = min(spans - (prompt_spans.shape[0] - 1), spans // 2)
    kv_cols = wk.shape[1]
    paired = tensor_size == 2
    swap = [(0, 1), (1, 0)]
    lay = Layout(spans, spans * pages_each, owners)

    if kv_cols < head:
        share = head // kv_cols
        sets = [list(range(i, i + share)) for i in range(0, tensor_size, share)]
        wk, wv = [
            lax.all_gather(w, "tensor", axis=1, tiled=True, axis_index_groups=sets)
            for w in (wk, wv)
        ]
    per_kv = wq.shape[1] // max(head, wk.shape[1])

    chip, core = group_rank // CORES, group_rank % CORES
    split = hidden_in.reshape(owners, rows, cols)

    def rows_for(hop, flip):
        to = lax.rem(chip + hop, chips) * CORES + lax.rem(core + flip, CORES)
        return lax.dynamic_index_in_dim(split, to, 0, keepdims=False)

    hops = hop_order(chips)
    paired_hops = hops[2:]
    near = [shift(rows_for(hop, flip), owners, hop, flip) for hop in hops[1:2] for flip in range(CORES)]
    swapped = shift(
        jnp.stack([rows_for(hop, 1) for hop in hops[:1] + paired_hops]), owners, 0, 1
    )
    arrived = [rows_for(0, 0), swapped[0]] + near
    moves = []
    for n, hop in enumerate(paired_hops):
        pair = [rows_for(hop, 0), swapped[1 + n]]
        if n < len(paired_hops) - 1:
            moves.append((hop, jnp.concatenate(pair)))
        else:
            moves += [(hop, block) for block in pair]

    ranks = jnp.stack([group_rank, tensor_rank]).astype(jnp.int32)
    table = make_tables(
        lay, spans, spans * pages_each, ranks, prompt_spans, span_source, span_target, page_slot
    )
    earlier = table[lay.earlier_at : lay.earlier_at + spans]
    cosine, sine = rope_tables(earlier, span_len, group_rank * rows, rows, head)

    cross = lambda x: lax.ppermute(x, "tensor", swap)
    crossed = [cross(x) for x in arrived] if paired else []
    if paired:
        gain = ln_gain[None]
        gains = [gain, cross(after(gain, crossed[1]))]
    else:
        gains = [lax.all_gather(ln_gain, "tensor", axis=0, tiled=True)[None]]
    for n, (hop, block) in enumerate(moves):
        if paired:
            landed = arrived[-1:] if n else near
            block = after(block, (landed, crossed[2 * n : 2 * n + 2] if n < 2 else crossed[n + 2]))
        arrived.append(shift(block, owners, hop, 0))
        if paired:
            crossed.append(cross(arrived[-1]))

    kgain = after(key_norm_gain[None], arrived[-1])
    kvs, norms, begun = [], [], 0
    for n in range(1, len(arrived) + 1):
        if sum(x.shape[0] for x in arrived[begun:n]) == here * rows:
            if paired:
                xs = [arrived[begun:n], crossed[begun:n]]
            else:
                whole = jnp.concatenate(arrived[begun:n])
                xs = [[lax.all_gather(whole, "tensor", axis=1, tiled=True)]]
            *normed, kv = make_kv(
                lay, table, xs, gains, wk, wv, kgain, cosine, sine, len(kvs)
            )
            kvs.append(kv.reshape(2, here, rows, kv.shape[2]))
            norms.append(normed)
            begun = n

    queries, gathered = [], [[] for _ in range(owners)]
    ready = kvs[-1]
    for back in range(chips):
        for p in range(PARTS):
            if back:
                if back == min(2, chips - 1):
                    kvs[p] = after(kvs[p], queries[p])
                kvs[p] = shift(kvs[p], owners, 1, 0)
            gathered[back * CORES].append(kvs[p])
            gathered[back * CORES + 1].append(shift(kvs[p], owners, 0, 1))
            if back == min(1, chips - 1):
                made = make_q(
                    lay, table, norms[p], wq, after(q_gain[None], ready), cosine, sine, p
                )
                queries.append(made.reshape(here, rows, made.shape[1]))
                ready = kvs[p]

    own_kv = wk.shape[1] // head
    sets = [own_kv // 2, own_kv - own_kv // 2] if own_kv > 1 else [own_kv]
    attended, pages, first = [], [], 0
    for count in sets:
        made, cut = make_attention(
            lay, most, table, queries, gathered, per_kv, head, pages_each, first, count
        )
        attended.append(made.reshape(spans * rows, -1))
        pages.append(cut)
        first += count

    if paired:
        tile = 512 if cols % 512 == 0 else cols
        tiles = cols // tile
        widths = [2, 2, 1] if tiles == 5 else [tiles]
        others = [cross(pages[0])]
        project = functools.partial(make_projection, lay, table, attended, wo, tile)
        send = project(lambda r: (1 - r) * tiles, widths[:1], "send_part", (others[0],))
        if widths[1:]:
            send += project(
                lambda r: (1 - r) * tiles + widths[0], widths[1:], "send_part", (send[0],)
            )
        own = project(lambda r: r * tiles, widths, "own_part", (send[-1],))
        whole, received, landed, first = (), [], [], 0
        for n, sent in enumerate(send):
            if n:
                sent = after(sent, (received[-1], own, landed[-2:-1]))
            received.append(cross(sent))
            moved = make_sum(
                lay, table, arrived, own[n].reshape(spans, rows, -1),
                received[-1].reshape(spans, rows, -1), first,
            )
            same = [
                shift(x, owners, hop, 0) if hop else x
                for hop, x in zip(hop_order(chips), moved)
            ]
            landed.append(same)
            swapped = shift(jnp.concatenate([x[1:] for x in same]), owners, 0, 1)
            whole = (make_placed(lay, table, same, swapped, first, cols, whole),)
            first += sent.shape[1]
        mixed = whole[0].reshape(1, span_len, cols)
        for cut in pages[1:]:
            others.append(cross(after(cut, received[-1])))
        low = [jnp.where(tensor_rank == 0, a, b) for a, b in zip(pages, others)]
        high = [jnp.where(tensor_rank == 0, b, a) for a, b in zip(pages, others)]
        cache = jnp.concatenate(low + high, axis=3)
    else:
        pages = jnp.concatenate(pages, axis=3)
        attended = jnp.concatenate(attended, axis=1)
        if kv_cols < head:
            pages = lax.dynamic_slice_in_dim(
                pages, lax.rem(tensor_rank, head // kv_cols) * kv_cols, kv_cols, 3
            )
        cache = lax.all_gather(pages, "tensor", axis=3, tiled=True)
        partial = jnp.dot(attended, wo, preferred_element_type=jnp.float32)
        summed = lax.psum_scatter(
            partial.astype(jnp.bfloat16), "tensor", scatter_dimension=1, tiled=True
        )
        summed = summed.reshape(spans, rows, cols).astype(jnp.float32)
        x = jnp.concatenate(arrived).reshape(spans, rows, cols).astype(jnp.float32)
        moved = (x + summed).astype(jnp.bfloat16)
        targets = table[lay.target_at : lay.target_at + spans]
        moved = jnp.zeros_like(moved).at[targets].set(moved, unique_indices=True)
        moved = lax.all_to_all(moved, "group", split_axis=0, concat_axis=0, tiled=True)
        mixed = moved.reshape(1, span_len, cols)
    return (mixed, cache)


def solution(mesh):
    in_specs = (
        P(("replica", "group"), None, "tensor"),
        P("tensor"),
        P(None, "tensor"),
        P(None, "tensor"),
        P(None, "tensor"),
        P(),
        P(),
        P("tensor", None),
        P("replica"),
        P("replica"),
        P("replica"),
        P("replica"),
    )
    out_specs = (P(("replica", "group"), None, "tensor"), P(("replica", "group"), None, None, None))
    return jax.shard_map(local, mesh=mesh, in_specs=in_specs, out_specs=out_specs, check_vma=False)
```

```python
import functools
import math

import jax
import jax.numpy as jnp
from jax import lax
from jax.experimental import pallas as pl
from jax.experimental.pallas import tpu as pltpu
from jax.sharding import PartitionSpec as P

PAGE_ROWS = 128
epsilon = 1e-06
rope_base = 1000000.0
very_negative = -1e30
PARTS = 2
CORES = 2
SHARE = 0.1


def params(mebibytes):
    return pltpu.CompilerParams(vmem_limit_bytes=mebibytes * 1024 * 1024)


def cost(flops, moved, transcendentals=0):
    return pl.CostEstimate(
        flops=int(flops * SHARE),
        bytes_accessed=int(moved * SHARE),
        transcendentals=int(transcendentals * SHARE),
    )


def hop_order(chips):
    return [0, 1, chips - 1] + list(range(2, chips - 1)) if chips > 2 else list(range(chips))


class Layout:
    def __init__(self, spans, pages, owners):
        self.chips = owners // CORES
        self.span_at = 0
        self.earlier_at = self.span_at + spans
        self.target_at = self.earlier_at + spans
        self.sent_as = self.target_at + spans
        self.page = self.sent_as + spans
        self.origin = self.page + pages
        self.group_rank = self.origin + owners * spans
        self.tensor_rank = self.group_rank + 1
        self.length = self.tensor_rank + 1


def tables_kernel(lay, spans, pages, ranks, prompt_spans, source, target, page_slot, out, span_of, start_of):
    chips = lay.chips
    group_rank = ranks[0]
    out[lay.group_rank] = group_rank
    out[lay.tensor_rank] = ranks[1]
    for k in range(spans):
        start = jnp.int32(0)
        begin = jnp.int32(0)
        for p in range(prompt_spans.shape[0]):
            start = jnp.where(begin <= k, begin, start)
            begin = begin + prompt_spans[p]
        start_of[k] = start
        span_of[source[k]] = jnp.int32(k)
    for p in range(pages):
        out[lay.page + page_slot[p]] = jnp.int32(p)
    chip, core = lax.div(group_rank, CORES), lax.rem(group_rank, CORES)
    hops = hop_order(chips)
    for back in range(chips):
        for other in range(CORES):
            at_chip = lax.rem(chip + chips - back, chips)
            at_core = jnp.where(other == 0, core, 1 - core)
            for n, hop in enumerate(hops):
                for flip in range(CORES):
                    from_chip = lax.rem(at_chip + chips - hop, chips)
                    from_core = jnp.where(flip == 0, at_core, 1 - at_core)
                    k = span_of[from_chip * CORES + from_core]
                    place = n * CORES + flip
                    out[lay.origin + (back * CORES + other) * spans + place] = k
                    if back == 0 and other == 0:
                        out[lay.span_at + place] = k
                        out[lay.earlier_at + place] = k - start_of[k]
                        owner = target[k]
                        ahead = lax.rem(lax.div(owner, CORES) + chips - chip, chips)
                        turn = jnp.int32(0)
                        for m, other_hop in enumerate(hops):
                            turn = jnp.where(ahead == other_hop, jnp.int32(m), turn)
                        crossing = jnp.where(lax.rem(owner, CORES) == core, 0, 1)
                        out[lay.target_at + place] = owner
                        out[lay.sent_as + place] = turn * CORES + crossing


def make_tables(lay, spans, pages, ranks, prompt_spans, source, target, page_slot):
    smem = pl.BlockSpec(memory_space=pltpu.SMEM)
    return pl.pallas_call(
        functools.partial(tables_kernel, lay, spans, pages),
        out_shape=jax.ShapeDtypeStruct((lay.length,), jnp.int32),
        in_specs=[smem] * 5,
        out_specs=smem,
        scratch_shapes=[pltpu.SMEM((spans,), jnp.int32)] * 2,
        name="tables",
    )(ranks, prompt_spans, source, target, page_slot)


def head_norm_rope(u, gain, cosine, sine):
    mean_sq = jnp.mean(u * u, axis=-1, keepdims=True)
    u = u * lax.rsqrt(mean_sq + epsilon) * gain
    half = u.shape[-1] // 2
    return u * cosine + pltpu.roll(u, half, 1) * sine


def half_index(lay, sides, side):
    if sides == 1:
        return lambda t: 0
    if side == 0:
        return lambda t: t[lay.tensor_rank]
    return lambda t: 1 - t[lay.tensor_rank]


def summed_dot(lefts, rights):
    total = None
    for left, right in zip(lefts, rights):
        term = jnp.dot(left[...], right[...], preferred_element_type=jnp.float32)
        total = term if total is None else total + term
    return total


def kv_kernel(sides, blocks, table, *refs):
    refs = list(refs)
    take = lambda n: [refs.pop(0) for _ in range(n)]
    xs = [take(blocks) for _ in range(sides)]
    gains, wks, wvs = take(sides), take(sides), take(sides)
    kgain, cosine, sine = take(3)
    normed, (kv,) = take(sides), take(1)
    head = kgain.shape[1]
    width = sum(x[0].shape[1] for x in xs)

    @pl.when(pl.program_id(0) == 0)
    def _():
        at = 0
        for b in range(blocks):
            wide = [x[b][...].astype(jnp.float32) for x in xs]
            total = sum(jnp.sum(w * w, axis=-1, keepdims=True) for w in wide)
            factor = lax.rsqrt(total / width + epsilon)
            rows = xs[0][b].shape[0]
            for w, gain, to in zip(wide, gains, normed):
                to[at : at + rows] = (w * factor * gain[...].astype(jnp.float32)).astype(
                    jnp.bfloat16
                )
            at += rows

    keys = summed_dot(normed, wks).astype(jnp.bfloat16)
    gains = kgain[...].astype(jnp.float32)
    for h in range(keys.shape[1] // head):
        u = keys[:, h * head : (h + 1) * head].astype(jnp.float32)
        kv[0, :, h * head : (h + 1) * head] = head_norm_rope(
            u, gains, cosine[...], sine[...]
        ).astype(jnp.bfloat16)
    kv[1] = summed_dot(normed, wvs).astype(jnp.bfloat16)


def make_kv(lay, table, xs, gains, wk, wv, kgain, cosine, sine, part):
    sides, blocks = len(xs), len(xs[0])
    rows = sum(x.shape[0] for x in xs[0])
    widths = [x[0].shape[1] for x in xs]
    width, cols = wk.shape
    tile = 256 if cols % 256 == 0 else cols
    head = kgain.shape[1]
    fixed = lambda n, t: (0, 0)
    here = lambda n, t: (part, 0)
    weights = []
    for side in range(sides):
        index = half_index(lay, sides, side)
        weights.append(
            pl.BlockSpec((widths[side], tile), lambda n, t, index=index: (index(t), n))
        )
    return pl.pallas_call(
        functools.partial(kv_kernel, sides, blocks),
        grid_spec=pltpu.PrefetchScalarGridSpec(
            num_scalar_prefetch=1,
            grid=(cols // tile,),
            in_specs=[pl.BlockSpec(x.shape, fixed) for side in xs for x in side]
            + [pl.BlockSpec((1, w), fixed) for w in widths]
            + weights
            + weights
            + [
                pl.BlockSpec((1, head), fixed),
                pl.BlockSpec((rows, head), here),
                pl.BlockSpec((rows, head), here),
            ],
            out_specs=[pl.BlockSpec((rows, w), fixed) for w in widths]
            + [pl.BlockSpec((2, rows, tile), lambda n, t: (0, 0, n))],
        ),
        out_shape=[jax.ShapeDtypeStruct((rows, w), jnp.bfloat16) for w in widths]
        + [jax.ShapeDtypeStruct((2, rows, cols), jnp.bfloat16)],
        compiler_params=params(32),
        cost_estimate=cost(4 * rows * width * cols, 4 * width * cols + 4 * rows * width),
        name="keys_values",
    )(
        table, *[x for side in xs for x in side], *gains, *[wk] * sides, *[wv] * sides,
        kgain, cosine, sine,
    )


def q_kernel(sides, table, *refs):
    normed, wqs = refs[:sides], refs[sides : 2 * sides]
    qgain, cosine, sine, out = refs[2 * sides :]
    head = qgain.shape[1]
    lin = summed_dot(normed, wqs)
    gains = qgain[...].astype(jnp.float32)
    for h in range(lin.shape[1] // head):
        out[:, h * head : (h + 1) * head] = head_norm_rope(
            lin[:, h * head : (h + 1) * head], gains, cosine[...], sine[...]
        ).astype(jnp.bfloat16)


def make_q(lay, table, normed, wq, qgain, cosine, sine, part):
    sides = len(normed)
    rows = normed[0].shape[0]
    width, cols = wq.shape
    tile = 512 if cols % 512 == 0 else cols
    head = qgain.shape[1]
    fixed = lambda n, t: (0, 0)
    here = lambda n, t: (part, 0)
    weights = []
    for side in range(sides):
        index = half_index(lay, sides, side)
        weights.append(
            pl.BlockSpec(
                (normed[side].shape[1], tile), lambda n, t, index=index: (index(t), n)
            )
        )
    return pl.pallas_call(
        functools.partial(q_kernel, sides),
        grid_spec=pltpu.PrefetchScalarGridSpec(
            num_scalar_prefetch=1,
            grid=(cols // tile,),
            in_specs=[pl.BlockSpec(x.shape, fixed) for x in normed]
            + weights
            + [
                pl.BlockSpec((1, head), fixed),
                pl.BlockSpec((rows, head), here),
                pl.BlockSpec((rows, head), here),
            ],
            out_specs=pl.BlockSpec((rows, tile), lambda n, t: (0, n)),
        ),
        out_shape=jax.ShapeDtypeStruct((rows, cols), jnp.bfloat16),
        compiler_params=params(24),
        cost_estimate=cost(2 * rows * width * cols, 2 * width * cols + 2 * rows * (width + cols)),
        name="queries",
    )(table, *normed, *[wq] * sides, qgain, cosine, sine)


def attention_kernel(lay, spans, most, per_kv, head, owners, pages_each, table, *refs):
    q_refs = refs[:PARTS]
    kv_refs = refs[PARTS : PARTS + owners * PARTS]
    out, pages, keys, values = refs[PARTS + owners * PARTS :]
    chips = lay.chips
    here, rows = kv_refs[0].shape[1], kv_refs[0].shape[2]
    group_rank = table[lay.group_rank]
    chip, core = lax.div(group_rank, CORES), lax.rem(group_rank, CORES)
    for o in range(owners):
        back, other = o // CORES, o % CORES
        owner = lax.rem(chip + chips - back, chips) * CORES + (core if other == 0 else 1 - core)
        at = pl.ds(pl.multiple_of(owner * rows, rows), rows)
        for p in range(PARTS):
            for i in range(here):
                k = table[lay.origin + o * spans + p * here + i]
                keys[k, at] = kv_refs[o * PARTS + p][0, i]
                values[k, at] = kv_refs[o * PARTS + p][1, i]

    for i in range(pages_each):
        page = table[lay.page + group_rank * pages_each + i]
        k = lax.div(page, pages_each)
        at = pl.ds(pl.multiple_of(lax.rem(page, pages_each) * PAGE_ROWS, PAGE_ROWS), PAGE_ROWS)
        pages[i, 0] = keys[k, at]
        pages[i, 1] = values[k, at]

    scale = (1.0 / math.sqrt(head)) * math.log2(math.e)
    q_rows, k_rows = per_kv * rows, owners * rows
    row = lax.broadcasted_iota(jnp.int32, (q_rows, k_rows), 0)
    col = lax.broadcasted_iota(jnp.int32, (q_rows, k_rows), 1)
    allowed = col <= group_rank * rows + row % rows

    def one_place(p, i, carry):
        k = table[lay.span_at + p * here + i]
        earlier = table[lay.earlier_at + p * here + i]
        queries = jnp.concatenate(
            [q_refs[p][i, :, g * head : (g + 1) * head] for g in range(per_kv)], axis=0
        )

        def with_earlier(count):
            scores = []
            for back in range(count + 1):
                s = lax.dot_general(
                    queries, keys[k - back], (((1,), (1,)), ((), ())),
                    preferred_element_type=jnp.float32,
                )
                if back == 0:
                    s = jnp.where(allowed, s, very_negative)
                scores.append(s)
            best = scores[0]
            for s in scores[1:]:
                best = jnp.maximum(best, s)
            best = jnp.max(best, axis=-1, keepdims=True)
            total = None
            summed = None
            for back, s in enumerate(scores):
                w = jnp.exp2((s - best) * scale)
                part = jnp.sum(w, axis=-1, keepdims=True)
                term = jnp.dot(
                    w.astype(jnp.bfloat16), values[k - back], preferred_element_type=jnp.float32
                )
                total = part if total is None else total + part
                summed = term if summed is None else summed + term
            result = (summed / total).astype(jnp.bfloat16)
            for g in range(per_kv):
                out[p * here + i, :, g * head : (g + 1) * head] = result[
                    g * rows : (g + 1) * rows
                ]

        for count in range(most):
            pl.when(earlier == count)(functools.partial(with_earlier, count))
        return carry

    for p in range(PARTS):
        lax.fori_loop(0, here, functools.partial(one_place, p), 0)


def make_attention(lay, most, table, queries, gathered, per_kv, head, pages_each, first, count):
    here, rows, cols = queries[0].shape
    spans = here * PARTS
    owners = len(gathered)
    q_spec = pl.BlockSpec((here, rows, per_kv * head), lambda h, t: (0, 0, first + h))
    kv_spec = pl.BlockSpec((2, here, rows, head), lambda h, t: (0, 0, 0, first + h))
    flat = [x for origin in gathered for x in origin]
    all_rows = spans * rows
    pairs = 2.2 * all_rows * owners * rows * per_kv * count
    return pl.pallas_call(
        functools.partial(
            attention_kernel, lay, spans, most, per_kv, head, owners, pages_each
        ),
        grid_spec=pltpu.PrefetchScalarGridSpec(
            num_scalar_prefetch=1,
            grid=(count,),
            in_specs=[q_spec] * PARTS + [kv_spec] * len(flat),
            out_specs=[
                pl.BlockSpec((spans, rows, per_kv * head), lambda h, t: (0, 0, h)),
                pl.BlockSpec((pages_each, 2, PAGE_ROWS, head), lambda h, t: (0, 0, 0, h)),
            ],
            scratch_shapes=[pltpu.VMEM((spans, owners * rows, head), jnp.bfloat16)] * 2,
        ),
        out_shape=[
            jax.ShapeDtypeStruct((spans, rows, count * per_kv * head), jnp.bfloat16),
            jax.ShapeDtypeStruct((pages_each, 2, PAGE_ROWS, count * head), jnp.bfloat16),
        ],
        compiler_params=params(20),
        cost_estimate=cost(
            4 * pairs * head, 4 * all_rows * cols + 2 * len(flat) * flat[0].size, pairs
        ),
        name="attention",
    )(table, *queries, *flat)


def project_kernel(pieces, follows, tile, table, *refs):
    attended, wo, outs = refs[:pieces], refs[pieces], refs[pieces + 1 + follows :]
    total, at = None, 0
    for piece in attended:
        depth = piece.shape[1]
        term = jnp.dot(piece[...], wo[at : at + depth], preferred_element_type=jnp.float32)
        total = term if total is None else total + term
        at += depth
    total = total.astype(jnp.bfloat16)
    step = 0
    for out in outs:
        for at in range(0, out.shape[1], tile):

            @pl.when(pl.program_id(0) == step)
            def _(out=out, at=at):
                out[:, at : at + tile] = total

            step += 1


def make_projection(lay, table, attended, wo, tile, first, widths, name, follows=()):
    rows = attended[0].shape[0]
    depth = wo.shape[0]
    count = sum(widths)
    return pl.pallas_call(
        functools.partial(project_kernel, len(attended), len(follows), tile),
        grid_spec=pltpu.PrefetchScalarGridSpec(
            num_scalar_prefetch=1,
            grid=(count,),
            in_specs=[pl.BlockSpec(x.shape, lambda n, t: (0, 0)) for x in attended]
            + [pl.BlockSpec((depth, tile), lambda n, t: (0, first(t[lay.tensor_rank]) + n))]
            + [pl.BlockSpec(memory_space=pl.ANY)] * len(follows),
            out_specs=[pl.BlockSpec((rows, w * tile), lambda n, t: (0, 0)) for w in widths],
        ),
        out_shape=[jax.ShapeDtypeStruct((rows, w * tile), jnp.bfloat16) for w in widths],
        compiler_params=params(20),
        cost_estimate=cost(
            2 * rows * depth * count * tile, 2 * (rows * depth + (rows + depth) * count * tile)
        ),
        name=name,
    )(table, *attended, wo, *follows)


def add_kernel(lay, blocks, table, *refs):
    x_refs, own, received = refs[:blocks], refs[blocks], refs[blocks + 1]
    outs, moved = refs[blocks + 2 : -1], refs[-1]
    rows = moved.shape[1]
    place = 0
    for x in x_refs:
        for at in range(0, x.shape[0], rows):
            summed = own[place].astype(jnp.float32) + received[place].astype(jnp.float32)
            moved[table[lay.sent_as + place]] = (
                x[at : at + rows].astype(jnp.float32) + summed
            ).astype(jnp.bfloat16)
            place += 1
    for n, out in enumerate(outs):
        for flip in range(CORES):
            out[flip] = moved[n * CORES + flip]


def make_sum(lay, table, arrived, own, received, first):
    spans, rows, cols = received.shape
    chunk = first // cols
    whole = lambda n, t: (0, 0, 0)
    return pl.pallas_call(
        functools.partial(add_kernel, lay, len(arrived)),
        grid_spec=pltpu.PrefetchScalarGridSpec(
            num_scalar_prefetch=1,
            grid=(1,),
            in_specs=[pl.BlockSpec((x.shape[0], cols), lambda n, t: (0, chunk)) for x in arrived]
            + [pl.BlockSpec((spans, rows, cols), whole)] * 2,
            out_specs=[pl.BlockSpec((CORES, rows, cols), whole)] * lay.chips,
            scratch_shapes=[pltpu.VMEM((spans, rows, cols), jnp.bfloat16)],
        ),
        out_shape=[jax.ShapeDtypeStruct((CORES, rows, cols), jnp.bfloat16)] * lay.chips,
        compiler_params=params(12),
        cost_estimate=cost(3 * spans * rows * cols, 8 * spans * rows * cols),
        name="residual",
    )(table, *arrived, own, received)


def place_kernel(lay, table, *refs):
    same, swapped, out = refs[: lay.chips], refs[lay.chips], refs[-1]
    rows = swapped.shape[1]
    group_rank = table[lay.group_rank]
    chip, core = lax.div(group_rank, CORES), lax.rem(group_rank, CORES)
    for n, hop in enumerate(hop_order(lay.chips)):
        owner = lax.rem(chip + lay.chips - hop, lay.chips) * CORES
        for block, at_core in ((same[n][0], core), (swapped[n], 1 - core)):
            at = pl.multiple_of((owner + at_core) * rows, rows)
            out[pl.ds(at, rows)] = block


def make_placed(lay, table, same, swapped, first, cols, whole):
    chips, rows, tile = swapped.shape
    chunk = first // tile
    return pl.pallas_call(
        functools.partial(place_kernel, lay),
        grid_spec=pltpu.PrefetchScalarGridSpec(
            num_scalar_prefetch=1,
            grid=(1,),
            in_specs=[pl.BlockSpec((CORES, rows, tile), lambda n, t: (0, 0, 0))] * chips
            + [pl.BlockSpec((chips, rows, tile), lambda n, t: (0, 0, 0))]
            + [pl.BlockSpec(memory_space=pl.ANY)] * len(whole),
            out_specs=pl.BlockSpec((chips * CORES * rows, tile), lambda n, t: (0, chunk)),
        ),
        out_shape=jax.ShapeDtypeStruct((chips * CORES * rows, cols), jnp.bfloat16),
        input_output_aliases={chips + 2: 0} if whole else {},
        compiler_params=params(12),
        cost_estimate=cost(0, 4 * chips * CORES * rows * tile),
        name="placed",
    )(table, *same, swapped, *whole)


def rope_tables(earlier, span_len, first_row, rows, head):
    half = head // 2
    freqs = jnp.power(
        jnp.float32(rope_base), -jnp.arange(half, dtype=jnp.float32) * 2.0 / head
    )
    at = earlier[:, None] * span_len + first_row + jnp.arange(rows, dtype=jnp.int32)[None, :]
    angles = at.reshape(-1).astype(jnp.float32)[:, None] * freqs[None, :]
    cosine, sine = jnp.cos(angles), jnp.sin(angles)
    return (
        jnp.concatenate([cosine, cosine], axis=1),
        jnp.concatenate([-sine, sine], axis=1),
    )


def after(x, done):
    return lax.optimization_barrier((x, done))[0]


def shift(x, owners, hop, flip):
    chips = owners // CORES
    pairs = [
        (z * CORES + c, (z + hop) % chips * CORES + (c ^ flip))
        for z in range(chips)
        for c in range(CORES)
    ]
    return lax.ppermute(x, "group", pairs)


def local(
    hidden_in, ln_gain, wq, wk, wv, q_gain, key_norm_gain, wo,
    prompt_spans, span_source, span_target, page_slot,
):
    _, span_len, cols = hidden_in.shape
    tensor_size = lax.axis_size("tensor")
    owners = lax.axis_size("group")
    tensor_rank = lax.axis_index("tensor")
    group_rank = lax.axis_index("group")
    chips = owners // CORES
    head = q_gain.shape[0]
    rows = span_len // owners
    pages_each = span_len // PAGE_ROWS
    spans = span_source.shape[0]
    here = spans // PARTS
    most = min(spans - (prompt_spans.shape[0] - 1), spans // 2)
    kv_cols = wk.shape[1]
    paired = tensor_size == 2
    swap = [(0, 1), (1, 0)]
    lay = Layout(spans, spans * pages_each, owners)

    if kv_cols < head:
        share = head // kv_cols
        sets = [list(range(i, i + share)) for i in range(0, tensor_size, share)]
        wk, wv = [
            lax.all_gather(w, "tensor", axis=1, tiled=True, axis_index_groups=sets)
            for w in (wk, wv)
        ]
    per_kv = wq.shape[1] // max(head, wk.shape[1])

    chip, core = group_rank // CORES, group_rank % CORES
    split = hidden_in.reshape(owners, rows, cols)

    def rows_for(hop, flip):
        to = lax.rem(chip + hop, chips) * CORES + lax.rem(core + flip, CORES)
        return lax.dynamic_index_in_dim(split, to, 0, keepdims=False)

    cross = lambda x: lax.ppermute(x, "tensor", swap)

    hops = hop_order(chips)
    paired_hops = hops[2:]
    near = [rows_for(hop, flip) for hop in hops[1:2] for flip in range(CORES)]
    split = after(split, near)
    near = [shift(x, owners, hops[1], flip) for flip, x in enumerate(near)]
    swapped = shift(
        jnp.stack([rows_for(hop, 1) for hop in hops[:1] + paired_hops]), owners, 0, 1
    )
    arrived = [rows_for(0, 0), swapped[0]] + near
    moves = []
    for n, hop in enumerate(paired_hops):
        pair = [rows_for(hop, 0), swapped[1 + n]]
        if n < len(paired_hops) - 1:
            moves.append((hop, jnp.concatenate(pair)))
        else:
            moves += [(hop, block) for block in pair]

    ranks = jnp.stack([group_rank, tensor_rank]).astype(jnp.int32)
    table = make_tables(
        lay, spans, spans * pages_each, ranks, prompt_spans, span_source, span_target, page_slot
    )
    earlier = table[lay.earlier_at : lay.earlier_at + spans]
    cosine, sine = rope_tables(earlier, span_len, group_rank * rows, rows, head)

    crossed = [cross(x) for x in arrived] if paired else []
    if paired:
        gain = ln_gain[None]
        gains = [gain, cross(after(gain, swapped))]
    else:
        gains = [lax.all_gather(ln_gain, "tensor", axis=0, tiled=True)[None]]

    kvs, norms = [], []

    def make_part(own_rows, crossed_rows, done):
        if paired:
            xs = [own_rows, crossed_rows]
        else:
            xs = [[lax.all_gather(jnp.concatenate(own_rows), "tensor", axis=1, tiled=True)]]
        kgain = after(key_norm_gain[None], done)
        *normed, kv = make_kv(lay, table, xs, gains, wk, wv, kgain, cosine, sine, len(kvs))
        kvs.append([kv.reshape(2, here, rows, kv.shape[2])])
        norms.append(normed)

    def one_back(p, done=()):
        kvs[p].append(shift(after(kvs[p][-1], done) if done else kvs[p][-1], owners, 1, 0))

    begun = 0
    for n in range(len(moves) + 1):
        if n:
            hop, block = moves[n - 1]
            if paired:
                landed = arrived[-1:] if n > 1 else near
                matching = crossed[2 * n - 2 : 2 * n] if n < 3 else crossed[n + 1]
                block = after(block, (landed, matching, gains))
            arrived.append(shift(block, owners, hop, 0))
            if paired:
                block = arrived[-1]
                if n == len(moves) and kvs:
                    block = after(block, kvs[0][0])
                crossed.append(cross(block))
        if sum(x.shape[0] for x in arrived[begun:]) == here * rows:
            make_part(arrived[begun:], crossed[begun:], kvs[0][1:2] if kvs else arrived[0])
            begun = len(arrived)
            for _ in range(min(2, chips - 1) if len(kvs) == 1 else min(1, chips - 1)):
                one_back(len(kvs) - 1)

    queries, done = [], (kvs[1][0], kvs[0][-1])
    for p in range(PARTS):
        made = make_q(
            lay, table, norms[p], wq, after(q_gain[None], done), cosine, sine, p
        )
        queries.append(made.reshape(here, rows, made.shape[1]))
        done = queries[-1]
    for p in range(PARTS):
        while len(kvs[p]) < chips:
            one_back(p, (queries, kvs[0][-1]) if p else ())
    gathered = []
    for back in range(chips):
        gathered.append([kv[back] for kv in kvs])
        gathered.append([shift(kv[back], owners, 0, 1) for kv in kvs])

    own_kv = wk.shape[1] // head
    sets = [own_kv // 2, own_kv - own_kv // 2] if own_kv > 1 else [own_kv]
    attended, pages, first = [], [], 0
    for count in sets:
        made, cut = make_attention(
            lay, most, table, queries, gathered, per_kv, head, pages_each, first, count
        )
        attended.append(made.reshape(spans * rows, -1))
        pages.append(cut)
        first += count

    if paired:
        tile = 512 if cols % 512 == 0 else cols
        tiles = cols // tile
        widths = [2, 2, 1] if tiles == 5 else [tiles]
        others = [cross(pages[0])]
        project = functools.partial(make_projection, lay, table, attended, wo, tile)
        send = project(lambda r: (1 - r) * tiles, widths[:1], "send_part", (others[0],))
        if widths[1:]:
            send += project(
                lambda r: (1 - r) * tiles + widths[0], widths[1:], "send_part", (send[0],)
            )
        own = project(lambda r: r * tiles, widths, "own_part", (send[-1],))
        whole, received, landed, first = (), [], [], 0
        for n, sent in enumerate(send):
            if n:
                sent = after(sent, (received[-1], own, landed[-2:-1]))
            received.append(cross(sent))
            moved = make_sum(
                lay, table, arrived, own[n].reshape(spans, rows, -1),
                received[-1].reshape(spans, rows, -1), first,
            )
            same = [
                shift(x, owners, hop, 0) if hop else x
                for hop, x in zip(hop_order(chips), moved)
            ]
            landed.append(same)
            swapped = shift(jnp.concatenate([x[1:] for x in same]), owners, 0, 1)
            whole = (make_placed(lay, table, same, swapped, first, cols, whole),)
            first += sent.shape[1]
        mixed = whole[0].reshape(1, span_len, cols)
        for cut in pages[1:]:
            others.append(cross(after(cut, received[-1])))
        low = [jnp.where(tensor_rank == 0, a, b) for a, b in zip(pages, others)]
        high = [jnp.where(tensor_rank == 0, b, a) for a, b in zip(pages, others)]
        cache = jnp.concatenate(low + high, axis=3)
    else:
        pages = jnp.concatenate(pages, axis=3)
        attended = jnp.concatenate(attended, axis=1)
        if kv_cols < head:
            pages = lax.dynamic_slice_in_dim(
                pages, lax.rem(tensor_rank, head // kv_cols) * kv_cols, kv_cols, 3
            )
        cache = lax.all_gather(pages, "tensor", axis=3, tiled=True)
        partial = jnp.dot(attended, wo, preferred_element_type=jnp.float32)
        summed = lax.psum_scatter(
            partial.astype(jnp.bfloat16), "tensor", scatter_dimension=1, tiled=True
        )
        summed = summed.reshape(spans, rows, cols).astype(jnp.float32)
        x = jnp.concatenate(arrived).reshape(spans, rows, cols).astype(jnp.float32)
        moved = (x + summed).astype(jnp.bfloat16)
        targets = table[lay.target_at : lay.target_at + spans]
        moved = jnp.zeros_like(moved).at[targets].set(moved, unique_indices=True)
        moved = lax.all_to_all(moved, "group", split_axis=0, concat_axis=0, tiled=True)
        mixed = moved.reshape(1, span_len, cols)
    return (mixed, cache)


def solution(mesh):
    in_specs = (
        P(("replica", "group"), None, "tensor"),
        P("tensor"),
        P(None, "tensor"),
        P(None, "tensor"),
        P(None, "tensor"),
        P(),
        P(),
        P("tensor", None),
        P("replica"),
        P("replica"),
        P("replica"),
        P("replica"),
    )
    out_specs = (P(("replica", "group"), None, "tensor"), P(("replica", "group"), None, None, None))
    return jax.shard_map(local, mesh=mesh, in_specs=in_specs, out_specs=out_specs, check_vma=False)
```

```python
import functools
import math

import jax
import jax.numpy as jnp
from jax import lax
from jax.experimental import pallas as pl
from jax.experimental.pallas import tpu as pltpu
from jax.sharding import PartitionSpec as P

PAGE_ROWS = 128
epsilon = 1e-06
rope_base = 1000000.0
very_negative = -1e30
PARTS = 2
CORES = 2
SHARE = 0.02


def params(mebibytes):
    return pltpu.CompilerParams(vmem_limit_bytes=mebibytes * 1024 * 1024)


def in_hbm(x):
    return pltpu.with_memory_space_constraint(x, pltpu.HBM)


def cost(flops, moved, transcendentals=0):
    return pl.CostEstimate(
        flops=int(flops * SHARE),
        bytes_accessed=int(moved * SHARE),
        transcendentals=int(transcendentals * SHARE),
    )


def hop_order(chips):
    return [0, 1, chips - 1] + list(range(2, chips - 1)) if chips > 2 else list(range(chips))


class Layout:
    def __init__(self, spans, pages, owners):
        self.chips = owners // CORES
        self.span_at = 0
        self.earlier_at = self.span_at + spans
        self.target_at = self.earlier_at + spans
        self.sent_as = self.target_at + spans
        self.page = self.sent_as + spans
        self.origin = self.page + pages
        self.group_rank = self.origin + owners * spans
        self.tensor_rank = self.group_rank + 1
        self.length = self.tensor_rank + 1


def tables_kernel(lay, spans, pages, ranks, prompt_spans, source, target, page_slot, out, span_of, start_of):
    chips = lay.chips
    group_rank = ranks[0]
    out[lay.group_rank] = group_rank
    out[lay.tensor_rank] = ranks[1]
    for k in range(spans):
        start = jnp.int32(0)
        begin = jnp.int32(0)
        for p in range(prompt_spans.shape[0]):
            start = jnp.where(begin <= k, begin, start)
            begin = begin + prompt_spans[p]
        start_of[k] = start
        span_of[source[k]] = jnp.int32(k)
    for p in range(pages):
        out[lay.page + page_slot[p]] = jnp.int32(p)
    chip, core = lax.div(group_rank, CORES), lax.rem(group_rank, CORES)
    hops = hop_order(chips)
    for back in range(chips):
        for other in range(CORES):
            at_chip = lax.rem(chip + chips - back, chips)
            at_core = jnp.where(other == 0, core, 1 - core)
            for n, hop in enumerate(hops):
                for flip in range(CORES):
                    from_chip = lax.rem(at_chip + chips - hop, chips)
                    from_core = jnp.where(flip == 0, at_core, 1 - at_core)
                    k = span_of[from_chip * CORES + from_core]
                    place = n * CORES + flip
                    out[lay.origin + (back * CORES + other) * spans + place] = k
                    if back == 0 and other == 0:
                        out[lay.span_at + place] = k
                        out[lay.earlier_at + place] = k - start_of[k]
                        owner = target[k]
                        ahead = lax.rem(lax.div(owner, CORES) + chips - chip, chips)
                        turn = jnp.int32(0)
                        for m, other_hop in enumerate(hops):
                            turn = jnp.where(ahead == other_hop, jnp.int32(m), turn)
                        crossing = jnp.where(lax.rem(owner, CORES) == core, 0, 1)
                        out[lay.target_at + place] = owner
                        out[lay.sent_as + place] = turn * CORES + crossing


def make_tables(lay, spans, pages, ranks, prompt_spans, source, target, page_slot):
    smem = pl.BlockSpec(memory_space=pltpu.SMEM)
    return pl.pallas_call(
        functools.partial(tables_kernel, lay, spans, pages),
        out_shape=jax.ShapeDtypeStruct((lay.length,), jnp.int32),
        in_specs=[smem] * 5,
        out_specs=smem,
        scratch_shapes=[pltpu.SMEM((spans,), jnp.int32)] * 2,
        name="tables",
    )(ranks, prompt_spans, source, target, page_slot)


def head_norm_rope(u, gain, cosine, sine):
    mean_sq = jnp.mean(u * u, axis=-1, keepdims=True)
    u = u * lax.rsqrt(mean_sq + epsilon) * gain
    half = u.shape[-1] // 2
    return u * cosine + pltpu.roll(u, half, 1) * sine


def half_index(lay, sides, side):
    if sides == 1:
        return lambda t: 0
    if side == 0:
        return lambda t: t[lay.tensor_rank]
    return lambda t: 1 - t[lay.tensor_rank]


def summed_dot(lefts, rights):
    total = None
    for left, right in zip(lefts, rights):
        term = jnp.dot(left[...], right[...], preferred_element_type=jnp.float32)
        total = term if total is None else total + term
    return total


def kv_kernel(sides, blocks, table, *refs):
    refs = list(refs)
    take = lambda n: [refs.pop(0) for _ in range(n)]
    xs = [take(blocks) for _ in range(sides)]
    gains, wks, wvs = take(sides), take(sides), take(sides)
    kgain, cosine, sine = take(3)
    normed, (kv,) = take(sides), take(1)
    head = kgain.shape[1]
    width = sum(x[0].shape[1] for x in xs)

    @pl.when(pl.program_id(0) == 0)
    def _():
        at = 0
        for b in range(blocks):
            wide = [x[b][...].astype(jnp.float32) for x in xs]
            total = sum(jnp.sum(w * w, axis=-1, keepdims=True) for w in wide)
            factor = lax.rsqrt(total / width + epsilon)
            rows = xs[0][b].shape[0]
            for w, gain, to in zip(wide, gains, normed):
                to[at : at + rows] = (w * factor * gain[...].astype(jnp.float32)).astype(
                    jnp.bfloat16
                )
            at += rows

    keys = summed_dot(normed, wks).astype(jnp.bfloat16)
    gains = kgain[...].astype(jnp.float32)
    for h in range(keys.shape[1] // head):
        u = keys[:, h * head : (h + 1) * head].astype(jnp.float32)
        kv[0, :, h * head : (h + 1) * head] = head_norm_rope(
            u, gains, cosine[...], sine[...]
        ).astype(jnp.bfloat16)
    kv[1] = summed_dot(normed, wvs).astype(jnp.bfloat16)


def make_kv(lay, table, xs, gains, wk, wv, kgain, cosine, sine, part):
    sides, blocks = len(xs), len(xs[0])
    rows = sum(x.shape[0] for x in xs[0])
    widths = [x[0].shape[1] for x in xs]
    width, cols = wk.shape
    tile = 256 if cols % 256 == 0 else cols
    head = kgain.shape[1]
    fixed = lambda n, t: (0, 0)
    here = lambda n, t: (part, 0)
    weights = []
    for side in range(sides):
        index = half_index(lay, sides, side)
        weights.append(
            pl.BlockSpec((widths[side], tile), lambda n, t, index=index: (index(t), n))
        )
    return pl.pallas_call(
        functools.partial(kv_kernel, sides, blocks),
        grid_spec=pltpu.PrefetchScalarGridSpec(
            num_scalar_prefetch=1,
            grid=(cols // tile,),
            in_specs=[pl.BlockSpec(x.shape, fixed) for side in xs for x in side]
            + [pl.BlockSpec((1, w), fixed) for w in widths]
            + weights
            + weights
            + [
                pl.BlockSpec((1, head), fixed),
                pl.BlockSpec((rows, head), here),
                pl.BlockSpec((rows, head), here),
            ],
            out_specs=[pl.BlockSpec((rows, w), fixed) for w in widths]
            + [pl.BlockSpec((2, rows, tile), lambda n, t: (0, 0, n))],
        ),
        out_shape=[jax.ShapeDtypeStruct((rows, w), jnp.bfloat16) for w in widths]
        + [jax.ShapeDtypeStruct((2, rows, cols), jnp.bfloat16)],
        compiler_params=params(32),
        cost_estimate=cost(4 * rows * width * cols, 4 * width * cols + 4 * rows * width),
        name="keys_values",
    )(
        table, *[x for side in xs for x in side], *gains,
        *[in_hbm(wk)] * sides, *[in_hbm(wv)] * sides,
        kgain, cosine, sine,
    )


def q_kernel(sides, table, *refs):
    normed, wqs = refs[:sides], refs[sides : 2 * sides]
    qgain, cosine, sine, out = refs[2 * sides :]
    head = qgain.shape[1]
    lin = summed_dot(normed, wqs)
    gains = qgain[...].astype(jnp.float32)
    for h in range(lin.shape[1] // head):
        out[:, h * head : (h + 1) * head] = head_norm_rope(
            lin[:, h * head : (h + 1) * head], gains, cosine[...], sine[...]
        ).astype(jnp.bfloat16)


def make_q(lay, table, normed, wq, qgain, cosine, sine, part):
    sides = len(normed)
    rows = normed[0].shape[0]
    width, cols = wq.shape
    tile = 512 if cols % 512 == 0 else cols
    head = qgain.shape[1]
    fixed = lambda n, t: (0, 0)
    here = lambda n, t: (part, 0)
    weights = []
    for side in range(sides):
        index = half_index(lay, sides, side)
        weights.append(
            pl.BlockSpec(
                (normed[side].shape[1], tile), lambda n, t, index=index: (index(t), n)
            )
        )
    return pl.pallas_call(
        functools.partial(q_kernel, sides),
        grid_spec=pltpu.PrefetchScalarGridSpec(
            num_scalar_prefetch=1,
            grid=(cols // tile,),
            in_specs=[pl.BlockSpec(x.shape, fixed) for x in normed]
            + weights
            + [
                pl.BlockSpec((1, head), fixed),
                pl.BlockSpec((rows, head), here),
                pl.BlockSpec((rows, head), here),
            ],
            out_specs=pl.BlockSpec((rows, tile), lambda n, t: (0, n)),
        ),
        out_shape=jax.ShapeDtypeStruct((rows, cols), jnp.bfloat16),
        compiler_params=params(24),
        cost_estimate=cost(2 * rows * width * cols, 2 * width * cols + 2 * rows * (width + cols)),
        name="queries",
    )(table, *normed, *[in_hbm(wq)] * sides, qgain, cosine, sine)


def attention_kernel(lay, spans, most, per_kv, head, owners, pages_each, table, *refs):
    q_refs = refs[:PARTS]
    kv_refs = refs[PARTS : PARTS + owners * PARTS]
    out, pages, keys, values = refs[PARTS + owners * PARTS :]
    chips = lay.chips
    here, rows = kv_refs[0].shape[1], kv_refs[0].shape[2]
    group_rank = table[lay.group_rank]
    chip, core = lax.div(group_rank, CORES), lax.rem(group_rank, CORES)
    for o in range(owners):
        back, other = o // CORES, o % CORES
        owner = lax.rem(chip + chips - back, chips) * CORES + (core if other == 0 else 1 - core)
        at = pl.ds(pl.multiple_of(owner * rows, rows), rows)
        for p in range(PARTS):
            for i in range(here):
                k = table[lay.origin + o * spans + p * here + i]
                keys[k, at] = kv_refs[o * PARTS + p][0, i]
                values[k, at] = kv_refs[o * PARTS + p][1, i]

    for i in range(pages_each):
        page = table[lay.page + group_rank * pages_each + i]
        k = lax.div(page, pages_each)
        at = pl.ds(pl.multiple_of(lax.rem(page, pages_each) * PAGE_ROWS, PAGE_ROWS), PAGE_ROWS)
        pages[i, 0] = keys[k, at]
        pages[i, 1] = values[k, at]

    scale = (1.0 / math.sqrt(head)) * math.log2(math.e)
    q_rows, k_rows = per_kv * rows, owners * rows
    row = lax.broadcasted_iota(jnp.int32, (q_rows, k_rows), 0)
    col = lax.broadcasted_iota(jnp.int32, (q_rows, k_rows), 1)
    allowed = col <= group_rank * rows + row % rows

    def one_place(p, i, carry):
        k = table[lay.span_at + p * here + i]
        earlier = table[lay.earlier_at + p * here + i]
        queries = jnp.concatenate(
            [q_refs[p][i, :, g * head : (g + 1) * head] for g in range(per_kv)], axis=0
        )

        def with_earlier(count):
            scores = []
            for back in range(count + 1):
                s = lax.dot_general(
                    queries, keys[k - back], (((1,), (1,)), ((), ())),
                    preferred_element_type=jnp.float32,
                )
                if back == 0:
                    s = jnp.where(allowed, s, very_negative)
                scores.append(s)
            best = scores[0]
            for s in scores[1:]:
                best = jnp.maximum(best, s)
            best = jnp.max(best, axis=-1, keepdims=True)
            total = None
            summed = None
            for back, s in enumerate(scores):
                w = jnp.exp2((s - best) * scale)
                part = jnp.sum(w, axis=-1, keepdims=True)
                term = jnp.dot(
                    w.astype(jnp.bfloat16), values[k - back], preferred_element_type=jnp.float32
                )
                total = part if total is None else total + part
                summed = term if summed is None else summed + term
            result = (summed / total).astype(jnp.bfloat16)
            for g in range(per_kv):
                out[p * here + i, :, g * head : (g + 1) * head] = result[
                    g * rows : (g + 1) * rows
                ]

        for count in range(most):
            pl.when(earlier == count)(functools.partial(with_earlier, count))
        return carry

    for p in range(PARTS):
        lax.fori_loop(0, here, functools.partial(one_place, p), 0)


def make_attention(lay, most, table, queries, gathered, per_kv, head, pages_each, first, count):
    here, rows, cols = queries[0].shape
    spans = here * PARTS
    owners = len(gathered)
    q_spec = pl.BlockSpec((here, rows, per_kv * head), lambda h, t: (0, 0, first + h))
    kv_spec = pl.BlockSpec((2, here, rows, head), lambda h, t: (0, 0, 0, first + h))
    flat = [x for origin in gathered for x in origin]
    all_rows = spans * rows
    pairs = 2.2 * all_rows * owners * rows * per_kv * count
    return pl.pallas_call(
        functools.partial(
            attention_kernel, lay, spans, most, per_kv, head, owners, pages_each
        ),
        grid_spec=pltpu.PrefetchScalarGridSpec(
            num_scalar_prefetch=1,
            grid=(count,),
            in_specs=[q_spec] * PARTS + [kv_spec] * len(flat),
            out_specs=[
                pl.BlockSpec((spans, rows, per_kv * head), lambda h, t: (0, 0, h)),
                pl.BlockSpec((pages_each, 2, PAGE_ROWS, head), lambda h, t: (0, 0, 0, h)),
            ],
            scratch_shapes=[pltpu.VMEM((spans, owners * rows, head), jnp.bfloat16)] * 2,
        ),
        out_shape=[
            jax.ShapeDtypeStruct((spans, rows, count * per_kv * head), jnp.bfloat16),
            jax.ShapeDtypeStruct((pages_each, 2, PAGE_ROWS, count * head), jnp.bfloat16),
        ],
        compiler_params=params(20),
        cost_estimate=cost(
            4 * pairs * head, 4 * all_rows * cols + 2 * len(flat) * flat[0].size, pairs
        ),
        name="attention",
    )(table, *queries, *flat)


def project_kernel(pieces, follows, tile, table, *refs):
    attended, wo, outs = refs[:pieces], refs[pieces], refs[pieces + 1 + follows :]
    total, at = None, 0
    for piece in attended:
        depth = piece.shape[1]
        term = jnp.dot(piece[...], wo[at : at + depth], preferred_element_type=jnp.float32)
        total = term if total is None else total + term
        at += depth
    total = total.astype(jnp.bfloat16)
    step = 0
    for out in outs:
        for at in range(0, out.shape[1], tile):

            @pl.when(pl.program_id(0) == step)
            def _(out=out, at=at):
                out[:, at : at + tile] = total

            step += 1


def make_projection(lay, table, attended, wo, tile, first, widths, name, follows=()):
    rows = attended[0].shape[0]
    depth = wo.shape[0]
    count = sum(widths)
    return pl.pallas_call(
        functools.partial(project_kernel, len(attended), len(follows), tile),
        grid_spec=pltpu.PrefetchScalarGridSpec(
            num_scalar_prefetch=1,
            grid=(count,),
            in_specs=[pl.BlockSpec(x.shape, lambda n, t: (0, 0)) for x in attended]
            + [pl.BlockSpec((depth, tile), lambda n, t: (0, first(t[lay.tensor_rank]) + n))]
            + [pl.BlockSpec(memory_space=pl.ANY)] * len(follows),
            out_specs=[pl.BlockSpec((rows, w * tile), lambda n, t: (0, 0)) for w in widths],
        ),
        out_shape=[jax.ShapeDtypeStruct((rows, w * tile), jnp.bfloat16) for w in widths],
        compiler_params=params(20),
        cost_estimate=cost(
            2 * rows * depth * count * tile, 2 * (rows * depth + (rows + depth) * count * tile)
        ),
        name=name,
    )(table, *attended, in_hbm(wo), *follows)


def add_kernel(lay, blocks, table, *refs):
    x_refs, own, received = refs[:blocks], refs[blocks], refs[blocks + 1]
    outs, moved = refs[blocks + 2 : -1], refs[-1]
    rows = moved.shape[1]
    place = 0
    for x in x_refs:
        for at in range(0, x.shape[0], rows):
            summed = own[place].astype(jnp.float32) + received[place].astype(jnp.float32)
            moved[table[lay.sent_as + place]] = (
                x[at : at + rows].astype(jnp.float32) + summed
            ).astype(jnp.bfloat16)
            place += 1
    for n, out in enumerate(outs):
        for flip in range(CORES):
            out[flip] = moved[n * CORES + flip]


def make_sum(lay, table, arrived, own, received, first):
    spans, rows, cols = received.shape
    chunk = first // cols
    whole = lambda n, t: (0, 0, 0)
    return pl.pallas_call(
        functools.partial(add_kernel, lay, len(arrived)),
        grid_spec=pltpu.PrefetchScalarGridSpec(
            num_scalar_prefetch=1,
            grid=(1,),
            in_specs=[pl.BlockSpec((x.shape[0], cols), lambda n, t: (0, chunk)) for x in arrived]
            + [pl.BlockSpec((spans, rows, cols), whole)] * 2,
            out_specs=[pl.BlockSpec((CORES, rows, cols), whole)] * lay.chips,
            scratch_shapes=[pltpu.VMEM((spans, rows, cols), jnp.bfloat16)],
        ),
        out_shape=[jax.ShapeDtypeStruct((CORES, rows, cols), jnp.bfloat16)] * lay.chips,
        compiler_params=params(12),
        cost_estimate=cost(3 * spans * rows * cols, 8 * spans * rows * cols),
        name="residual",
    )(table, *arrived, own, received)


def place_kernel(lay, table, *refs):
    same, swapped, out = refs[: lay.chips], refs[lay.chips], refs[-1]
    rows = swapped.shape[1]
    group_rank = table[lay.group_rank]
    chip, core = lax.div(group_rank, CORES), lax.rem(group_rank, CORES)
    for n, hop in enumerate(hop_order(lay.chips)):
        owner = lax.rem(chip + lay.chips - hop, lay.chips) * CORES
        for block, at_core in ((same[n][0], core), (swapped[n], 1 - core)):
            at = pl.multiple_of((owner + at_core) * rows, rows)
            out[pl.ds(at, rows)] = block


def make_placed(lay, table, same, swapped, first, cols, whole):
    chips, rows, tile = swapped.shape
    chunk = first // tile
    return pl.pallas_call(
        functools.partial(place_kernel, lay),
        grid_spec=pltpu.PrefetchScalarGridSpec(
            num_scalar_prefetch=1,
            grid=(1,),
            in_specs=[pl.BlockSpec((CORES, rows, tile), lambda n, t: (0, 0, 0))] * chips
            + [pl.BlockSpec((chips, rows, tile), lambda n, t: (0, 0, 0))]
            + [pl.BlockSpec(memory_space=pl.ANY)] * len(whole),
            out_specs=pl.BlockSpec((chips * CORES * rows, tile), lambda n, t: (0, chunk)),
        ),
        out_shape=jax.ShapeDtypeStruct((chips * CORES * rows, cols), jnp.bfloat16),
        input_output_aliases={chips + 2: 0} if whole else {},
        compiler_params=params(12),
        cost_estimate=cost(0, 4 * chips * CORES * rows * tile),
        name="placed",
    )(table, *same, swapped, *whole)


def rope_tables(earlier, span_len, first_row, rows, head):
    half = head // 2
    freqs = jnp.power(
        jnp.float32(rope_base), -jnp.arange(half, dtype=jnp.float32) * 2.0 / head
    )
    at = earlier[:, None] * span_len + first_row + jnp.arange(rows, dtype=jnp.int32)[None, :]
    angles = at.reshape(-1).astype(jnp.float32)[:, None] * freqs[None, :]
    cosine, sine = jnp.cos(angles), jnp.sin(angles)
    return (
        jnp.concatenate([cosine, cosine], axis=1),
        jnp.concatenate([-sine, sine], axis=1),
    )


def after(x, done):
    return lax.optimization_barrier((x, done))[0]


def shift(x, owners, hop, flip):
    chips = owners // CORES
    pairs = [
        (z * CORES + c, (z + hop) % chips * CORES + (c ^ flip))
        for z in range(chips)
        for c in range(CORES)
    ]
    return lax.ppermute(x, "group", pairs)


def local(
    hidden_in, ln_gain, wq, wk, wv, q_gain, key_norm_gain, wo,
    prompt_spans, span_source, span_target, page_slot,
):
    _, span_len, cols = hidden_in.shape
    tensor_size = lax.axis_size("tensor")
    owners = lax.axis_size("group")
    tensor_rank = lax.axis_index("tensor")
    group_rank = lax.axis_index("group")
    chips = owners // CORES
    head = q_gain.shape[0]
    rows = span_len // owners
    pages_each = span_len // PAGE_ROWS
    spans = span_source.shape[0]
    here = spans // PARTS
    most = min(spans - (prompt_spans.shape[0] - 1), spans // 2)
    kv_cols = wk.shape[1]
    paired = tensor_size == 2
    swap = [(0, 1), (1, 0)]
    lay = Layout(spans, spans * pages_each, owners)

    if kv_cols < head:
        share = head // kv_cols
        sets = [list(range(i, i + share)) for i in range(0, tensor_size, share)]
        wk, wv = [
            lax.all_gather(w, "tensor", axis=1, tiled=True, axis_index_groups=sets)
            for w in (wk, wv)
        ]
    per_kv = wq.shape[1] // max(head, wk.shape[1])

    chip, core = group_rank // CORES, group_rank % CORES
    split = hidden_in.reshape(owners, rows, cols)

    def rows_for(hop, flip):
        to = lax.rem(chip + hop, chips) * CORES + lax.rem(core + flip, CORES)
        return lax.dynamic_index_in_dim(split, to, 0, keepdims=False)

    cross = lambda x: lax.ppermute(x, "tensor", swap)

    hops = hop_order(chips)
    paired_hops = hops[2:]
    near = [rows_for(hop, flip) for hop in hops[1:2] for flip in range(CORES)]
    near = [shift(x, owners, hops[1], flip) for flip, x in enumerate(near)]
    swapped = shift(
        jnp.stack([rows_for(hop, 1) for hop in hops[:1] + paired_hops]), owners, 0, 1
    )
    arrived = [rows_for(0, 0), swapped[0]] + near
    moves = []
    for n, hop in enumerate(paired_hops):
        pair = [rows_for(hop, 0), swapped[1 + n]]
        if n < len(paired_hops) - 1:
            moves.append((hop, jnp.concatenate(pair)))
        else:
            moves += [(hop, block) for block in pair]

    ranks = jnp.stack([group_rank, tensor_rank]).astype(jnp.int32)
    table = make_tables(
        lay, spans, spans * pages_each, ranks, prompt_spans, span_source, span_target, page_slot
    )
    earlier = table[lay.earlier_at : lay.earlier_at + spans]
    cosine, sine = rope_tables(earlier, span_len, group_rank * rows, rows, head)

    crossed = [cross(x) for x in arrived] if paired else []
    if paired:
        gain = ln_gain[None]
        gains = [gain, cross(after(gain, swapped))]
    else:
        gains = [lax.all_gather(ln_gain, "tensor", axis=0, tiled=True)[None]]

    kvs, norms = [], []

    def make_part(own_rows, crossed_rows):
        if paired:
            xs = [own_rows, crossed_rows]
        else:
            xs = [[lax.all_gather(jnp.concatenate(own_rows), "tensor", axis=1, tiled=True)]]
        *normed, kv = make_kv(
            lay, table, xs, gains, wk, wv, key_norm_gain[None], cosine, sine, len(kvs)
        )
        kvs.append([kv.reshape(2, here, rows, kv.shape[2])])
        norms.append(normed)

    def one_back(p, done=()):
        kvs[p].append(shift(after(kvs[p][-1], done), owners, 1, 0))

    begun = 0
    for n in range(len(moves) + 1):
        if n:
            hop, block = moves[n - 1]
            if paired:
                landed = arrived[-1:] if n > 1 else near
                matching = crossed[2 * n - 2 : 2 * n] if n < 3 else crossed[n + 1]
                block = after(block, (landed, matching, gains))
            arrived.append(shift(block, owners, hop, 0))
            if paired:
                block = arrived[-1]
                if n == len(moves) and kvs:
                    block = after(block, kvs[0][0])
                crossed.append(cross(block))
        if sum(x.shape[0] for x in arrived[begun:]) == here * rows:
            make_part(arrived[begun:], crossed[begun:])
            begun = len(arrived)
            for _ in range(min(2, chips - 1) if len(kvs) == 1 else min(1, chips - 1)):
                one_back(len(kvs) - 1)

    queries, done = [], kvs[1][0]
    for p in range(PARTS):
        made = make_q(
            lay, table, norms[p], wq, after(q_gain[None], done), cosine, sine, p
        )
        queries.append(made.reshape(here, rows, made.shape[1]))
        done = queries[-1]
    for p in range(PARTS):
        while len(kvs[p]) < chips:
            one_back(p, queries[p])
    gathered = []
    for back in range(chips):
        gathered.append([kv[back] for kv in kvs])
        gathered.append([shift(kv[back], owners, 0, 1) for kv in kvs])

    own_kv = wk.shape[1] // head
    sets = [own_kv // 2, own_kv - own_kv // 2] if own_kv > 1 else [own_kv]
    attended, pages, first = [], [], 0
    for count in sets:
        made, cut = make_attention(
            lay, most, table, queries, gathered, per_kv, head, pages_each, first, count
        )
        attended.append(made.reshape(spans * rows, -1))
        pages.append(cut)
        first += count

    if paired:
        tile = 512 if cols % 512 == 0 else cols
        tiles = cols // tile
        widths = [2, 2, 1] if tiles == 5 else [tiles]
        others = [cross(pages[0])]
        project = functools.partial(make_projection, lay, table, attended, wo, tile)
        send = project(lambda r: (1 - r) * tiles, widths[:1], "send_part", (others[0],))
        if widths[1:]:
            send += project(
                lambda r: (1 - r) * tiles + widths[0], widths[1:], "send_part", (send[0],)
            )
        own = project(lambda r: r * tiles, widths, "own_part", (send[-1],))
        whole, received, landed, first = (), [], [], 0
        for n, sent in enumerate(send):
            if n:
                sent = after(sent, (received[-1], own, landed[-2:-1]))
            received.append(cross(sent))
            moved = make_sum(
                lay, table, arrived, own[n].reshape(spans, rows, -1),
                received[-1].reshape(spans, rows, -1), first,
            )
            same = [
                shift(x, owners, hop, 0) if hop else x
                for hop, x in zip(hop_order(chips), moved)
            ]
            landed.append(same)
            swapped = shift(jnp.concatenate([x[1:] for x in same]), owners, 0, 1)
            whole = (make_placed(lay, table, same, swapped, first, cols, whole),)
            first += sent.shape[1]
        mixed = whole[0].reshape(1, span_len, cols)
        for cut in pages[1:]:
            others.append(cross(after(cut, received[-1])))
        low = [jnp.where(tensor_rank == 0, a, b) for a, b in zip(pages, others)]
        high = [jnp.where(tensor_rank == 0, b, a) for a, b in zip(pages, others)]
        cache = jnp.concatenate(low + high, axis=3)
    else:
        pages = jnp.concatenate(pages, axis=3)
        attended = jnp.concatenate(attended, axis=1)
        if kv_cols < head:
            pages = lax.dynamic_slice_in_dim(
                pages, lax.rem(tensor_rank, head // kv_cols) * kv_cols, kv_cols, 3
            )
        cache = lax.all_gather(pages, "tensor", axis=3, tiled=True)
        partial = jnp.dot(attended, wo, preferred_element_type=jnp.float32)
        summed = lax.psum_scatter(
            partial.astype(jnp.bfloat16), "tensor", scatter_dimension=1, tiled=True
        )
        summed = summed.reshape(spans, rows, cols).astype(jnp.float32)
        x = jnp.concatenate(arrived).reshape(spans, rows, cols).astype(jnp.float32)
        moved = (x + summed).astype(jnp.bfloat16)
        targets = table[lay.target_at : lay.target_at + spans]
        moved = jnp.zeros_like(moved).at[targets].set(moved, unique_indices=True)
        moved = lax.all_to_all(moved, "group", split_axis=0, concat_axis=0, tiled=True)
        mixed = moved.reshape(1, span_len, cols)
    return (mixed, cache)


def solution(mesh):
    in_specs = (
        P(("replica", "group"), None, "tensor"),
        P("tensor"),
        P(None, "tensor"),
        P(None, "tensor"),
        P(None, "tensor"),
        P(),
        P(),
        P("tensor", None),
        P("replica"),
        P("replica"),
        P("replica"),
        P("replica"),
    )
    out_specs = (P(("replica", "group"), None, "tensor"), P(("replica", "group"), None, None, None))
    return jax.shard_map(local, mesh=mesh, in_specs=in_specs, out_specs=out_specs, check_vma=False)
```

```python
import functools
import math

import jax
import jax.numpy as jnp
from jax import lax
from jax.experimental import pallas as pl
from jax.experimental.pallas import tpu as pltpu
from jax.sharding import PartitionSpec as P

PAGE_ROWS = 128
epsilon = 1e-06
rope_base = 1000000.0
very_negative = -1e30
PARTS = 2
CORES = 2
SHARE = 0.02


def params(mebibytes):
    return pltpu.CompilerParams(vmem_limit_bytes=mebibytes * 1024 * 1024)


def in_hbm(x):
    return pltpu.with_memory_space_constraint(x, pltpu.HBM)


def cost(flops, moved, transcendentals=0):
    return pl.CostEstimate(
        flops=int(flops * SHARE),
        bytes_accessed=int(moved * SHARE),
        transcendentals=int(transcendentals * SHARE),
    )


def hop_order(chips):
    return [0, 1, chips - 1] + list(range(2, chips - 1)) if chips > 2 else list(range(chips))


class Layout:
    def __init__(self, spans, pages, owners):
        self.chips = owners // CORES
        self.span_at = 0
        self.earlier_at = self.span_at + spans
        self.target_at = self.earlier_at + spans
        self.sent_as = self.target_at + spans
        self.home_at = self.sent_as + spans
        self.home = self.home_at + spans
        self.page = self.home + spans
        self.origin = self.page + pages
        self.group_rank = self.origin + owners * spans
        self.tensor_rank = self.group_rank + 1
        self.length = self.tensor_rank + 1


def tables_kernel(lay, spans, pages, ranks, prompt_spans, source, target, page_slot, out, span_of, start_of):
    chips = lay.chips
    group_rank = ranks[0]
    out[lay.group_rank] = group_rank
    out[lay.tensor_rank] = ranks[1]
    for k in range(spans):
        start = jnp.int32(0)
        begin = jnp.int32(0)
        for p in range(prompt_spans.shape[0]):
            start = jnp.where(begin <= k, begin, start)
            begin = begin + prompt_spans[p]
        start_of[k] = start
        span_of[source[k]] = jnp.int32(k)
        out[lay.home + k] = lax.div(source[k], CORES)
    for p in range(pages):
        out[lay.page + page_slot[p]] = jnp.int32(p)
    chip, core = lax.div(group_rank, CORES), lax.rem(group_rank, CORES)
    hops = hop_order(chips)
    for back in range(chips):
        for other in range(CORES):
            at_chip = lax.rem(chip + chips - back, chips)
            at_core = jnp.where(other == 0, core, 1 - core)
            for n, hop in enumerate(hops):
                for flip in range(CORES):
                    from_chip = lax.rem(at_chip + chips - hop, chips)
                    from_core = jnp.where(flip == 0, at_core, 1 - at_core)
                    k = span_of[from_chip * CORES + from_core]
                    place = n * CORES + flip
                    out[lay.origin + (back * CORES + other) * spans + place] = k
                    if back == 0 and other == 0:
                        out[lay.span_at + place] = k
                        out[lay.earlier_at + place] = k - start_of[k]
                        owner = target[k]
                        ahead = lax.rem(lax.div(owner, CORES) + chips - chip, chips)
                        turn = jnp.int32(0)
                        for m, other_hop in enumerate(hops):
                            turn = jnp.where(ahead == other_hop, jnp.int32(m), turn)
                        crossing = jnp.where(lax.rem(owner, CORES) == core, 0, 1)
                        out[lay.target_at + place] = owner
                        out[lay.home_at + place] = from_chip
                        out[lay.sent_as + place] = turn * CORES + crossing


def make_tables(lay, spans, pages, ranks, prompt_spans, source, target, page_slot):
    smem = pl.BlockSpec(memory_space=pltpu.SMEM)
    return pl.pallas_call(
        functools.partial(tables_kernel, lay, spans, pages),
        out_shape=jax.ShapeDtypeStruct((lay.length,), jnp.int32),
        in_specs=[smem] * 5,
        out_specs=smem,
        scratch_shapes=[pltpu.SMEM((spans,), jnp.int32)] * 2,
        name="tables",
    )(ranks, prompt_spans, source, target, page_slot)


def head_norm_rope(u, gain, cosine, sine):
    mean_sq = jnp.mean(u * u, axis=-1, keepdims=True)
    u = u * lax.rsqrt(mean_sq + epsilon) * gain
    half = u.shape[-1] // 2
    return u * cosine + pltpu.roll(u, half, 1) * sine


def half_index(lay, sides, side):
    if sides == 1:
        return lambda t: 0
    if side == 0:
        return lambda t: t[lay.tensor_rank]
    return lambda t: 1 - t[lay.tensor_rank]


def summed_dot(lefts, rights):
    total = None
    for left, right in zip(lefts, rights):
        term = jnp.dot(left[...], right[...], preferred_element_type=jnp.float32)
        total = term if total is None else total + term
    return total


def kv_kernel(sides, blocks, table, *refs):
    refs = list(refs)
    take = lambda n: [refs.pop(0) for _ in range(n)]
    xs = [take(blocks) for _ in range(sides)]
    gains, wks, wvs = take(sides), take(sides), take(sides)
    kgain, cosine, sine = take(3)
    normed, (kv,) = take(sides), take(1)
    head = kgain.shape[1]
    width = sum(x[0].shape[1] for x in xs)

    @pl.when(pl.program_id(0) == 0)
    def _():
        at = 0
        for b in range(blocks):
            wide = [x[b][...].astype(jnp.float32) for x in xs]
            total = sum(jnp.sum(w * w, axis=-1, keepdims=True) for w in wide)
            factor = lax.rsqrt(total / width + epsilon)
            rows = xs[0][b].shape[0]
            for w, gain, to in zip(wide, gains, normed):
                to[at : at + rows] = (w * factor * gain[...].astype(jnp.float32)).astype(
                    jnp.bfloat16
                )
            at += rows

    keys = summed_dot(normed, wks).astype(jnp.bfloat16)
    gains = kgain[...].astype(jnp.float32)
    for h in range(keys.shape[1] // head):
        u = keys[:, h * head : (h + 1) * head].astype(jnp.float32)
        kv[0, :, h * head : (h + 1) * head] = head_norm_rope(
            u, gains, cosine[...], sine[...]
        ).astype(jnp.bfloat16)
    kv[1] = summed_dot(normed, wvs).astype(jnp.bfloat16)


def make_kv(lay, table, xs, gains, wk, wv, kgain, cosine, sine, part):
    sides, blocks = len(xs), len(xs[0])
    rows = sum(x.shape[0] for x in xs[0])
    widths = [x[0].shape[1] for x in xs]
    width, cols = wk.shape
    tile = 256 if cols % 256 == 0 else cols
    head = kgain.shape[1]
    fixed = lambda n, t: (0, 0)
    here = lambda n, t: (part, 0)
    weights = []
    for side in range(sides):
        index = half_index(lay, sides, side)
        weights.append(
            pl.BlockSpec((widths[side], tile), lambda n, t, index=index: (index(t), n))
        )
    return pl.pallas_call(
        functools.partial(kv_kernel, sides, blocks),
        grid_spec=pltpu.PrefetchScalarGridSpec(
            num_scalar_prefetch=1,
            grid=(cols // tile,),
            in_specs=[pl.BlockSpec(x.shape, fixed) for side in xs for x in side]
            + [pl.BlockSpec((1, w), fixed) for w in widths]
            + weights
            + weights
            + [
                pl.BlockSpec((1, head), fixed),
                pl.BlockSpec((rows, head), here),
                pl.BlockSpec((rows, head), here),
            ],
            out_specs=[pl.BlockSpec((rows, w), fixed) for w in widths]
            + [pl.BlockSpec((2, rows, tile), lambda n, t: (0, 0, n))],
        ),
        out_shape=[jax.ShapeDtypeStruct((rows, w), jnp.bfloat16) for w in widths]
        + [jax.ShapeDtypeStruct((2, rows, cols), jnp.bfloat16)],
        compiler_params=params(32),
        cost_estimate=cost(4 * rows * width * cols, 4 * width * cols + 4 * rows * width),
        name="keys_values",
    )(
        table, *[x for side in xs for x in side], *gains,
        *[in_hbm(wk)] * sides, *[in_hbm(wv)] * sides,
        kgain, cosine, sine,
    )


def q_kernel(sides, table, *refs):
    normed, wqs = refs[:sides], refs[sides : 2 * sides]
    qgain, cosine, sine, out = refs[2 * sides :]
    head = qgain.shape[1]
    lin = summed_dot(normed, wqs)
    gains = qgain[...].astype(jnp.float32)
    for h in range(lin.shape[1] // head):
        out[:, h * head : (h + 1) * head] = head_norm_rope(
            lin[:, h * head : (h + 1) * head], gains, cosine[...], sine[...]
        ).astype(jnp.bfloat16)


def make_q(lay, table, normed, wq, qgain, cosine, sine, part):
    sides = len(normed)
    rows = normed[0].shape[0]
    width, cols = wq.shape
    tile = 512 if cols % 512 == 0 else cols
    head = qgain.shape[1]
    fixed = lambda n, t: (0, 0)
    here = lambda n, t: (part, 0)
    weights = []
    for side in range(sides):
        index = half_index(lay, sides, side)
        weights.append(
            pl.BlockSpec(
                (normed[side].shape[1], tile), lambda n, t, index=index: (index(t), n)
            )
        )
    return pl.pallas_call(
        functools.partial(q_kernel, sides),
        grid_spec=pltpu.PrefetchScalarGridSpec(
            num_scalar_prefetch=1,
            grid=(cols // tile,),
            in_specs=[pl.BlockSpec(x.shape, fixed) for x in normed]
            + weights
            + [
                pl.BlockSpec((1, head), fixed),
                pl.BlockSpec((rows, head), here),
                pl.BlockSpec((rows, head), here),
            ],
            out_specs=pl.BlockSpec((rows, tile), lambda n, t: (0, n)),
        ),
        out_shape=jax.ShapeDtypeStruct((rows, cols), jnp.bfloat16),
        compiler_params=params(24),
        cost_estimate=cost(2 * rows * width * cols, 2 * width * cols + 2 * rows * (width + cols)),
        name="queries",
    )(table, *normed, *[in_hbm(wq)] * sides, qgain, cosine, sine)


def attention_kernel(lay, spans, most, per_kv, head, owners, pages_each, part, last, table, *refs):
    refs = list(refs)
    take = lambda n: [refs.pop(0) for _ in range(n)]
    q_refs, kv_refs = take(PARTS), take(owners)
    before = take(3) if part else None
    if last:
        out, pages, keys, values = refs
    else:
        summed_out, state_out, pages, keys, values = refs
    chips, hops = lay.chips, hop_order(lay.chips)
    here, rows = kv_refs[0].shape[1], kv_refs[0].shape[2]
    group_rank = table[lay.group_rank]
    chip, core = lax.div(group_rank, CORES), lax.rem(group_rank, CORES)
    for o in range(owners):
        at_core = core if o % CORES == 0 else 1 - core
        for i in range(here):
            k = table[lay.origin + o * spans + part * here + i]
            at = pl.ds(pl.multiple_of(at_core * rows, rows), rows)
            keys[k, i // CORES, at] = kv_refs[o][0, i]
            values[k, i // CORES, at] = kv_refs[o][1, i]

    turns = here // CORES
    for i in range(pages_each):
        page = table[lay.page + group_rank * pages_each + i]
        k = lax.div(page, pages_each)
        hop = lax.rem(lax.rem(page, pages_each) + chips - table[lay.home + k], chips)
        if part:
            pages[i] = before[2][i]
        for j in range(turns):

            @pl.when(hop == hops[part * turns + j])
            def _(i=i, j=j, k=k):
                pages[i, 0] = keys[k, j]
                pages[i, 1] = values[k, j]

    scale = (1.0 / math.sqrt(head)) * math.log2(math.e)
    q_rows, both, k_rows = per_kv * rows, CORES * rows, turns * CORES * rows
    row = lax.broadcasted_iota(jnp.int32, (q_rows, k_rows), 0)
    col = lax.broadcasted_iota(jnp.int32, (q_rows, k_rows), 1)
    q_at = group_rank * rows + row % rows
    lane = lax.broadcasted_iota(jnp.int32, (q_rows, head), 1)

    def one_place(p, i, carry):
        place = p * here + i
        k = table[lay.span_at + place]
        earlier = table[lay.earlier_at + place]
        home = table[lay.home_at + place]
        queries = jnp.concatenate(
            [q_refs[p][i, :, g * head : (g + 1) * head] for g in range(per_kv)], axis=0
        )
        k_at = col
        for j in range(turns):
            begin = lax.rem(home + hops[part * turns + j], chips) * both
            k_at = jnp.where(col // both == j, col + (begin - j * both), k_at)
        allowed = k_at <= q_at

        def with_earlier(count):
            scores = []
            for back in range(count + 1):
                s = lax.dot_general(
                    queries, keys[k - back].reshape(k_rows, head), (((1,), (1,)), ((), ())),
                    preferred_element_type=jnp.float32,
                )
                if back == 0:
                    s = jnp.where(allowed, s, very_negative)
                scores.append(s)
            best = scores[0]
            for s in scores[1:]:
                best = jnp.maximum(best, s)
            best = jnp.max(best, axis=-1, keepdims=True)
            total = None
            summed = None
            if part:
                state = before[1][0, place]
                best = jnp.maximum(best, state[:, 0:1])
                keep = jnp.exp2((state[:, 0:1] - best) * scale)
                total = state[:, 1:2] * keep
                summed = before[0][0, place] * keep
            for back, s in enumerate(scores):
                w = jnp.exp2((s - best) * scale)
                part_total = jnp.sum(w, axis=-1, keepdims=True)
                term = jnp.dot(
                    w.astype(jnp.bfloat16), values[k - back].reshape(k_rows, head),
                    preferred_element_type=jnp.float32,
                )
                total = part_total if total is None else total + part_total
                summed = term if summed is None else summed + term
            if not last:
                summed_out[0, place] = summed
                state_out[0, place] = jnp.where(lane == 0, best, total)
                return
            result = (summed / total).astype(jnp.bfloat16)
            for g in range(per_kv):
                out[place, :, g * head : (g + 1) * head] = result[g * rows : (g + 1) * rows]

        for count in range(most):
            pl.when(earlier == count)(functools.partial(with_earlier, count))
        return carry

    for p in range(PARTS):
        lax.fori_loop(0, here, functools.partial(one_place, p), 0)


def make_attention(lay, most, table, queries, gathered, per_kv, head, pages_each, first, count, part, before):
    here, rows, cols = queries[0].shape
    spans, last = here * PARTS, part == PARTS - 1
    owners = len(gathered)
    q_spec = pl.BlockSpec((here, rows, per_kv * head), lambda h, t: (0, 0, first + h))
    kv_spec = pl.BlockSpec((2, here, rows, head), lambda h, t: (0, 0, 0, first + h))
    state_spec = pl.BlockSpec((1, spans, per_kv * rows, head), lambda h, t: (h, 0, 0, 0))
    page_spec = pl.BlockSpec((pages_each, 2, PAGE_ROWS, head), lambda h, t: (0, 0, 0, h))
    state_shape = jax.ShapeDtypeStruct((count, spans, per_kv * rows, head), jnp.float32)
    page_shape = jax.ShapeDtypeStruct((pages_each, 2, PAGE_ROWS, count * head), jnp.bfloat16)
    out_spec = pl.BlockSpec((spans, rows, per_kv * head), lambda h, t: (0, 0, h))
    out_shape = jax.ShapeDtypeStruct((spans, rows, count * per_kv * head), jnp.bfloat16)
    pairs = 2.2 * spans * rows * owners * here * rows // CORES * per_kv * count
    return pl.pallas_call(
        functools.partial(
            attention_kernel, lay, spans, most, per_kv, head, owners, pages_each, part, last
        ),
        grid_spec=pltpu.PrefetchScalarGridSpec(
            num_scalar_prefetch=1,
            grid=(count,),
            in_specs=[q_spec] * PARTS + [kv_spec] * owners
            + ([state_spec, state_spec, page_spec] if part else []),
            out_specs=[out_spec, page_spec] if last else [state_spec, state_spec, page_spec],
            scratch_shapes=[
                pltpu.VMEM((spans, here // CORES, CORES * rows, head), jnp.bfloat16)
            ] * 2,
        ),
        out_shape=[out_shape, page_shape] if last else [state_shape, state_shape, page_shape],
        compiler_params=params(24),
        cost_estimate=cost(4 * pairs * head, 4 * spans * rows * cols, pairs),
        name="attention",
    )(table, *queries, *gathered, *before)


def project_kernel(pieces, follows, tile, table, *refs):
    attended, wo, outs = refs[:pieces], refs[pieces], refs[pieces + 1 + follows :]
    total, at = None, 0
    for piece in attended:
        depth = piece.shape[1]
        term = jnp.dot(piece[...], wo[at : at + depth], preferred_element_type=jnp.float32)
        total = term if total is None else total + term
        at += depth
    total = total.astype(jnp.bfloat16)
    step = 0
    for out in outs:
        for at in range(0, out.shape[1], tile):

            @pl.when(pl.program_id(0) == step)
            def _(out=out, at=at):
                out[:, at : at + tile] = total

            step += 1


def make_projection(lay, table, attended, wo, tile, first, widths, name, follows=()):
    rows = attended[0].shape[0]
    depth = wo.shape[0]
    count = sum(widths)
    return pl.pallas_call(
        functools.partial(project_kernel, len(attended), len(follows), tile),
        grid_spec=pltpu.PrefetchScalarGridSpec(
            num_scalar_prefetch=1,
            grid=(count,),
            in_specs=[pl.BlockSpec(x.shape, lambda n, t: (0, 0)) for x in attended]
            + [pl.BlockSpec((depth, tile), lambda n, t: (0, first(t[lay.tensor_rank]) + n))]
            + [pl.BlockSpec(memory_space=pl.ANY)] * len(follows),
            out_specs=[pl.BlockSpec((rows, w * tile), lambda n, t: (0, 0)) for w in widths],
        ),
        out_shape=[jax.ShapeDtypeStruct((rows, w * tile), jnp.bfloat16) for w in widths],
        compiler_params=params(20),
        cost_estimate=cost(
            2 * rows * depth * count * tile, 2 * (rows * depth + (rows + depth) * count * tile)
        ),
        name=name,
    )(table, *attended, in_hbm(wo), *follows)


def add_kernel(lay, blocks, table, *refs):
    x_refs, own, received = refs[:blocks], refs[blocks], refs[blocks + 1]
    outs, moved = refs[blocks + 2 : -1], refs[-1]
    rows = moved.shape[1]
    place = 0
    for x in x_refs:
        for at in range(0, x.shape[0], rows):
            summed = own[place].astype(jnp.float32) + received[place].astype(jnp.float32)
            moved[table[lay.sent_as + place]] = (
                x[at : at + rows].astype(jnp.float32) + summed
            ).astype(jnp.bfloat16)
            place += 1
    for n, out in enumerate(outs):
        for flip in range(CORES):
            out[flip] = moved[n * CORES + flip]


def make_sum(lay, table, arrived, own, received, first):
    spans, rows, cols = received.shape
    chunk = first // cols
    whole = lambda n, t: (0, 0, 0)
    return pl.pallas_call(
        functools.partial(add_kernel, lay, len(arrived)),
        grid_spec=pltpu.PrefetchScalarGridSpec(
            num_scalar_prefetch=1,
            grid=(1,),
            in_specs=[pl.BlockSpec((x.shape[0], cols), lambda n, t: (0, chunk)) for x in arrived]
            + [pl.BlockSpec((spans, rows, cols), whole)] * 2,
            out_specs=[pl.BlockSpec((CORES, rows, cols), whole)] * lay.chips,
            scratch_shapes=[pltpu.VMEM((spans, rows, cols), jnp.bfloat16)],
        ),
        out_shape=[jax.ShapeDtypeStruct((CORES, rows, cols), jnp.bfloat16)] * lay.chips,
        compiler_params=params(12),
        cost_estimate=cost(3 * spans * rows * cols, 8 * spans * rows * cols),
        name="residual",
    )(table, *arrived, own, received)


def place_kernel(lay, table, *refs):
    same, swapped, out = refs[: lay.chips], refs[lay.chips], refs[-1]
    rows = swapped.shape[1]
    group_rank = table[lay.group_rank]
    chip, core = lax.div(group_rank, CORES), lax.rem(group_rank, CORES)
    for n, hop in enumerate(hop_order(lay.chips)):
        owner = lax.rem(chip + lay.chips - hop, lay.chips) * CORES
        for block, at_core in ((same[n][0], core), (swapped[n], 1 - core)):
            at = pl.multiple_of((owner + at_core) * rows, rows)
            out[pl.ds(at, rows)] = block


def make_placed(lay, table, same, swapped, first, cols, whole):
    chips, rows, tile = swapped.shape
    chunk = first // tile
    return pl.pallas_call(
        functools.partial(place_kernel, lay),
        grid_spec=pltpu.PrefetchScalarGridSpec(
            num_scalar_prefetch=1,
            grid=(1,),
            in_specs=[pl.BlockSpec((CORES, rows, tile), lambda n, t: (0, 0, 0))] * chips
            + [pl.BlockSpec((chips, rows, tile), lambda n, t: (0, 0, 0))]
            + [pl.BlockSpec(memory_space=pl.ANY)] * len(whole),
            out_specs=pl.BlockSpec((chips * CORES * rows, tile), lambda n, t: (0, chunk)),
        ),
        out_shape=jax.ShapeDtypeStruct((chips * CORES * rows, cols), jnp.bfloat16),
        input_output_aliases={chips + 2: 0} if whole else {},
        compiler_params=params(12),
        cost_estimate=cost(0, 4 * chips * CORES * rows * tile),
        name="placed",
    )(table, *same, swapped, *whole)


def rope_tables(earlier, span_len, first_row, rows, head):
    half = head // 2
    freqs = jnp.power(
        jnp.float32(rope_base), -jnp.arange(half, dtype=jnp.float32) * 2.0 / head
    )
    at = earlier[:, None] * span_len + first_row + jnp.arange(rows, dtype=jnp.int32)[None, :]
    angles = at.reshape(-1).astype(jnp.float32)[:, None] * freqs[None, :]
    cosine, sine = jnp.cos(angles), jnp.sin(angles)
    return (
        jnp.concatenate([cosine, cosine], axis=1),
        jnp.concatenate([-sine, sine], axis=1),
    )


def after(x, done):
    return lax.optimization_barrier((x, done))[0]


def shift(x, owners, hop, flip):
    chips = owners // CORES
    pairs = [
        (z * CORES + c, (z + hop) % chips * CORES + (c ^ flip))
        for z in range(chips)
        for c in range(CORES)
    ]
    return lax.ppermute(x, "group", pairs)


def local(
    hidden_in, ln_gain, wq, wk, wv, q_gain, key_norm_gain, wo,
    prompt_spans, span_source, span_target, page_slot,
):
    _, span_len, cols = hidden_in.shape
    tensor_size = lax.axis_size("tensor")
    owners = lax.axis_size("group")
    tensor_rank = lax.axis_index("tensor")
    group_rank = lax.axis_index("group")
    chips = owners // CORES
    head = q_gain.shape[0]
    rows = span_len // owners
    pages_each = span_len // PAGE_ROWS
    spans = span_source.shape[0]
    here = spans // PARTS
    most = min(spans - (prompt_spans.shape[0] - 1), spans // 2)
    kv_cols = wk.shape[1]
    paired = tensor_size == 2
    swap = [(0, 1), (1, 0)]
    lay = Layout(spans, spans * pages_each, owners)

    if kv_cols < head:
        share = head // kv_cols
        sets = [list(range(i, i + share)) for i in range(0, tensor_size, share)]
        wk, wv = [
            lax.all_gather(w, "tensor", axis=1, tiled=True, axis_index_groups=sets)
            for w in (wk, wv)
        ]
    per_kv = wq.shape[1] // max(head, wk.shape[1])

    chip, core = group_rank // CORES, group_rank % CORES
    split = hidden_in.reshape(owners, rows, cols)

    def rows_for(hop, flip):
        to = lax.rem(chip + hop, chips) * CORES + lax.rem(core + flip, CORES)
        return lax.dynamic_index_in_dim(split, to, 0, keepdims=False)

    cross = lambda x: lax.ppermute(x, "tensor", swap)

    hops = hop_order(chips)
    paired_hops = hops[2:]
    near = [rows_for(hop, flip) for hop in hops[1:2] for flip in range(CORES)]
    near = [shift(x, owners, hops[1], flip) for flip, x in enumerate(near)]
    swapped = shift(
        jnp.stack([rows_for(hop, 1) for hop in hops[:1] + paired_hops]), owners, 0, 1
    )
    arrived = [rows_for(0, 0), swapped[0]] + near
    moves = []
    for n, hop in enumerate(paired_hops):
        pair = [rows_for(hop, 0), swapped[1 + n]]
        if n < len(paired_hops) - 1:
            moves.append((hop, jnp.concatenate(pair)))
        else:
            moves += [(hop, block) for block in pair]

    ranks = jnp.stack([group_rank, tensor_rank]).astype(jnp.int32)
    table = make_tables(
        lay, spans, spans * pages_each, ranks, prompt_spans, span_source, span_target, page_slot
    )
    earlier = table[lay.earlier_at : lay.earlier_at + spans]
    cosine, sine = rope_tables(earlier, span_len, group_rank * rows, rows, head)

    crossed = [cross(x) for x in arrived] if paired else []
    if paired:
        gain = ln_gain[None]
        gains = [gain, cross(after(gain, swapped))]
    else:
        gains = [lax.all_gather(ln_gain, "tensor", axis=0, tiled=True)[None]]

    kvs, norms = [], []

    def make_part(own_rows, crossed_rows, done):
        if paired:
            xs = [own_rows, crossed_rows]
        else:
            xs = [[lax.all_gather(jnp.concatenate(own_rows), "tensor", axis=1, tiled=True)]]
        kgain = after(key_norm_gain[None], done)
        *normed, kv = make_kv(lay, table, xs, gains, wk, wv, kgain, cosine, sine, len(kvs))
        kvs.append([kv.reshape(2, here, rows, kv.shape[2])])
        norms.append(normed)

    def one_back(p, done=()):
        kvs[p].append(shift(after(kvs[p][-1], done), owners, 1, 0))

    begun = len(arrived)
    for n, (hop, block) in enumerate(moves):
        if n == len(moves) - 1:
            make_part(arrived[:begun], crossed[:begun], (arrived[begun:], crossed[begun : begun + 1]))
        if paired:
            landed = arrived[-1:] if n else near
            matching = crossed[2 * n : 2 * n + 2] if n < 2 else crossed[n + 2]
            block = after(block, (landed, matching, gains))
        block = shift(block, owners, hop, 0)
        arrived.append(block)
        if paired:
            crossed.append(cross(after(block, kvs[0][0]) if kvs else block))
    make_part(arrived[begun:], crossed[begun:], ())
    one_back(0)
    one_back(0)
    one_back(1)

    queries, done = [], kvs[1][0]
    for p in range(PARTS):
        made = make_q(
            lay, table, norms[p], wq, after(q_gain[None], done), cosine, sine, p
        )
        queries.append(made.reshape(here, rows, made.shape[1]))
        done = (queries[-1], kvs[0][-1], kvs[1][-1])

    own_kv = wk.shape[1] // head
    sets = [own_kv // 2, own_kv - own_kv // 2] if own_kv > 1 else [own_kv]
    states = [()] * len(sets)
    for p in range(PARTS):
        while len(kvs[p]) < chips:
            one_back(p, queries if p and len(kvs[p]) == chips - 1 else queries[0])
        gathered = []
        for kv in kvs[p]:
            gathered.append(kv)
            if kv is kvs[p][-1]:
                kv = after(kv, states if p else queries)
            gathered.append(shift(kv, owners, 0, 1))
        states = [
            make_attention(
                lay, most, table, queries, gathered, per_kv, head, pages_each,
                sum(sets[:n]), count, p, states[n],
            )
            for n, count in enumerate(sets)
        ]
    attended = [made.reshape(spans * rows, -1) for made, _ in states]
    pages = [cut for _, cut in states]

    if paired:
        tile = 512 if cols % 512 == 0 else cols
        tiles = cols // tile
        widths = [2, 2, 1] if tiles == 5 else [tiles]
        others = [cross(pages[0])]
        project = functools.partial(make_projection, lay, table, attended, wo, tile)
        send = project(lambda r: (1 - r) * tiles, widths[:1], "send_part", (others[0],))
        if widths[1:]:
            send += project(
                lambda r: (1 - r) * tiles + widths[0], widths[1:], "send_part", (send[0],)
            )
        own = project(lambda r: r * tiles, widths, "own_part", (send[-1],))
        whole, received, landed, first = (), [], [], 0
        for n, sent in enumerate(send):
            if n:
                sent = after(sent, (received[-1], own, landed[-2:-1]))
            received.append(cross(sent))
            moved = make_sum(
                lay, table, arrived, own[n].reshape(spans, rows, -1),
                received[-1].reshape(spans, rows, -1), first,
            )
            same = [
                shift(x, owners, hop, 0) if hop else x
                for hop, x in zip(hop_order(chips), moved)
            ]
            landed.append(same)
            swapped = jnp.concatenate([x[1:] for x in same])
            if n == len(send) - 1:
                for cut in pages[1:]:
                    others.append(cross(after(cut, received[-1])))
                low = [jnp.where(tensor_rank == 0, a, b) for a, b in zip(pages, others)]
                high = [jnp.where(tensor_rank == 0, b, a) for a, b in zip(pages, others)]
                cache = jnp.concatenate(low + high, axis=3)
                swapped = after(swapped, (cache, whole))
            swapped = shift(swapped, owners, 0, 1)
            whole = (make_placed(lay, table, same, swapped, first, cols, whole),)
            first += sent.shape[1]
        mixed = whole[0].reshape(1, span_len, cols)
    else:
        pages = jnp.concatenate(pages, axis=3)
        attended = jnp.concatenate(attended, axis=1)
        if kv_cols < head:
            pages = lax.dynamic_slice_in_dim(
                pages, lax.rem(tensor_rank, head // kv_cols) * kv_cols, kv_cols, 3
            )
        cache = lax.all_gather(pages, "tensor", axis=3, tiled=True)
        partial = jnp.dot(attended, wo, preferred_element_type=jnp.float32)
        summed = lax.psum_scatter(
            partial.astype(jnp.bfloat16), "tensor", scatter_dimension=1, tiled=True
        )
        summed = summed.reshape(spans, rows, cols).astype(jnp.float32)
        x = jnp.concatenate(arrived).reshape(spans, rows, cols).astype(jnp.float32)
        moved = (x + summed).astype(jnp.bfloat16)
        targets = table[lay.target_at : lay.target_at + spans]
        moved = jnp.zeros_like(moved).at[targets].set(moved, unique_indices=True)
        moved = lax.all_to_all(moved, "group", split_axis=0, concat_axis=0, tiled=True)
        mixed = moved.reshape(1, span_len, cols)
    return (mixed, cache)


def solution(mesh):
    in_specs = (
        P(("replica", "group"), None, "tensor"),
        P("tensor"),
        P(None, "tensor"),
        P(None, "tensor"),
        P(None, "tensor"),
        P(),
        P(),
        P("tensor", None),
        P("replica"),
        P("replica"),
        P("replica"),
        P("replica"),
    )
    out_specs = (P(("replica", "group"), None, "tensor"), P(("replica", "group"), None, None, None))
    return jax.shard_map(local, mesh=mesh, in_specs=in_specs, out_specs=out_specs, check_vma=False)
```

```python
import functools
import math

import jax
import jax.numpy as jnp
from jax import lax
from jax.experimental import pallas as pl
from jax.experimental.pallas import tpu as pltpu
from jax.sharding import PartitionSpec as P

PAGE_ROWS = 128
epsilon = 1e-06
rope_base = 1000000.0
very_negative = -1e30
PARTS = 2
CORES = 2
SHARE = 0.02


def params(mebibytes):
    return pltpu.CompilerParams(vmem_limit_bytes=mebibytes * 1024 * 1024)


def in_hbm(x):
    return pltpu.with_memory_space_constraint(x, pltpu.HBM)


def cost(flops, moved, transcendentals=0):
    return pl.CostEstimate(
        flops=int(flops * SHARE),
        bytes_accessed=int(moved * SHARE),
        transcendentals=int(transcendentals * SHARE),
    )


def hop_order(chips):
    return [0, 1, chips - 1] + list(range(2, chips - 1)) if chips > 2 else list(range(chips))


class Layout:
    def __init__(self, spans, pages, owners):
        self.chips = owners // CORES
        self.span_at = 0
        self.earlier_at = self.span_at + spans
        self.target_at = self.earlier_at + spans
        self.sent_as = self.target_at + spans
        self.page = self.sent_as + spans
        self.origin = self.page + pages
        self.group_rank = self.origin + owners * spans
        self.tensor_rank = self.group_rank + 1
        self.length = self.tensor_rank + 1


def tables_kernel(lay, spans, pages, ranks, prompt_spans, source, target, page_slot, out, span_of, start_of):
    chips = lay.chips
    group_rank = ranks[0]
    out[lay.group_rank] = group_rank
    out[lay.tensor_rank] = ranks[1]
    for k in range(spans):
        start = jnp.int32(0)
        begin = jnp.int32(0)
        for p in range(prompt_spans.shape[0]):
            start = jnp.where(begin <= k, begin, start)
            begin = begin + prompt_spans[p]
        start_of[k] = start
        span_of[source[k]] = jnp.int32(k)
    for p in range(pages):
        out[lay.page + page_slot[p]] = jnp.int32(p)
    chip, core = lax.div(group_rank, CORES), lax.rem(group_rank, CORES)
    hops = hop_order(chips)
    for back in range(chips):
        for other in range(CORES):
            at_chip = lax.rem(chip + chips - back, chips)
            at_core = jnp.where(other == 0, core, 1 - core)
            for n, hop in enumerate(hops):
                for flip in range(CORES):
                    from_chip = lax.rem(at_chip + chips - hop, chips)
                    from_core = jnp.where(flip == 0, at_core, 1 - at_core)
                    k = span_of[from_chip * CORES + from_core]
                    place = n * CORES + flip
                    out[lay.origin + (back * CORES + other) * spans + place] = k
                    if back == 0 and other == 0:
                        out[lay.span_at + place] = k
                        out[lay.earlier_at + place] = k - start_of[k]
                        owner = target[k]
                        ahead = lax.rem(lax.div(owner, CORES) + chips - chip, chips)
                        turn = jnp.int32(0)
                        for m, other_hop in enumerate(hops):
                            turn = jnp.where(ahead == other_hop, jnp.int32(m), turn)
                        crossing = jnp.where(lax.rem(owner, CORES) == core, 0, 1)
                        out[lay.target_at + place] = owner
                        out[lay.sent_as + place] = turn * CORES + crossing


def make_tables(lay, spans, pages, ranks, prompt_spans, source, target, page_slot):
    smem = pl.BlockSpec(memory_space=pltpu.SMEM)
    return pl.pallas_call(
        functools.partial(tables_kernel, lay, spans, pages),
        out_shape=jax.ShapeDtypeStruct((lay.length,), jnp.int32),
        in_specs=[smem] * 5,
        out_specs=smem,
        scratch_shapes=[pltpu.SMEM((spans,), jnp.int32)] * 2,
        compiler_params=params(4),
        name="tables",
    )(ranks, prompt_spans, source, target, page_slot)


def head_norm_rope(u, gain, cosine, sine):
    mean_sq = jnp.mean(u * u, axis=-1, keepdims=True)
    u = u * lax.rsqrt(mean_sq + epsilon) * gain
    half = u.shape[-1] // 2
    return u * cosine + pltpu.roll(u, half, 1) * sine


def half_index(lay, sides, side):
    if sides == 1:
        return lambda t: 0
    if side == 0:
        return lambda t: t[lay.tensor_rank]
    return lambda t: 1 - t[lay.tensor_rank]


def summed_dot(lefts, rights):
    total = None
    for left, right in zip(lefts, rights):
        term = jnp.dot(left[...], right[...], preferred_element_type=jnp.float32)
        total = term if total is None else total + term
    return total


def kv_kernel(sides, blocks, table, *refs):
    refs = list(refs)
    take = lambda n: [refs.pop(0) for _ in range(n)]
    xs = [take(blocks) for _ in range(sides)]
    gains, wks, wvs = take(sides), take(sides), take(sides)
    kgain, cosine, sine = take(3)
    normed, (kv,) = take(sides), take(1)
    head = kgain.shape[1]
    width = sum(x[0].shape[1] for x in xs)

    @pl.when(pl.program_id(0) == 0)
    def _():
        at = 0
        for b in range(blocks):
            wide = [x[b][...].astype(jnp.float32) for x in xs]
            total = sum(jnp.sum(w * w, axis=-1, keepdims=True) for w in wide)
            factor = lax.rsqrt(total / width + epsilon)
            rows = xs[0][b].shape[0]
            for w, gain, to in zip(wide, gains, normed):
                to[at : at + rows] = (w * factor * gain[...].astype(jnp.float32)).astype(
                    jnp.bfloat16
                )
            at += rows

    keys = summed_dot(normed, wks).astype(jnp.bfloat16)
    gains = kgain[...].astype(jnp.float32)
    for h in range(keys.shape[1] // head):
        u = keys[:, h * head : (h + 1) * head].astype(jnp.float32)
        kv[0, :, h * head : (h + 1) * head] = head_norm_rope(
            u, gains, cosine[...], sine[...]
        ).astype(jnp.bfloat16)
    kv[1] = summed_dot(normed, wvs).astype(jnp.bfloat16)


def make_kv(lay, table, xs, gains, wk, wv, kgain, cosine, sine, part):
    sides, blocks = len(xs), len(xs[0])
    rows = sum(x.shape[0] for x in xs[0])
    widths = [x[0].shape[1] for x in xs]
    width, cols = wk.shape
    tile = 256 if cols % 256 == 0 else cols
    head = kgain.shape[1]
    fixed = lambda n, t: (0, 0)
    here = lambda n, t: (part, 0)
    weights = []
    for side in range(sides):
        index = half_index(lay, sides, side)
        weights.append(
            pl.BlockSpec((widths[side], tile), lambda n, t, index=index: (index(t), n))
        )
    return pl.pallas_call(
        functools.partial(kv_kernel, sides, blocks),
        grid_spec=pltpu.PrefetchScalarGridSpec(
            num_scalar_prefetch=1,
            grid=(cols // tile,),
            in_specs=[pl.BlockSpec(x.shape, fixed) for side in xs for x in side]
            + [pl.BlockSpec((1, w), fixed) for w in widths]
            + weights
            + weights
            + [
                pl.BlockSpec((1, head), fixed),
                pl.BlockSpec((rows, head), here),
                pl.BlockSpec((rows, head), here),
            ],
            out_specs=[pl.BlockSpec((rows, w), fixed) for w in widths]
            + [pl.BlockSpec((2, rows, tile), lambda n, t: (0, 0, n))],
        ),
        out_shape=[jax.ShapeDtypeStruct((rows, w), jnp.bfloat16) for w in widths]
        + [jax.ShapeDtypeStruct((2, rows, cols), jnp.bfloat16)],
        compiler_params=params(32),
        cost_estimate=cost(4 * rows * width * cols, 4 * width * cols + 4 * rows * width),
        name="keys_values",
    )(
        table, *[x for side in xs for x in side], *gains,
        *[in_hbm(wk)] * sides, *[in_hbm(wv)] * sides,
        kgain, cosine, sine,
    )


def q_kernel(sides, table, *refs):
    normed, wqs = refs[:sides], refs[sides : 2 * sides]
    qgain, cosine, sine, out = refs[2 * sides :]
    head = qgain.shape[1]
    lin = summed_dot(normed, wqs)
    gains = qgain[...].astype(jnp.float32)
    for h in range(lin.shape[1] // head):
        out[:, h * head : (h + 1) * head] = head_norm_rope(
            lin[:, h * head : (h + 1) * head], gains, cosine[...], sine[...]
        ).astype(jnp.bfloat16)


def make_q(lay, table, normed, wq, qgain, cosine, sine, part):
    sides = len(normed)
    rows = normed[0].shape[0]
    width, cols = wq.shape
    tile = 512 if cols % 512 == 0 else cols
    head = qgain.shape[1]
    fixed = lambda n, t: (0, 0)
    here = lambda n, t: (part, 0)
    weights = []
    for side in range(sides):
        index = half_index(lay, sides, side)
        weights.append(
            pl.BlockSpec(
                (normed[side].shape[1], tile), lambda n, t, index=index: (index(t), n)
            )
        )
    return pl.pallas_call(
        functools.partial(q_kernel, sides),
        grid_spec=pltpu.PrefetchScalarGridSpec(
            num_scalar_prefetch=1,
            grid=(cols // tile,),
            in_specs=[pl.BlockSpec(x.shape, fixed) for x in normed]
            + weights
            + [
                pl.BlockSpec((1, head), fixed),
                pl.BlockSpec((rows, head), here),
                pl.BlockSpec((rows, head), here),
            ],
            out_specs=pl.BlockSpec((rows, tile), lambda n, t: (0, n)),
        ),
        out_shape=jax.ShapeDtypeStruct((rows, cols), jnp.bfloat16),
        compiler_params=params(24),
        cost_estimate=cost(2 * rows * width * cols, 2 * width * cols + 2 * rows * (width + cols)),
        name="queries",
    )(table, *normed, *[in_hbm(wq)] * sides, qgain, cosine, sine)


def attention_kernel(lay, spans, most, per_kv, head, beside, owners, pages_each, table, *refs):
    q_refs = refs[:PARTS]
    kv_refs = refs[PARTS : PARTS + owners * PARTS]
    out, pages, keys, values = refs[PARTS + owners * PARTS :]
    chips = lay.chips
    here, rows = kv_refs[0].shape[1], kv_refs[0].shape[2]
    group_rank = table[lay.group_rank]
    chip, core = lax.div(group_rank, CORES), lax.rem(group_rank, CORES)
    heads = range(beside)
    for o in range(owners):
        back, other = o // CORES, o % CORES
        owner = lax.rem(chip + chips - back, chips) * CORES + (core if other == 0 else 1 - core)
        at = pl.ds(pl.multiple_of(owner * rows, rows), rows)
        for p in range(PARTS):
            for i in range(here):
                k = table[lay.origin + o * spans + p * here + i]
                for h in heads:
                    lanes = slice(h * head, (h + 1) * head)
                    keys[h, k, at] = kv_refs[o * PARTS + p][0, i, :, lanes]
                    values[h, k, at] = kv_refs[o * PARTS + p][1, i, :, lanes]

    for i in range(pages_each):
        page = table[lay.page + group_rank * pages_each + i]
        k = lax.div(page, pages_each)
        at = pl.ds(pl.multiple_of(lax.rem(page, pages_each) * PAGE_ROWS, PAGE_ROWS), PAGE_ROWS)
        for h in heads:
            lanes = slice(h * head, (h + 1) * head)
            pages[i, 0, :, lanes] = keys[h, k, at]
            pages[i, 1, :, lanes] = values[h, k, at]

    scale = (1.0 / math.sqrt(head)) * math.log2(math.e)
    q_rows, k_rows = per_kv * rows, owners * rows
    row = lax.broadcasted_iota(jnp.int32, (q_rows, k_rows), 0)
    col = lax.broadcasted_iota(jnp.int32, (q_rows, k_rows), 1)
    allowed = col <= group_rank * rows + row % rows

    def one_place(p, i, carry):
        k = table[lay.span_at + p * here + i]
        earlier = table[lay.earlier_at + p * here + i]

        def with_earlier(count):
            scores = [[] for _ in heads]
            for h in heads:
                queries = jnp.concatenate(
                    [
                        q_refs[p][i, :, (h * per_kv + g) * head : (h * per_kv + g + 1) * head]
                        for g in range(per_kv)
                    ],
                    axis=0,
                )
                for back in range(count + 1):
                    s = lax.dot_general(
                        queries, keys[h, k - back], (((1,), (1,)), ((), ())),
                        preferred_element_type=jnp.float32,
                    )
                    if back == 0:
                        s = jnp.where(allowed, s, very_negative)
                    scores[h].append(s)
            for h in heads:
                best = functools.reduce(jnp.maximum, scores[h])
                best = jnp.max(best, axis=-1, keepdims=True)
                shifted = best * scale
                weights = [jnp.exp2(s * scale - shifted) for s in scores[h]]
                total = jnp.sum(
                    functools.reduce(lambda a, b: a + b, weights), axis=-1, keepdims=True
                )
                summed = None
                for back, w in enumerate(weights):
                    term = jnp.dot(
                        w.astype(jnp.bfloat16), values[h, k - back],
                        preferred_element_type=jnp.float32,
                    )
                    summed = term if summed is None else summed + term
                result = (summed / total).astype(jnp.bfloat16)
                for g in range(per_kv):
                    at = (h * per_kv + g) * head
                    out[p * here + i, :, at : at + head] = result[g * rows : (g + 1) * rows]

        for count in range(most):
            pl.when(earlier == count)(functools.partial(with_earlier, count))
        return carry

    for p in range(PARTS):
        lax.fori_loop(0, here, functools.partial(one_place, p), 0)


def make_attention(lay, most, table, queries, gathered, per_kv, head, pages_each, first, count):
    here, rows, cols = queries[0].shape
    spans = here * PARTS
    owners = len(gathered)
    at = first // count
    q_spec = pl.BlockSpec((here, rows, count * per_kv * head), lambda h, t: (0, 0, at + h))
    kv_spec = pl.BlockSpec((2, here, rows, count * head), lambda h, t: (0, 0, 0, at + h))
    flat = [x for origin in gathered for x in origin]
    all_rows = spans * rows
    pairs = 2.2 * all_rows * owners * rows * per_kv * count
    return pl.pallas_call(
        functools.partial(
            attention_kernel, lay, spans, most, per_kv, head, count, owners, pages_each
        ),
        grid_spec=pltpu.PrefetchScalarGridSpec(
            num_scalar_prefetch=1,
            grid=(1,),
            in_specs=[q_spec] * PARTS + [kv_spec] * len(flat),
            out_specs=[
                pl.BlockSpec((spans, rows, count * per_kv * head), lambda h, t: (0, 0, h)),
                pl.BlockSpec((pages_each, 2, PAGE_ROWS, count * head), lambda h, t: (0, 0, 0, h)),
            ],
            scratch_shapes=[pltpu.VMEM((count, spans, owners * rows, head), jnp.bfloat16)] * 2,
        ),
        out_shape=[
            jax.ShapeDtypeStruct((spans, rows, count * per_kv * head), jnp.bfloat16),
            jax.ShapeDtypeStruct((pages_each, 2, PAGE_ROWS, count * head), jnp.bfloat16),
        ],
        compiler_params=params(32),
        cost_estimate=cost(
            4 * pairs * head, 4 * all_rows * cols + 2 * len(flat) * flat[0].size, pairs
        ),
        name="attention",
    )(table, *queries, *flat)


def project_kernel(pieces, follows, tile, table, *refs):
    attended, wo, outs = refs[:pieces], refs[pieces], refs[pieces + 1 + follows :]
    total, at = None, 0
    for piece in attended:
        depth = piece.shape[1]
        term = jnp.dot(piece[...], wo[at : at + depth], preferred_element_type=jnp.float32)
        total = term if total is None else total + term
        at += depth
    total = total.astype(jnp.bfloat16)
    step = 0
    for out in outs:
        for at in range(0, out.shape[1], tile):

            @pl.when(pl.program_id(0) == step)
            def _(out=out, at=at):
                out[:, at : at + tile] = total

            step += 1


def make_projection(lay, table, attended, wo, tile, first, widths, name, follows=()):
    rows = attended[0].shape[0]
    depth = wo.shape[0]
    count = sum(widths)
    return pl.pallas_call(
        functools.partial(project_kernel, len(attended), len(follows), tile),
        grid_spec=pltpu.PrefetchScalarGridSpec(
            num_scalar_prefetch=1,
            grid=(count,),
            in_specs=[pl.BlockSpec(x.shape, lambda n, t: (0, 0)) for x in attended]
            + [pl.BlockSpec((depth, tile), lambda n, t: (0, first(t[lay.tensor_rank]) + n))]
            + [pl.BlockSpec(memory_space=pl.ANY)] * len(follows),
            out_specs=[pl.BlockSpec((rows, w * tile), lambda n, t: (0, 0)) for w in widths],
        ),
        out_shape=[jax.ShapeDtypeStruct((rows, w * tile), jnp.bfloat16) for w in widths],
        compiler_params=params(20),
        cost_estimate=cost(
            2 * rows * depth * count * tile, 2 * (rows * depth + (rows + depth) * count * tile)
        ),
        name=name,
    )(table, *attended, in_hbm(wo), *follows)


def add_kernel(lay, blocks, table, *refs):
    x_refs, own, received = refs[:blocks], refs[blocks], refs[blocks + 1]
    outs, moved = refs[blocks + 2 : -1], refs[-1]
    rows = moved.shape[1]
    place = 0
    for x in x_refs:
        for at in range(0, x.shape[0], rows):
            summed = own[place].astype(jnp.float32) + received[place].astype(jnp.float32)
            moved[table[lay.sent_as + place]] = (
                x[at : at + rows].astype(jnp.float32) + summed
            ).astype(jnp.bfloat16)
            place += 1
    for n, out in enumerate(outs):
        for flip in range(CORES):
            out[flip] = moved[n * CORES + flip]


def make_sum(lay, table, arrived, own, received, first):
    spans, rows, cols = received.shape
    chunk = first // cols
    whole = lambda n, t: (0, 0, 0)
    return pl.pallas_call(
        functools.partial(add_kernel, lay, len(arrived)),
        grid_spec=pltpu.PrefetchScalarGridSpec(
            num_scalar_prefetch=1,
            grid=(1,),
            in_specs=[pl.BlockSpec((x.shape[0], cols), lambda n, t: (0, chunk)) for x in arrived]
            + [pl.BlockSpec((spans, rows, cols), whole)] * 2,
            out_specs=[pl.BlockSpec((CORES, rows, cols), whole)] * lay.chips,
            scratch_shapes=[pltpu.VMEM((spans, rows, cols), jnp.bfloat16)],
        ),
        out_shape=[jax.ShapeDtypeStruct((CORES, rows, cols), jnp.bfloat16)] * lay.chips,
        compiler_params=params(12),
        cost_estimate=cost(3 * spans * rows * cols, 8 * spans * rows * cols),
        name="residual",
    )(table, *arrived, own, received)


def place_kernel(lay, table, *refs):
    same, swapped, out = refs[: lay.chips], refs[lay.chips], refs[-1]
    rows = swapped.shape[1]
    group_rank = table[lay.group_rank]
    chip, core = lax.div(group_rank, CORES), lax.rem(group_rank, CORES)
    for n, hop in enumerate(hop_order(lay.chips)):
        owner = lax.rem(chip + lay.chips - hop, lay.chips) * CORES
        for block, at_core in ((same[n][0], core), (swapped[n], 1 - core)):
            at = pl.multiple_of((owner + at_core) * rows, rows)
            out[pl.ds(at, rows)] = block


def make_placed(lay, table, same, swapped, first, cols, whole):
    chips, rows, tile = swapped.shape
    chunk = first // tile
    return pl.pallas_call(
        functools.partial(place_kernel, lay),
        grid_spec=pltpu.PrefetchScalarGridSpec(
            num_scalar_prefetch=1,
            grid=(1,),
            in_specs=[pl.BlockSpec((CORES, rows, tile), lambda n, t: (0, 0, 0))] * chips
            + [pl.BlockSpec((chips, rows, tile), lambda n, t: (0, 0, 0))]
            + [pl.BlockSpec(memory_space=pl.ANY)] * len(whole),
            out_specs=pl.BlockSpec((chips * CORES * rows, tile), lambda n, t: (0, chunk)),
        ),
        out_shape=jax.ShapeDtypeStruct((chips * CORES * rows, cols), jnp.bfloat16),
        input_output_aliases={chips + 2: 0} if whole else {},
        compiler_params=params(12),
        cost_estimate=cost(0, 4 * chips * CORES * rows * tile),
        name="placed",
    )(table, *same, swapped, *whole)


def rope_tables(earlier, span_len, first_row, rows, head):
    half = head // 2
    freqs = jnp.power(
        jnp.float32(rope_base), -jnp.arange(half, dtype=jnp.float32) * 2.0 / head
    )
    at = earlier[:, None] * span_len + first_row + jnp.arange(rows, dtype=jnp.int32)[None, :]
    angles = at.reshape(-1).astype(jnp.float32)[:, None] * freqs[None, :]
    cosine, sine = jnp.cos(angles), jnp.sin(angles)
    return (
        jnp.concatenate([cosine, cosine], axis=1),
        jnp.concatenate([-sine, sine], axis=1),
    )


def after(x, done):
    return lax.optimization_barrier((x, done))[0]


def shift(x, owners, hop, flip):
    chips = owners // CORES
    pairs = [
        (z * CORES + c, (z + hop) % chips * CORES + (c ^ flip))
        for z in range(chips)
        for c in range(CORES)
    ]
    return lax.ppermute(x, "group", pairs)


def local(
    hidden_in, ln_gain, wq, wk, wv, q_gain, key_norm_gain, wo,
    prompt_spans, span_source, span_target, page_slot,
):
    _, span_len, cols = hidden_in.shape
    tensor_size = lax.axis_size("tensor")
    owners = lax.axis_size("group")
    tensor_rank = lax.axis_index("tensor")
    group_rank = lax.axis_index("group")
    chips = owners // CORES
    head = q_gain.shape[0]
    rows = span_len // owners
    pages_each = span_len // PAGE_ROWS
    spans = span_source.shape[0]
    here = spans // PARTS
    most = min(spans - (prompt_spans.shape[0] - 1), spans // 2)
    kv_cols = wk.shape[1]
    paired = tensor_size == 2
    swap = [(0, 1), (1, 0)]
    lay = Layout(spans, spans * pages_each, owners)

    if kv_cols < head:
        share = head // kv_cols
        sets = [list(range(i, i + share)) for i in range(0, tensor_size, share)]
        wk, wv = [
            lax.all_gather(w, "tensor", axis=1, tiled=True, axis_index_groups=sets)
            for w in (wk, wv)
        ]
    per_kv = wq.shape[1] // max(head, wk.shape[1])

    chip, core = group_rank // CORES, group_rank % CORES
    split = hidden_in.reshape(owners, rows, cols)

    def rows_for(hop, flip):
        to = lax.rem(chip + hop, chips) * CORES + lax.rem(core + flip, CORES)
        return lax.dynamic_index_in_dim(split, to, 0, keepdims=False)

    cross = lambda x: lax.ppermute(x, "tensor", swap)

    hops = hop_order(chips)
    paired_hops = hops[2:]
    near = [rows_for(hop, flip) for hop in hops[1:2] for flip in range(CORES)]
    near = [shift(x, owners, hops[1], flip) for flip, x in enumerate(near)]
    swapped = shift(
        jnp.stack([rows_for(hop, 1) for hop in hops[:1] + paired_hops]), owners, 0, 1
    )
    arrived = [rows_for(0, 0), swapped[0]] + near
    moves = []
    for n, hop in enumerate(paired_hops):
        pair = [rows_for(hop, 0), swapped[1 + n]]
        if n < len(paired_hops) - 1:
            moves.append((hop, jnp.concatenate(pair)))
        else:
            moves += [(hop, block) for block in pair]

    ranks = jnp.stack([group_rank, tensor_rank]).astype(jnp.int32)
    table = make_tables(
        lay, spans, spans * pages_each, ranks, prompt_spans, span_source, span_target, page_slot
    )
    earlier = table[lay.earlier_at : lay.earlier_at + spans]
    cosine, sine = rope_tables(earlier, span_len, group_rank * rows, rows, head)

    crossed = [cross(x) for x in arrived] if paired else []
    if paired:
        gain = ln_gain[None]
        gains = [gain, cross(after(gain, swapped))]
    else:
        gains = [lax.all_gather(ln_gain, "tensor", axis=0, tiled=True)[None]]

    kvs, norms = [], []

    def make_part(own_rows, crossed_rows):
        if paired:
            xs = [own_rows, crossed_rows]
        else:
            xs = [[lax.all_gather(jnp.concatenate(own_rows), "tensor", axis=1, tiled=True)]]
        *normed, kv = make_kv(
            lay, table, xs, gains, wk, wv, key_norm_gain[None], cosine, sine, len(kvs)
        )
        kvs.append([kv.reshape(2, here, rows, kv.shape[2])])
        norms.append(normed)

    def one_back(p, done=()):
        kvs[p].append(shift(after(kvs[p][-1], done), owners, 1, 0))

    begun = 0
    for n in range(len(moves) + 1):
        if n:
            hop, block = moves[n - 1]
            if paired:
                landed = arrived[-1:] if n > 1 else near
                matching = crossed[2 * n - 2 : 2 * n] if n < 3 else crossed[n + 1]
                block = after(block, (landed, matching, gains))
            arrived.append(shift(block, owners, hop, 0))
            if paired:
                block = arrived[-1]
                if n == len(moves) and kvs:
                    block = after(block, kvs[0][0])
                crossed.append(cross(block))
        if sum(x.shape[0] for x in arrived[begun:]) == here * rows:
            make_part(arrived[begun:], crossed[begun:])
            begun = len(arrived)
            for _ in range(min(2, chips - 1) if len(kvs) == 1 else min(1, chips - 1)):
                one_back(len(kvs) - 1)

    queries, done = [], kvs[1][0]
    for p in range(PARTS):
        made = make_q(
            lay, table, norms[p], wq, after(q_gain[None], done), cosine, sine, p
        )
        queries.append(made.reshape(here, rows, made.shape[1]))
        done = queries[-1]
    for p in range(PARTS):
        while len(kvs[p]) < chips:
            one_back(p, queries[p])
    gathered = []
    for back in range(chips):
        gathered.append([kv[back] for kv in kvs])
        gathered.append([shift(kv[back], owners, 0, 1) for kv in kvs])

    own_kv = wk.shape[1] // head
    sets = [own_kv // 2] * 2 if own_kv % 2 == 0 else [1] * own_kv
    attended, pages, first = [], [], 0
    for count in sets:
        made, cut = make_attention(
            lay, most, table, queries, gathered, per_kv, head, pages_each, first, count
        )
        attended.append(made.reshape(spans * rows, -1))
        pages.append(cut)
        first += count

    if paired:
        tile = 512 if cols % 512 == 0 else cols
        tiles = cols // tile
        widths = [2, 2, 1] if tiles == 5 else [tiles]
        others = [cross(pages[0])]
        project = functools.partial(make_projection, lay, table, attended, wo, tile)
        send = project(lambda r: (1 - r) * tiles, widths[:1], "send_part", (others[0],))
        if widths[1:]:
            send += project(
                lambda r: (1 - r) * tiles + widths[0], widths[1:], "send_part", (send[0],)
            )
        own = project(lambda r: r * tiles, widths, "own_part", (send[-1],))
        whole, received, landed, first = (), [], [], 0
        for n, sent in enumerate(send):
            if n:
                sent = after(sent, (received[-1], own, landed[-2:-1]))
            received.append(cross(sent))
            moved = make_sum(
                lay, table, arrived, own[n].reshape(spans, rows, -1),
                received[-1].reshape(spans, rows, -1), first,
            )
            same = [
                shift(x, owners, hop, 0) if hop else x
                for hop, x in zip(hop_order(chips), moved)
            ]
            landed.append(same)
            swapped = shift(jnp.concatenate([x[1:] for x in same]), owners, 0, 1)
            whole = (make_placed(lay, table, same, swapped, first, cols, whole),)
            first += sent.shape[1]
        mixed = whole[0].reshape(1, span_len, cols)
        for cut in pages[1:]:
            others.append(cross(after(cut, received[-1])))
        low = [jnp.where(tensor_rank == 0, a, b) for a, b in zip(pages, others)]
        high = [jnp.where(tensor_rank == 0, b, a) for a, b in zip(pages, others)]
        cache = jnp.concatenate(low + high, axis=3)
    else:
        pages = jnp.concatenate(pages, axis=3)
        attended = jnp.concatenate(attended, axis=1)
        if kv_cols < head:
            pages = lax.dynamic_slice_in_dim(
                pages, lax.rem(tensor_rank, head // kv_cols) * kv_cols, kv_cols, 3
            )
        cache = lax.all_gather(pages, "tensor", axis=3, tiled=True)
        partial = jnp.dot(attended, wo, preferred_element_type=jnp.float32)
        summed = lax.psum_scatter(
            partial.astype(jnp.bfloat16), "tensor", scatter_dimension=1, tiled=True
        )
        summed = summed.reshape(spans, rows, cols).astype(jnp.float32)
        x = jnp.concatenate(arrived).reshape(spans, rows, cols).astype(jnp.float32)
        moved = (x + summed).astype(jnp.bfloat16)
        targets = table[lay.target_at : lay.target_at + spans]
        moved = jnp.zeros_like(moved).at[targets].set(moved, unique_indices=True)
        moved = lax.all_to_all(moved, "group", split_axis=0, concat_axis=0, tiled=True)
        mixed = moved.reshape(1, span_len, cols)
    return (mixed, cache)


def solution(mesh):
    in_specs = (
        P(("replica", "group"), None, "tensor"),
        P("tensor"),
        P(None, "tensor"),
        P(None, "tensor"),
        P(None, "tensor"),
        P(),
        P(),
        P("tensor", None),
        P("replica"),
        P("replica"),
        P("replica"),
        P("replica"),
    )
    out_specs = (P(("replica", "group"), None, "tensor"), P(("replica", "group"), None, None, None))
    return jax.shard_map(local, mesh=mesh, in_specs=in_specs, out_specs=out_specs, check_vma=False)
```

```python
import functools
import math

import jax
import jax.numpy as jnp
from jax import lax
from jax.experimental import pallas as pl
from jax.experimental.pallas import tpu as pltpu
from jax.sharding import PartitionSpec as P

PAGE_ROWS = 128
epsilon = 1e-06
rope_base = 1000000.0
very_negative = -1e30
PARTS = 2
CORES = 2
SHARE = 0.02


def params(mebibytes):
    return pltpu.CompilerParams(vmem_limit_bytes=mebibytes * 1024 * 1024)


def in_hbm(x):
    return pltpu.with_memory_space_constraint(x, pltpu.HBM)


def cost(flops, moved, transcendentals=0):
    return pl.CostEstimate(
        flops=int(flops * SHARE),
        bytes_accessed=int(moved * SHARE),
        transcendentals=int(transcendentals * SHARE),
    )


def hop_order(chips):
    return [0, 1, chips - 1] + list(range(2, chips - 1)) if chips > 2 else list(range(chips))


class Layout:
    def __init__(self, spans, pages, owners):
        self.chips = owners // CORES
        self.span_at = 0
        self.earlier_at = self.span_at + spans
        self.target_at = self.earlier_at + spans
        self.sent_as = self.target_at + spans
        self.page = self.sent_as + spans
        self.origin = self.page + pages
        self.group_rank = self.origin + owners * spans
        self.tensor_rank = self.group_rank + 1
        self.length = self.tensor_rank + 1


def tables_kernel(lay, spans, pages, ranks, prompt_spans, source, target, page_slot, out, span_of, start_of):
    chips = lay.chips
    group_rank = ranks[0]
    out[lay.group_rank] = group_rank
    out[lay.tensor_rank] = ranks[1]
    for k in range(spans):
        start = jnp.int32(0)
        begin = jnp.int32(0)
        for p in range(prompt_spans.shape[0]):
            start = jnp.where(begin <= k, begin, start)
            begin = begin + prompt_spans[p]
        start_of[k] = start
        span_of[source[k]] = jnp.int32(k)
    for p in range(pages):
        out[lay.page + page_slot[p]] = jnp.int32(p)
    chip, core = lax.div(group_rank, CORES), lax.rem(group_rank, CORES)
    hops = hop_order(chips)
    for back in range(chips):
        for other in range(CORES):
            at_chip = lax.rem(chip + chips - back, chips)
            at_core = jnp.where(other == 0, core, 1 - core)
            for n, hop in enumerate(hops):
                for flip in range(CORES):
                    from_chip = lax.rem(at_chip + chips - hop, chips)
                    from_core = jnp.where(flip == 0, at_core, 1 - at_core)
                    k = span_of[from_chip * CORES + from_core]
                    place = n * CORES + flip
                    out[lay.origin + (back * CORES + other) * spans + place] = k
                    if back == 0 and other == 0:
                        out[lay.span_at + place] = k
                        out[lay.earlier_at + place] = k - start_of[k]
                        owner = target[k]
                        ahead = lax.rem(lax.div(owner, CORES) + chips - chip, chips)
                        turn = jnp.int32(0)
                        for m, other_hop in enumerate(hops):
                            turn = jnp.where(ahead == other_hop, jnp.int32(m), turn)
                        crossing = jnp.where(lax.rem(owner, CORES) == core, 0, 1)
                        out[lay.target_at + place] = owner
                        out[lay.sent_as + place] = turn * CORES + crossing


def make_tables(lay, spans, pages, ranks, prompt_spans, source, target, page_slot):
    smem = pl.BlockSpec(memory_space=pltpu.SMEM)
    return pl.pallas_call(
        functools.partial(tables_kernel, lay, spans, pages),
        out_shape=jax.ShapeDtypeStruct((lay.length,), jnp.int32),
        in_specs=[smem] * 5,
        out_specs=smem,
        scratch_shapes=[pltpu.SMEM((spans,), jnp.int32)] * 2,
        compiler_params=params(4),
        name="tables",
    )(ranks, prompt_spans, source, target, page_slot)


def head_norm_rope(u, gain, cosine, sine):
    mean_sq = jnp.mean(u * u, axis=-1, keepdims=True)
    u = u * lax.rsqrt(mean_sq + epsilon) * gain
    half = u.shape[-1] // 2
    return u * cosine + pltpu.roll(u, half, 1) * sine


def half_index(lay, sides, side):
    if sides == 1:
        return lambda t: 0
    if side == 0:
        return lambda t: t[lay.tensor_rank]
    return lambda t: 1 - t[lay.tensor_rank]


def summed_dot(lefts, rights):
    total = None
    for left, right in zip(lefts, rights):
        term = jnp.dot(left[...], right[...], preferred_element_type=jnp.float32)
        total = term if total is None else total + term
    return total


def kv_kernel(sides, blocks, table, *refs):
    refs = list(refs)
    take = lambda n: [refs.pop(0) for _ in range(n)]
    xs = [take(blocks) for _ in range(sides)]
    gains, wks, wvs = take(sides), take(sides), take(sides)
    kgain, cosine, sine = take(3)
    normed, (kv,) = take(sides), take(1)
    head = kgain.shape[1]
    width = sum(x[0].shape[1] for x in xs)

    @pl.when(pl.program_id(0) == 0)
    def _():
        at = 0
        for b in range(blocks):
            wide = [x[b][...].astype(jnp.float32) for x in xs]
            total = sum(jnp.sum(w * w, axis=-1, keepdims=True) for w in wide)
            factor = lax.rsqrt(total / width + epsilon)
            rows = xs[0][b].shape[0]
            for w, gain, to in zip(wide, gains, normed):
                to[at : at + rows] = (w * factor * gain[...].astype(jnp.float32)).astype(
                    jnp.bfloat16
                )
            at += rows

    keys = summed_dot(normed, wks).astype(jnp.bfloat16)
    gains = kgain[...].astype(jnp.float32)
    for h in range(keys.shape[1] // head):
        u = keys[:, h * head : (h + 1) * head].astype(jnp.float32)
        kv[0, :, h * head : (h + 1) * head] = head_norm_rope(
            u, gains, cosine[...], sine[...]
        ).astype(jnp.bfloat16)
    kv[1] = summed_dot(normed, wvs).astype(jnp.bfloat16)


def make_kv(lay, table, xs, gains, wk, wv, kgain, cosine, sine, part):
    sides, blocks = len(xs), len(xs[0])
    rows = sum(x.shape[0] for x in xs[0])
    widths = [x[0].shape[1] for x in xs]
    width, cols = wk.shape
    tile = 256 if cols % 256 == 0 else cols
    head = kgain.shape[1]
    fixed = lambda n, t: (0, 0)
    here = lambda n, t: (part, 0)
    weights = []
    for side in range(sides):
        index = half_index(lay, sides, side)
        weights.append(
            pl.BlockSpec((widths[side], tile), lambda n, t, index=index: (index(t), n))
        )
    return pl.pallas_call(
        functools.partial(kv_kernel, sides, blocks),
        grid_spec=pltpu.PrefetchScalarGridSpec(
            num_scalar_prefetch=1,
            grid=(cols // tile,),
            in_specs=[pl.BlockSpec(x.shape, fixed) for side in xs for x in side]
            + [pl.BlockSpec((1, w), fixed) for w in widths]
            + weights
            + weights
            + [
                pl.BlockSpec((1, head), fixed),
                pl.BlockSpec((rows, head), here),
                pl.BlockSpec((rows, head), here),
            ],
            out_specs=[pl.BlockSpec((rows, w), fixed) for w in widths]
            + [pl.BlockSpec((2, rows, tile), lambda n, t: (0, 0, n))],
        ),
        out_shape=[jax.ShapeDtypeStruct((rows, w), jnp.bfloat16) for w in widths]
        + [jax.ShapeDtypeStruct((2, rows, cols), jnp.bfloat16)],
        compiler_params=params(32),
        cost_estimate=cost(4 * rows * width * cols, 4 * width * cols + 4 * rows * width),
        name="keys_values",
    )(
        table, *[x for side in xs for x in side], *gains,
        *[in_hbm(wk)] * sides, *[in_hbm(wv)] * sides,
        kgain, cosine, sine,
    )


def q_kernel(sides, table, *refs):
    normed, wqs = refs[:sides], refs[sides : 2 * sides]
    qgain, cosine, sine, out = refs[2 * sides :]
    head = qgain.shape[1]
    lin = summed_dot(normed, wqs)
    gains = qgain[...].astype(jnp.float32)
    for h in range(lin.shape[1] // head):
        out[:, h * head : (h + 1) * head] = head_norm_rope(
            lin[:, h * head : (h + 1) * head], gains, cosine[...], sine[...]
        ).astype(jnp.bfloat16)


def make_q(lay, table, normed, wq, qgain, cosine, sine, part):
    sides = len(normed)
    rows = normed[0].shape[0]
    width, cols = wq.shape
    tile = 512 if cols % 512 == 0 else cols
    head = qgain.shape[1]
    fixed = lambda n, t: (0, 0)
    here = lambda n, t: (part, 0)
    weights = []
    for side in range(sides):
        index = half_index(lay, sides, side)
        weights.append(
            pl.BlockSpec(
                (normed[side].shape[1], tile), lambda n, t, index=index: (index(t), n)
            )
        )
    return pl.pallas_call(
        functools.partial(q_kernel, sides),
        grid_spec=pltpu.PrefetchScalarGridSpec(
            num_scalar_prefetch=1,
            grid=(cols // tile,),
            in_specs=[pl.BlockSpec(x.shape, fixed) for x in normed]
            + weights
            + [
                pl.BlockSpec((1, head), fixed),
                pl.BlockSpec((rows, head), here),
                pl.BlockSpec((rows, head), here),
            ],
            out_specs=pl.BlockSpec((rows, tile), lambda n, t: (0, n)),
        ),
        out_shape=jax.ShapeDtypeStruct((rows, cols), jnp.bfloat16),
        compiler_params=params(24),
        cost_estimate=cost(2 * rows * width * cols, 2 * width * cols + 2 * rows * (width + cols)),
        name="queries",
    )(table, *normed, *[in_hbm(wq)] * sides, qgain, cosine, sine)


def attention_kernel(lay, spans, most, per_kv, head, beside, owners, pages_each, table, *refs):
    q_refs = refs[:PARTS]
    kv_refs = refs[PARTS : PARTS + owners * PARTS]
    out, pages, keys, values, asked = refs[PARTS + owners * PARTS :]
    chips = lay.chips
    here, rows = kv_refs[0].shape[1], kv_refs[0].shape[2]
    group_rank = table[lay.group_rank]
    chip, core = lax.div(group_rank, CORES), lax.rem(group_rank, CORES)
    heads = range(beside)
    for p in range(PARTS):
        asked[p * here : (p + 1) * here] = q_refs[p][...]
    for o in range(owners):
        back, other = o // CORES, o % CORES
        owner = lax.rem(chip + chips - back, chips) * CORES + (core if other == 0 else 1 - core)
        at = pl.ds(pl.multiple_of(owner * rows, rows), rows)
        for p in range(PARTS):
            for i in range(here):
                k = table[lay.origin + o * spans + p * here + i]
                for h in heads:
                    lanes = slice(h * head, (h + 1) * head)
                    keys[h, k, at] = kv_refs[o * PARTS + p][0, i, :, lanes]
                    values[h, k, at] = kv_refs[o * PARTS + p][1, i, :, lanes]

    for i in range(pages_each):
        page = table[lay.page + group_rank * pages_each + i]
        k = lax.div(page, pages_each)
        at = pl.ds(pl.multiple_of(lax.rem(page, pages_each) * PAGE_ROWS, PAGE_ROWS), PAGE_ROWS)
        for h in heads:
            lanes = slice(h * head, (h + 1) * head)
            pages[i, 0, :, lanes] = keys[h, k, at]
            pages[i, 1, :, lanes] = values[h, k, at]

    scale = (1.0 / math.sqrt(head)) * math.log2(math.e)
    q_rows, k_rows = per_kv * rows, owners * rows
    row = lax.broadcasted_iota(jnp.int32, (q_rows, k_rows), 0)
    col = lax.broadcasted_iota(jnp.int32, (q_rows, k_rows), 1)
    allowed = col <= group_rank * rows + row % rows

    def one_place(place, carry):
        k = table[lay.span_at + place]
        earlier = table[lay.earlier_at + place]

        def with_earlier(count):
            scores = [[] for _ in heads]
            for h in heads:
                queries = jnp.concatenate(
                    [
                        asked[place, :, (h * per_kv + g) * head : (h * per_kv + g + 1) * head]
                        for g in range(per_kv)
                    ],
                    axis=0,
                )
                for back in range(count + 1):
                    s = lax.dot_general(
                        queries, keys[h, k - back], (((1,), (1,)), ((), ())),
                        preferred_element_type=jnp.float32,
                    )
                    if back == 0:
                        s = jnp.where(allowed, s, very_negative)
                    scores[h].append(s)
            for h in heads:
                best = functools.reduce(jnp.maximum, scores[h])
                best = jnp.max(best, axis=-1, keepdims=True)
                shifted = best * scale
                weights = [jnp.exp2(s * scale - shifted) for s in scores[h]]
                total = jnp.sum(
                    functools.reduce(lambda a, b: a + b, weights), axis=-1, keepdims=True
                )
                summed = None
                for back, w in enumerate(weights):
                    term = jnp.dot(
                        w.astype(jnp.bfloat16), values[h, k - back],
                        preferred_element_type=jnp.float32,
                    )
                    summed = term if summed is None else summed + term
                result = (summed / total).astype(jnp.bfloat16)
                for g in range(per_kv):
                    at = (h * per_kv + g) * head
                    out[place, :, at : at + head] = result[g * rows : (g + 1) * rows]

        for count in range(most):
            pl.when(earlier == count)(functools.partial(with_earlier, count))
        return carry

    lax.fori_loop(0, spans, one_place, 0)


def make_attention(lay, most, table, queries, gathered, per_kv, head, pages_each, first, count):
    here, rows, cols = queries[0].shape
    spans = here * PARTS
    owners = len(gathered)
    at = first // count
    q_spec = pl.BlockSpec((here, rows, count * per_kv * head), lambda h, t: (0, 0, at + h))
    kv_spec = pl.BlockSpec((2, here, rows, count * head), lambda h, t: (0, 0, 0, at + h))
    flat = [x for origin in gathered for x in origin]
    all_rows = spans * rows
    pairs = 2.2 * all_rows * owners * rows * per_kv * count
    return pl.pallas_call(
        functools.partial(
            attention_kernel, lay, spans, most, per_kv, head, count, owners, pages_each
        ),
        grid_spec=pltpu.PrefetchScalarGridSpec(
            num_scalar_prefetch=1,
            grid=(1,),
            in_specs=[q_spec] * PARTS + [kv_spec] * len(flat),
            out_specs=[
                pl.BlockSpec((spans, rows, count * per_kv * head), lambda h, t: (0, 0, h)),
                pl.BlockSpec((pages_each, 2, PAGE_ROWS, count * head), lambda h, t: (0, 0, 0, h)),
            ],
            scratch_shapes=[pltpu.VMEM((count, spans, owners * rows, head), jnp.bfloat16)] * 2
            + [pltpu.VMEM((spans, rows, count * per_kv * head), jnp.bfloat16)],
        ),
        out_shape=[
            jax.ShapeDtypeStruct((spans, rows, count * per_kv * head), jnp.bfloat16),
            jax.ShapeDtypeStruct((pages_each, 2, PAGE_ROWS, count * head), jnp.bfloat16),
        ],
        compiler_params=params(32),
        cost_estimate=cost(
            4 * pairs * head, 4 * all_rows * cols + 2 * len(flat) * flat[0].size, pairs
        ),
        name="attention",
    )(table, *queries, *flat)


def project_kernel(pieces, follows, tile, table, *refs):
    attended, wo, outs = refs[:pieces], refs[pieces], refs[pieces + 1 + follows :]
    total, at = None, 0
    for piece in attended:
        depth = piece.shape[1]
        term = jnp.dot(piece[...], wo[at : at + depth], preferred_element_type=jnp.float32)
        total = term if total is None else total + term
        at += depth
    total = total.astype(jnp.bfloat16)
    step = 0
    for out in outs:
        for at in range(0, out.shape[1], tile):

            @pl.when(pl.program_id(0) == step)
            def _(out=out, at=at):
                out[:, at : at + tile] = total

            step += 1


def make_projection(lay, table, attended, wo, tile, first, widths, name, follows=()):
    rows = attended[0].shape[0]
    depth = wo.shape[0]
    count = sum(widths)
    return pl.pallas_call(
        functools.partial(project_kernel, len(attended), len(follows), tile),
        grid_spec=pltpu.PrefetchScalarGridSpec(
            num_scalar_prefetch=1,
            grid=(count,),
            in_specs=[pl.BlockSpec(x.shape, lambda n, t: (0, 0)) for x in attended]
            + [pl.BlockSpec((depth, tile), lambda n, t: (0, first(t[lay.tensor_rank]) + n))]
            + [pl.BlockSpec(memory_space=pl.ANY)] * len(follows),
            out_specs=[pl.BlockSpec((rows, w * tile), lambda n, t: (0, 0)) for w in widths],
        ),
        out_shape=[jax.ShapeDtypeStruct((rows, w * tile), jnp.bfloat16) for w in widths],
        compiler_params=params(20),
        cost_estimate=cost(
            2 * rows * depth * count * tile, 2 * (rows * depth + (rows + depth) * count * tile)
        ),
        name=name,
    )(table, *attended, in_hbm(wo), *follows)


def add_kernel(lay, blocks, table, *refs):
    x_refs, own, received = refs[:blocks], refs[blocks], refs[blocks + 1]
    outs, moved = refs[blocks + 2 : -1], refs[-1]
    rows = moved.shape[1]
    place = 0
    for x in x_refs:
        for at in range(0, x.shape[0], rows):
            summed = own[place].astype(jnp.float32) + received[place].astype(jnp.float32)
            moved[table[lay.sent_as + place]] = (
                x[at : at + rows].astype(jnp.float32) + summed
            ).astype(jnp.bfloat16)
            place += 1
    for n, out in enumerate(outs):
        for flip in range(CORES):
            out[flip] = moved[n * CORES + flip]


def make_sum(lay, table, arrived, own, received, first):
    spans, rows, cols = received.shape
    chunk = first // cols
    whole = lambda n, t: (0, 0, 0)
    return pl.pallas_call(
        functools.partial(add_kernel, lay, len(arrived)),
        grid_spec=pltpu.PrefetchScalarGridSpec(
            num_scalar_prefetch=1,
            grid=(1,),
            in_specs=[pl.BlockSpec((x.shape[0], cols), lambda n, t: (0, chunk)) for x in arrived]
            + [pl.BlockSpec((spans, rows, cols), whole)] * 2,
            out_specs=[pl.BlockSpec((CORES, rows, cols), whole)] * lay.chips,
            scratch_shapes=[pltpu.VMEM((spans, rows, cols), jnp.bfloat16)],
        ),
        out_shape=[jax.ShapeDtypeStruct((CORES, rows, cols), jnp.bfloat16)] * lay.chips,
        compiler_params=params(12),
        cost_estimate=cost(3 * spans * rows * cols, 8 * spans * rows * cols),
        name="residual",
    )(table, *arrived, own, received)


def place_kernel(lay, chunks, table, *refs):
    out = refs[-1]
    chips = lay.chips
    group_rank = table[lay.group_rank]
    chip, core = lax.div(group_rank, CORES), lax.rem(group_rank, CORES)
    first = 0
    for c in range(chunks):
        same, swapped = refs[c * (chips + 1) : (c + 1) * (chips + 1) - 1], refs[(c + 1) * (chips + 1) - 1]
        rows, cols = swapped.shape[1:]
        for n, hop in enumerate(hop_order(chips)):
            owner = lax.rem(chip + chips - hop, chips) * CORES
            for block, at_core in ((same[n][0], core), (swapped[n], 1 - core)):
                at = pl.multiple_of((owner + at_core) * rows, rows)
                out[pl.ds(at, rows), first : first + cols] = block
        first += cols


def make_placed(lay, table, pieces, cols):
    flat = [x for same, swapped in pieces for x in [*same, swapped]]
    chips, rows, _ = pieces[0][1].shape
    shape = (chips * CORES * rows, cols)
    return pl.pallas_call(
        functools.partial(place_kernel, lay, len(pieces)),
        grid_spec=pltpu.PrefetchScalarGridSpec(
            num_scalar_prefetch=1,
            grid=(1,),
            in_specs=[pl.BlockSpec(x.shape, lambda n, t: (0, 0, 0)) for x in flat],
            out_specs=pl.BlockSpec(shape, lambda n, t: (0, 0)),
        ),
        out_shape=jax.ShapeDtypeStruct(shape, jnp.bfloat16),
        compiler_params=params(16),
        cost_estimate=cost(0, 4 * shape[0] * shape[1]),
        name="placed",
    )(table, *flat)


def rope_tables(earlier, span_len, first_row, rows, head):
    half = head // 2
    freqs = jnp.power(
        jnp.float32(rope_base), -jnp.arange(half, dtype=jnp.float32) * 2.0 / head
    )
    at = earlier[:, None] * span_len + first_row + jnp.arange(rows, dtype=jnp.int32)[None, :]
    angles = at.reshape(-1).astype(jnp.float32)[:, None] * freqs[None, :]
    cosine, sine = jnp.cos(angles), jnp.sin(angles)
    return (
        jnp.concatenate([cosine, cosine], axis=1),
        jnp.concatenate([-sine, sine], axis=1),
    )


def after(x, done):
    return lax.optimization_barrier((x, done))[0]


def shift(x, owners, hop, flip):
    chips = owners // CORES
    pairs = [
        (z * CORES + c, (z + hop) % chips * CORES + (c ^ flip))
        for z in range(chips)
        for c in range(CORES)
    ]
    return lax.ppermute(x, "group", pairs)


def local(
    hidden_in, ln_gain, wq, wk, wv, q_gain, key_norm_gain, wo,
    prompt_spans, span_source, span_target, page_slot,
):
    _, span_len, cols = hidden_in.shape
    tensor_size = lax.axis_size("tensor")
    owners = lax.axis_size("group")
    tensor_rank = lax.axis_index("tensor")
    group_rank = lax.axis_index("group")
    chips = owners // CORES
    head = q_gain.shape[0]
    rows = span_len // owners
    pages_each = span_len // PAGE_ROWS
    spans = span_source.shape[0]
    here = spans // PARTS
    most = min(spans - (prompt_spans.shape[0] - 1), spans // 2)
    kv_cols = wk.shape[1]
    paired = tensor_size == 2
    swap = [(0, 1), (1, 0)]
    lay = Layout(spans, spans * pages_each, owners)

    if kv_cols < head:
        share = head // kv_cols
        sets = [list(range(i, i + share)) for i in range(0, tensor_size, share)]
        wk, wv = [
            lax.all_gather(w, "tensor", axis=1, tiled=True, axis_index_groups=sets)
            for w in (wk, wv)
        ]
    per_kv = wq.shape[1] // max(head, wk.shape[1])

    chip, core = group_rank // CORES, group_rank % CORES
    split = hidden_in.reshape(owners, rows, cols)

    def rows_for(hop, flip):
        to = lax.rem(chip + hop, chips) * CORES + lax.rem(core + flip, CORES)
        return lax.dynamic_index_in_dim(split, to, 0, keepdims=False)

    cross = lambda x: lax.ppermute(x, "tensor", swap)

    hops = hop_order(chips)
    paired_hops = hops[2:]
    near = [rows_for(hop, flip) for hop in hops[1:2] for flip in range(CORES)]
    near = [shift(x, owners, hops[1], flip) for flip, x in enumerate(near)]
    swapped = shift(
        jnp.stack([rows_for(hop, 1) for hop in hops[:1] + paired_hops]), owners, 0, 1
    )
    arrived = [rows_for(0, 0), swapped[0]] + near
    moves = []
    for n, hop in enumerate(paired_hops):
        pair = [rows_for(hop, 0), swapped[1 + n]]
        if n < len(paired_hops) - 1:
            moves.append((hop, jnp.concatenate(pair)))
        else:
            moves += [(hop, block) for block in pair]

    ranks = jnp.stack([group_rank, tensor_rank]).astype(jnp.int32)
    table = make_tables(
        lay, spans, spans * pages_each, ranks, prompt_spans, span_source, span_target, page_slot
    )
    earlier = table[lay.earlier_at : lay.earlier_at + spans]
    cosine, sine = rope_tables(earlier, span_len, group_rank * rows, rows, head)

    crossed = [cross(x) for x in arrived] if paired else []
    if paired:
        gain = ln_gain[None]
        gains = [gain, cross(after(gain, swapped))]
    else:
        gains = [lax.all_gather(ln_gain, "tensor", axis=0, tiled=True)[None]]

    kvs, norms = [], []

    def make_part(own_rows, crossed_rows):
        if paired:
            xs = [own_rows, [in_hbm(x) for x in crossed_rows]]
        else:
            xs = [[lax.all_gather(jnp.concatenate(own_rows), "tensor", axis=1, tiled=True)]]
        *normed, kv = make_kv(
            lay, table, xs, gains, wk, wv, key_norm_gain[None], cosine, sine, len(kvs)
        )
        kvs.append([kv.reshape(2, here, rows, kv.shape[2])])
        norms.append(normed)

    def one_back(p, done=()):
        kvs[p].append(shift(after(kvs[p][-1], done), owners, 1, 0))

    begun = 0
    for n in range(len(moves) + 1):
        if n:
            hop, block = moves[n - 1]
            if paired:
                landed = arrived[-1:] if n > 1 else near
                matching = crossed[2 * n - 2 : 2 * n] if n < 3 else crossed[n + 1]
                block = after(block, (landed, matching, gains))
            arrived.append(shift(block, owners, hop, 0))
            if paired:
                block = arrived[-1]
                if n == len(moves) and kvs:
                    block = after(block, kvs[0][0])
                crossed.append(cross(block))
        if sum(x.shape[0] for x in arrived[begun:]) == here * rows:
            make_part(arrived[begun:], crossed[begun:])
            begun = len(arrived)
            for _ in range(min(2, chips - 1) if len(kvs) == 1 else min(1, chips - 1)):
                one_back(len(kvs) - 1)

    queries, done = [], kvs[1][0]
    for p in range(PARTS):
        made = make_q(
            lay, table, norms[p], wq, after(q_gain[None], done), cosine, sine, p
        )
        queries.append(made.reshape(here, rows, made.shape[1]))
        done = queries[-1]
    for p in range(PARTS):
        while len(kvs[p]) < chips:
            one_back(p, queries[p])
    gathered = []
    for back in range(chips):
        gathered.append([kv[back] for kv in kvs])
        gathered.append([shift(kv[back], owners, 0, 1) for kv in kvs])

    own_kv = wk.shape[1] // head
    sets = [own_kv // 2] * 2 if own_kv % 2 == 0 else [1] * own_kv
    attended, pages, first = [], [], 0
    for count in sets:
        made, cut = make_attention(
            lay, most, table, queries, gathered, per_kv, head, pages_each, first, count
        )
        attended.append(made.reshape(spans * rows, -1))
        pages.append(cut)
        first += count

    if paired:
        tile = 512 if cols % 512 == 0 else cols
        tiles = cols // tile
        widths = [2, 2, 1] if tiles == 5 else [tiles]
        others = [cross(pages[0])]
        project = functools.partial(make_projection, lay, table, attended, wo, tile)
        send = project(lambda r: (1 - r) * tiles, widths[:1], "send_part", (others[0],))
        if widths[1:]:
            send += project(
                lambda r: (1 - r) * tiles + widths[0], widths[1:], "send_part", (send[0],)
            )
        own = project(lambda r: r * tiles, widths, "own_part", (send[-1],))
        pieces, received, landed, first = [], [], [], 0
        for n, sent in enumerate(send):
            if n:
                sent = after(sent, (received[-1], own, landed[-2:-1]))
            received.append(cross(sent))
            moved = make_sum(
                lay, table, arrived, own[n].reshape(spans, rows, -1),
                received[-1].reshape(spans, rows, -1), first,
            )
            same = [
                shift(x, owners, hop, 0) if hop else x
                for hop, x in zip(hop_order(chips), moved)
            ]
            landed.append(same)
            swapped = shift(jnp.concatenate([x[1:] for x in same]), owners, 0, 1)
            pieces.append((same, swapped))
            first += sent.shape[1]
        mixed = make_placed(lay, table, pieces, cols).reshape(1, span_len, cols)
        for cut in pages[1:]:
            others.append(cross(after(cut, received[-1])))
        low = [jnp.where(tensor_rank == 0, a, b) for a, b in zip(pages, others)]
        high = [jnp.where(tensor_rank == 0, b, a) for a, b in zip(pages, others)]
        cache = jnp.concatenate(low + high, axis=3)
    else:
        pages = jnp.concatenate(pages, axis=3)
        attended = jnp.concatenate(attended, axis=1)
        if kv_cols < head:
            pages = lax.dynamic_slice_in_dim(
                pages, lax.rem(tensor_rank, head // kv_cols) * kv_cols, kv_cols, 3
            )
        cache = lax.all_gather(pages, "tensor", axis=3, tiled=True)
        partial = jnp.dot(attended, wo, preferred_element_type=jnp.float32)
        summed = lax.psum_scatter(
            partial.astype(jnp.bfloat16), "tensor", scatter_dimension=1, tiled=True
        )
        summed = summed.reshape(spans, rows, cols).astype(jnp.float32)
        x = jnp.concatenate(arrived).reshape(spans, rows, cols).astype(jnp.float32)
        moved = (x + summed).astype(jnp.bfloat16)
        targets = table[lay.target_at : lay.target_at + spans]
        moved = jnp.zeros_like(moved).at[targets].set(moved, unique_indices=True)
        moved = lax.all_to_all(moved, "group", split_axis=0, concat_axis=0, tiled=True)
        mixed = moved.reshape(1, span_len, cols)
    return (mixed, cache)


def solution(mesh):
    in_specs = (
        P(("replica", "group"), None, "tensor"),
        P("tensor"),
        P(None, "tensor"),
        P(None, "tensor"),
        P(None, "tensor"),
        P(),
        P(),
        P("tensor", None),
        P("replica"),
        P("replica"),
        P("replica"),
        P("replica"),
    )
    out_specs = (P(("replica", "group"), None, "tensor"), P(("replica", "group"), None, None, None))
    return jax.shard_map(local, mesh=mesh, in_specs=in_specs, out_specs=out_specs, check_vma=False)
```

```python
import functools
import math

import jax
import jax.numpy as jnp
from jax import lax
from jax.experimental import pallas as pl
from jax.experimental.pallas import tpu as pltpu
from jax.sharding import PartitionSpec as P

PAGE_ROWS = 128
epsilon = 1e-06
rope_base = 1000000.0
very_negative = -1e30
PARTS = 2
CORES = 2
SHARE = 0.02


def params(mebibytes):
    return pltpu.CompilerParams(vmem_limit_bytes=mebibytes * 1024 * 1024)


def in_hbm(x):
    return pltpu.with_memory_space_constraint(x, pltpu.HBM)


def cost(flops, moved, transcendentals=0):
    return pl.CostEstimate(
        flops=int(flops * SHARE),
        bytes_accessed=int(moved * SHARE),
        transcendentals=int(transcendentals * SHARE),
    )


def hop_order(chips):
    return [0, 1, chips - 1] + list(range(2, chips - 1)) if chips > 2 else list(range(chips))


class Layout:
    def __init__(self, spans, pages, owners):
        self.chips = owners // CORES
        self.span_at = 0
        self.earlier_at = self.span_at + spans
        self.target_at = self.earlier_at + spans
        self.sent_as = self.target_at + spans
        self.page = self.sent_as + spans
        self.origin = self.page + pages
        self.group_rank = self.origin + owners * spans
        self.tensor_rank = self.group_rank + 1
        self.length = self.tensor_rank + 1


def tables_kernel(lay, spans, pages, ranks, prompt_spans, source, target, page_slot, out, span_of, start_of):
    chips = lay.chips
    group_rank = ranks[0]
    out[lay.group_rank] = group_rank
    out[lay.tensor_rank] = ranks[1]
    for k in range(spans):
        start = jnp.int32(0)
        begin = jnp.int32(0)
        for p in range(prompt_spans.shape[0]):
            start = jnp.where(begin <= k, begin, start)
            begin = begin + prompt_spans[p]
        start_of[k] = start
        span_of[source[k]] = jnp.int32(k)
    for p in range(pages):
        out[lay.page + page_slot[p]] = jnp.int32(p)
    chip, core = lax.div(group_rank, CORES), lax.rem(group_rank, CORES)
    hops = hop_order(chips)
    for back in range(chips):
        for other in range(CORES):
            at_chip = lax.rem(chip + chips - back, chips)
            at_core = jnp.where(other == 0, core, 1 - core)
            for n, hop in enumerate(hops):
                for flip in range(CORES):
                    from_chip = lax.rem(at_chip + chips - hop, chips)
                    from_core = jnp.where(flip == 0, at_core, 1 - at_core)
                    k = span_of[from_chip * CORES + from_core]
                    place = n * CORES + flip
                    out[lay.origin + (back * CORES + other) * spans + place] = k
                    if back == 0 and other == 0:
                        out[lay.span_at + place] = k
                        out[lay.earlier_at + place] = k - start_of[k]
                        owner = target[k]
                        ahead = lax.rem(lax.div(owner, CORES) + chips - chip, chips)
                        turn = jnp.int32(0)
                        for m, other_hop in enumerate(hops):
                            turn = jnp.where(ahead == other_hop, jnp.int32(m), turn)
                        crossing = jnp.where(lax.rem(owner, CORES) == core, 0, 1)
                        out[lay.target_at + place] = owner
                        out[lay.sent_as + place] = turn * CORES + crossing


def make_tables(lay, spans, pages, ranks, prompt_spans, source, target, page_slot):
    smem = pl.BlockSpec(memory_space=pltpu.SMEM)
    return pl.pallas_call(
        functools.partial(tables_kernel, lay, spans, pages),
        out_shape=jax.ShapeDtypeStruct((lay.length,), jnp.int32),
        in_specs=[smem] * 5,
        out_specs=smem,
        scratch_shapes=[pltpu.SMEM((spans,), jnp.int32)] * 2,
        compiler_params=params(4),
        name="tables",
    )(ranks, prompt_spans, source, target, page_slot)


def head_norm_rope(u, gain, cosine, sine):
    mean_sq = jnp.mean(u * u, axis=-1, keepdims=True)
    u = u * lax.rsqrt(mean_sq + epsilon) * gain
    half = u.shape[-1] // 2
    return u * cosine + pltpu.roll(u, half, 1) * sine


def half_index(lay, sides, side):
    if sides == 1:
        return lambda t: 0
    if side == 0:
        return lambda t: t[lay.tensor_rank]
    return lambda t: 1 - t[lay.tensor_rank]


def summed_dot(lefts, rights):
    total = None
    for left, right in zip(lefts, rights):
        term = jnp.dot(left[...], right[...], preferred_element_type=jnp.float32)
        total = term if total is None else total + term
    return total


def kv_kernel(sides, blocks, table, *refs):
    refs = list(refs)
    take = lambda n: [refs.pop(0) for _ in range(n)]
    xs = [take(blocks) for _ in range(sides)]
    gains, wks, wvs = take(sides), take(sides), take(sides)
    kgain, cosine, sine = take(3)
    normed, (kv,) = take(sides), take(1)
    head = kgain.shape[1]
    width = sum(x[0].shape[1] for x in xs)

    @pl.when(pl.program_id(0) == 0)
    def _():
        at = 0
        for b in range(blocks):
            wide = [x[b][...].astype(jnp.float32) for x in xs]
            total = sum(jnp.sum(w * w, axis=-1, keepdims=True) for w in wide)
            factor = lax.rsqrt(total / width + epsilon)
            rows = xs[0][b].shape[0]
            for w, gain, to in zip(wide, gains, normed):
                to[at : at + rows] = (w * factor * gain[...].astype(jnp.float32)).astype(
                    jnp.bfloat16
                )
            at += rows

    keys = summed_dot(normed, wks).astype(jnp.bfloat16)
    gains = kgain[...].astype(jnp.float32)
    for h in range(keys.shape[1] // head):
        u = keys[:, h * head : (h + 1) * head].astype(jnp.float32)
        kv[0, :, h * head : (h + 1) * head] = head_norm_rope(
            u, gains, cosine[...], sine[...]
        ).astype(jnp.bfloat16)
    kv[1] = summed_dot(normed, wvs).astype(jnp.bfloat16)


def make_kv(lay, table, xs, gains, wk, wv, kgain, cosine, sine, part):
    sides, blocks = len(xs), len(xs[0])
    rows = sum(x.shape[0] for x in xs[0])
    widths = [x[0].shape[1] for x in xs]
    width, cols = wk.shape
    tile = 256 if cols % 256 == 0 else cols
    head = kgain.shape[1]
    fixed = lambda n, t: (0, 0)
    here = lambda n, t: (part, 0)
    weights = []
    for side in range(sides):
        index = half_index(lay, sides, side)
        weights.append(
            pl.BlockSpec((widths[side], tile), lambda n, t, index=index: (index(t), n))
        )
    return pl.pallas_call(
        functools.partial(kv_kernel, sides, blocks),
        grid_spec=pltpu.PrefetchScalarGridSpec(
            num_scalar_prefetch=1,
            grid=(cols // tile,),
            in_specs=[pl.BlockSpec(x.shape, fixed) for side in xs for x in side]
            + [pl.BlockSpec((1, w), fixed) for w in widths]
            + weights
            + weights
            + [
                pl.BlockSpec((1, head), fixed),
                pl.BlockSpec((rows, head), here),
                pl.BlockSpec((rows, head), here),
            ],
            out_specs=[pl.BlockSpec((rows, w), fixed) for w in widths]
            + [pl.BlockSpec((2, rows, tile), lambda n, t: (0, 0, n))],
        ),
        out_shape=[jax.ShapeDtypeStruct((rows, w), jnp.bfloat16) for w in widths]
        + [jax.ShapeDtypeStruct((2, rows, cols), jnp.bfloat16)],
        compiler_params=params(32),
        cost_estimate=cost(4 * rows * width * cols, 4 * width * cols + 4 * rows * width),
        name="keys_values",
    )(
        table, *[x for side in xs for x in side], *gains,
        *[in_hbm(wk)] * sides, *[in_hbm(wv)] * sides,
        kgain, cosine, sine,
    )


def q_kernel(sides, table, *refs):
    normed, wqs = refs[:sides], refs[sides : 2 * sides]
    qgain, cosine, sine, out = refs[2 * sides :]
    head = qgain.shape[1]
    lin = summed_dot(normed, wqs)
    gains = qgain[...].astype(jnp.float32)
    for h in range(lin.shape[1] // head):
        out[:, h * head : (h + 1) * head] = head_norm_rope(
            lin[:, h * head : (h + 1) * head], gains, cosine[...], sine[...]
        ).astype(jnp.bfloat16)


def make_q(lay, table, normed, wq, qgain, cosine, sine, part):
    sides = len(normed)
    rows = normed[0].shape[0]
    width, cols = wq.shape
    tile = 512 if cols % 512 == 0 else cols
    head = qgain.shape[1]
    fixed = lambda n, t: (0, 0)
    here = lambda n, t: (part, 0)
    weights = []
    for side in range(sides):
        index = half_index(lay, sides, side)
        weights.append(
            pl.BlockSpec(
                (normed[side].shape[1], tile), lambda n, t, index=index: (index(t), n)
            )
        )
    return pl.pallas_call(
        functools.partial(q_kernel, sides),
        grid_spec=pltpu.PrefetchScalarGridSpec(
            num_scalar_prefetch=1,
            grid=(cols // tile,),
            in_specs=[pl.BlockSpec(x.shape, fixed) for x in normed]
            + weights
            + [
                pl.BlockSpec((1, head), fixed),
                pl.BlockSpec((rows, head), here),
                pl.BlockSpec((rows, head), here),
            ],
            out_specs=pl.BlockSpec((rows, tile), lambda n, t: (0, n)),
        ),
        out_shape=jax.ShapeDtypeStruct((rows, cols), jnp.bfloat16),
        compiler_params=params(24),
        cost_estimate=cost(2 * rows * width * cols, 2 * width * cols + 2 * rows * (width + cols)),
        name="queries",
    )(table, *normed, *[in_hbm(wq)] * sides, qgain, cosine, sine)


def attention_kernel(lay, spans, most, per_kv, head, beside, owners, pages_each, table, *refs):
    q_refs = refs[:PARTS]
    kv_refs = refs[PARTS : PARTS + owners * PARTS]
    out, pages, keys, values, asked = refs[PARTS + owners * PARTS :]
    chips = lay.chips
    here, rows = kv_refs[0].shape[1], kv_refs[0].shape[2]
    group_rank = table[lay.group_rank]
    chip, core = lax.div(group_rank, CORES), lax.rem(group_rank, CORES)
    heads = range(beside)
    for p in range(PARTS):
        asked[p * here : (p + 1) * here] = q_refs[p][...]
    for o in range(owners):
        back, other = o // CORES, o % CORES
        owner = lax.rem(chip + chips - back, chips) * CORES + (core if other == 0 else 1 - core)
        at = pl.ds(pl.multiple_of(owner * rows, rows), rows)
        for p in range(PARTS):
            for i in range(here):
                k = table[lay.origin + o * spans + p * here + i]
                for h in heads:
                    lanes = slice(h * head, (h + 1) * head)
                    keys[h, k, at] = kv_refs[o * PARTS + p][0, i, :, lanes]
                    values[h, k, at] = kv_refs[o * PARTS + p][1, i, :, lanes]

    for i in range(pages_each):
        page = table[lay.page + group_rank * pages_each + i]
        k = lax.div(page, pages_each)
        at = pl.ds(pl.multiple_of(lax.rem(page, pages_each) * PAGE_ROWS, PAGE_ROWS), PAGE_ROWS)
        for h in heads:
            lanes = slice(h * head, (h + 1) * head)
            pages[i, 0, :, lanes] = keys[h, k, at]
            pages[i, 1, :, lanes] = values[h, k, at]

    scale = (1.0 / math.sqrt(head)) * math.log2(math.e)
    q_rows, k_rows = per_kv * rows, owners * rows
    row = lax.broadcasted_iota(jnp.int32, (q_rows, k_rows), 0)
    col = lax.broadcasted_iota(jnp.int32, (q_rows, k_rows), 1)
    allowed = col <= group_rank * rows + row % rows

    def one_place(place, carry):
        k = table[lay.span_at + place]
        earlier = table[lay.earlier_at + place]

        def with_earlier(count):
            scores = [[] for _ in heads]
            for h in heads:
                queries = jnp.concatenate(
                    [
                        asked[place, :, (h * per_kv + g) * head : (h * per_kv + g + 1) * head]
                        for g in range(per_kv)
                    ],
                    axis=0,
                )
                for back in range(count + 1):
                    s = lax.dot_general(
                        queries, keys[h, k - back], (((1,), (1,)), ((), ())),
                        preferred_element_type=jnp.float32,
                    )
                    if back == 0:
                        s = jnp.where(allowed, s, very_negative)
                    scores[h].append(s)
            for h in heads:
                best = functools.reduce(jnp.maximum, scores[h])
                best = jnp.max(best, axis=-1, keepdims=True)
                shifted = best * scale
                weights = [jnp.exp2(s * scale - shifted) for s in scores[h]]
                total = jnp.sum(
                    functools.reduce(lambda a, b: a + b, weights), axis=-1, keepdims=True
                )
                summed = None
                for back, w in enumerate(weights):
                    term = jnp.dot(
                        w.astype(jnp.bfloat16), values[h, k - back],
                        preferred_element_type=jnp.float32,
                    )
                    summed = term if summed is None else summed + term
                result = (summed / total).astype(jnp.bfloat16)
                for g in range(per_kv):
                    at = (h * per_kv + g) * head
                    out[place, :, at : at + head] = result[g * rows : (g + 1) * rows]

        for count in range(most):
            pl.when(earlier == count)(functools.partial(with_earlier, count))
        return carry

    lax.fori_loop(0, spans, one_place, 0)


def make_attention(lay, most, table, queries, gathered, per_kv, head, pages_each, first, count):
    here, rows, cols = queries[0].shape
    spans = here * PARTS
    owners = len(gathered)
    at = first // count
    q_spec = pl.BlockSpec((here, rows, count * per_kv * head), lambda h, t: (0, 0, at + h))
    kv_spec = pl.BlockSpec((2, here, rows, count * head), lambda h, t: (0, 0, 0, at + h))
    flat = [x for origin in gathered for x in origin]
    all_rows = spans * rows
    pairs = 2.2 * all_rows * owners * rows * per_kv * count
    return pl.pallas_call(
        functools.partial(
            attention_kernel, lay, spans, most, per_kv, head, count, owners, pages_each
        ),
        grid_spec=pltpu.PrefetchScalarGridSpec(
            num_scalar_prefetch=1,
            grid=(1,),
            in_specs=[q_spec] * PARTS + [kv_spec] * len(flat),
            out_specs=[
                pl.BlockSpec((spans, rows, count * per_kv * head), lambda h, t: (0, 0, h)),
                pl.BlockSpec((pages_each, 2, PAGE_ROWS, count * head), lambda h, t: (0, 0, 0, h)),
            ],
            scratch_shapes=[pltpu.VMEM((count, spans, owners * rows, head), jnp.bfloat16)] * 2
            + [pltpu.VMEM((spans, rows, count * per_kv * head), jnp.bfloat16)],
        ),
        out_shape=[
            jax.ShapeDtypeStruct((spans, rows, count * per_kv * head), jnp.bfloat16),
            jax.ShapeDtypeStruct((pages_each, 2, PAGE_ROWS, count * head), jnp.bfloat16),
        ],
        compiler_params=params(32),
        cost_estimate=cost(
            4 * pairs * head, 4 * all_rows * cols + 2 * len(flat) * flat[0].size, pairs
        ),
        name="attention",
    )(table, *queries, *flat)


def project_kernel(pieces, follows, tile, table, *refs):
    attended, wo, outs = refs[:pieces], refs[pieces], refs[pieces + 1 + follows :]
    total, at = None, 0
    for piece in attended:
        depth = piece.shape[1]
        term = jnp.dot(piece[...], wo[at : at + depth], preferred_element_type=jnp.float32)
        total = term if total is None else total + term
        at += depth
    total = total.astype(jnp.bfloat16)
    step = 0
    for out in outs:
        for at in range(0, out.shape[1], tile):

            @pl.when(pl.program_id(0) == step)
            def _(out=out, at=at):
                out[:, at : at + tile] = total

            step += 1


def make_projection(lay, table, attended, wo, tile, first, widths, name, follows=()):
    rows = attended[0].shape[0]
    depth = wo.shape[0]
    count = sum(widths)
    return pl.pallas_call(
        functools.partial(project_kernel, len(attended), len(follows), tile),
        grid_spec=pltpu.PrefetchScalarGridSpec(
            num_scalar_prefetch=1,
            grid=(count,),
            in_specs=[pl.BlockSpec(x.shape, lambda n, t: (0, 0)) for x in attended]
            + [pl.BlockSpec((depth, tile), lambda n, t: (0, first(t[lay.tensor_rank]) + n))]
            + [pl.BlockSpec(memory_space=pl.ANY)] * len(follows),
            out_specs=[pl.BlockSpec((rows, w * tile), lambda n, t: (0, 0)) for w in widths],
        ),
        out_shape=[jax.ShapeDtypeStruct((rows, w * tile), jnp.bfloat16) for w in widths],
        compiler_params=params(20),
        cost_estimate=cost(
            2 * rows * depth * count * tile, 2 * (rows * depth + (rows + depth) * count * tile)
        ),
        name=name,
    )(table, *attended, in_hbm(wo), *follows)


def add_kernel(lay, blocks, table, *refs):
    x_refs, own, received = refs[:blocks], refs[blocks], refs[blocks + 1]
    outs, moved = refs[blocks + 2 : -1], refs[-1]
    rows = moved.shape[1]
    place = 0
    for x in x_refs:
        for at in range(0, x.shape[0], rows):
            summed = own[place].astype(jnp.float32) + received[place].astype(jnp.float32)
            moved[table[lay.sent_as + place]] = (
                x[at : at + rows].astype(jnp.float32) + summed
            ).astype(jnp.bfloat16)
            place += 1
    for n, out in enumerate(outs):
        for flip in range(CORES):
            out[flip] = moved[n * CORES + flip]


def make_sum(lay, table, arrived, own, received, first):
    spans, rows, cols = received.shape
    chunk = first // cols
    whole = lambda n, t: (0, 0, 0)
    return pl.pallas_call(
        functools.partial(add_kernel, lay, len(arrived)),
        grid_spec=pltpu.PrefetchScalarGridSpec(
            num_scalar_prefetch=1,
            grid=(1,),
            in_specs=[pl.BlockSpec((x.shape[0], cols), lambda n, t: (0, chunk)) for x in arrived]
            + [pl.BlockSpec((spans, rows, cols), whole)] * 2,
            out_specs=[pl.BlockSpec((CORES, rows, cols), whole)] * lay.chips,
            scratch_shapes=[pltpu.VMEM((spans, rows, cols), jnp.bfloat16)],
        ),
        out_shape=[jax.ShapeDtypeStruct((CORES, rows, cols), jnp.bfloat16)] * lay.chips,
        compiler_params=params(12),
        cost_estimate=cost(3 * spans * rows * cols, 8 * spans * rows * cols),
        name="residual",
    )(table, *arrived, own, received)


def place_kernel(lay, chunks, table, *refs):
    out = refs[-1]
    chips = lay.chips
    group_rank = table[lay.group_rank]
    chip, core = lax.div(group_rank, CORES), lax.rem(group_rank, CORES)
    first = 0
    for c in range(chunks):
        same, swapped = refs[c * (chips + 1) : (c + 1) * (chips + 1) - 1], refs[(c + 1) * (chips + 1) - 1]
        rows, cols = swapped.shape[1:]
        for n, hop in enumerate(hop_order(chips)):
            owner = lax.rem(chip + chips - hop, chips) * CORES
            for block, at_core in ((same[n][0], core), (swapped[n], 1 - core)):
                at = pl.multiple_of((owner + at_core) * rows, rows)
                out[pl.ds(at, rows), first : first + cols] = block
        first += cols


def make_placed(lay, table, pieces, cols):
    flat = [x for same, swapped in pieces for x in [*same, swapped]]
    chips, rows, _ = pieces[0][1].shape
    shape = (chips * CORES * rows, cols)
    return pl.pallas_call(
        functools.partial(place_kernel, lay, len(pieces)),
        grid_spec=pltpu.PrefetchScalarGridSpec(
            num_scalar_prefetch=1,
            grid=(1,),
            in_specs=[pl.BlockSpec(x.shape, lambda n, t: (0, 0, 0)) for x in flat],
            out_specs=pl.BlockSpec(shape, lambda n, t: (0, 0)),
        ),
        out_shape=jax.ShapeDtypeStruct(shape, jnp.bfloat16),
        compiler_params=params(16),
        cost_estimate=cost(0, 4 * shape[0] * shape[1]),
        name="placed",
    )(table, *flat)


def rope_tables(earlier, span_len, first_row, rows, head):
    half = head // 2
    freqs = jnp.power(
        jnp.float32(rope_base), -jnp.arange(half, dtype=jnp.float32) * 2.0 / head
    )
    at = earlier[:, None] * span_len + first_row + jnp.arange(rows, dtype=jnp.int32)[None, :]
    angles = at.reshape(-1).astype(jnp.float32)[:, None] * freqs[None, :]
    cosine, sine = jnp.cos(angles), jnp.sin(angles)
    return (
        jnp.concatenate([cosine, cosine], axis=1),
        jnp.concatenate([-sine, sine], axis=1),
    )


def after(x, done):
    return lax.optimization_barrier((x, done))[0]


def shift(x, owners, hop, flip):
    chips = owners // CORES
    pairs = [
        (z * CORES + c, (z + hop) % chips * CORES + (c ^ flip))
        for z in range(chips)
        for c in range(CORES)
    ]
    return lax.ppermute(x, "group", pairs)


def local(
    hidden_in, ln_gain, wq, wk, wv, q_gain, key_norm_gain, wo,
    prompt_spans, span_source, span_target, page_slot,
):
    _, span_len, cols = hidden_in.shape
    tensor_size = lax.axis_size("tensor")
    owners = lax.axis_size("group")
    tensor_rank = lax.axis_index("tensor")
    group_rank = lax.axis_index("group")
    chips = owners // CORES
    head = q_gain.shape[0]
    rows = span_len // owners
    pages_each = span_len // PAGE_ROWS
    spans = span_source.shape[0]
    here = spans // PARTS
    most = min(spans - (prompt_spans.shape[0] - 1), spans // 2)
    kv_cols = wk.shape[1]
    paired = tensor_size == 2
    swap = [(0, 1), (1, 0)]
    lay = Layout(spans, spans * pages_each, owners)

    if kv_cols < head:
        share = head // kv_cols
        sets = [list(range(i, i + share)) for i in range(0, tensor_size, share)]
        wk, wv = [
            lax.all_gather(w, "tensor", axis=1, tiled=True, axis_index_groups=sets)
            for w in (wk, wv)
        ]
    per_kv = wq.shape[1] // max(head, wk.shape[1])

    chip, core = group_rank // CORES, group_rank % CORES
    split = hidden_in.reshape(owners, rows, cols)

    def rows_for(hop, flip):
        to = lax.rem(chip + hop, chips) * CORES + lax.rem(core + flip, CORES)
        return lax.dynamic_index_in_dim(split, to, 0, keepdims=False)

    cross = lambda x: lax.ppermute(x, "tensor", swap)

    hops = hop_order(chips)
    paired_hops = hops[2:]
    near = [rows_for(hop, flip) for hop in hops[1:2] for flip in range(CORES)]
    near = [shift(x, owners, hops[1], flip) for flip, x in enumerate(near)]
    swapped = shift(
        jnp.stack([rows_for(hop, 1) for hop in hops[:1] + paired_hops]), owners, 0, 1
    )
    arrived = [rows_for(0, 0), swapped[0]] + near
    moves = []
    for n, hop in enumerate(paired_hops):
        pair = [rows_for(hop, 0), swapped[1 + n]]
        if n < len(paired_hops) - 1:
            moves.append((hop, jnp.concatenate(pair)))
        else:
            moves += [(hop, block) for block in pair]

    ranks = jnp.stack([group_rank, tensor_rank]).astype(jnp.int32)
    table = make_tables(
        lay, spans, spans * pages_each, ranks, prompt_spans, span_source, span_target, page_slot
    )
    earlier = table[lay.earlier_at : lay.earlier_at + spans]
    cosine, sine = rope_tables(earlier, span_len, group_rank * rows, rows, head)

    crossed = [cross(x) for x in arrived] if paired else []
    if paired:
        gain = ln_gain[None]
        gains = [gain, cross(after(gain, swapped))]
    else:
        gains = [lax.all_gather(ln_gain, "tensor", axis=0, tiled=True)[None]]

    kvs, norms = [], []

    def make_part(own_rows, crossed_rows):
        if paired:
            xs = [own_rows, [in_hbm(x) for x in crossed_rows]]
        else:
            xs = [[lax.all_gather(jnp.concatenate(own_rows), "tensor", axis=1, tiled=True)]]
        *normed, kv = make_kv(
            lay, table, xs, gains, wk, wv, key_norm_gain[None], cosine, sine, len(kvs)
        )
        kvs.append([kv.reshape(2, here, rows, kv.shape[2])])
        norms.append(normed)

    def one_back(p, done=()):
        kvs[p].append(shift(after(kvs[p][-1], done), owners, 1, 0))

    begun = 0
    for n in range(len(moves) + 1):
        if n:
            hop, block = moves[n - 1]
            if paired:
                landed = arrived[-1:] if n > 1 else near
                matching = crossed[2 * n - 2 : 2 * n] if n < 3 else crossed[n + 1]
                block = after(block, (landed, matching, gains))
            arrived.append(shift(block, owners, hop, 0))
            if paired:
                block = arrived[-1]
                if n == len(moves) and kvs:
                    block = after(block, kvs[0][0])
                crossed.append(cross(block))
        if sum(x.shape[0] for x in arrived[begun:]) == here * rows:
            make_part(arrived[begun:], crossed[begun:])
            begun = len(arrived)
            for _ in range(min(2, chips - 1) if len(kvs) == 1 else min(1, chips - 1)):
                one_back(len(kvs) - 1)

    queries, done = [], kvs[1][0]
    for p in range(PARTS):
        made = make_q(
            lay, table, norms[p], wq, after(q_gain[None], done), cosine, sine, p
        )
        queries.append(made.reshape(here, rows, made.shape[1]))
        done = queries[-1]
    for p in range(PARTS):
        while len(kvs[p]) < chips:
            one_back(p, queries[p])
    gathered = []
    for back in range(chips):
        gathered.append([kv[back] for kv in kvs])
        gathered.append([shift(kv[back], owners, 0, 1) for kv in kvs])

    own_kv = wk.shape[1] // head
    sets = [own_kv // 2] * 2 if own_kv % 2 == 0 else [1] * own_kv
    attended, pages, first = [], [], 0
    for count in sets:
        made, cut = make_attention(
            lay, most, table, queries, gathered, per_kv, head, pages_each, first, count
        )
        attended.append(made.reshape(spans * rows, -1))
        pages.append(cut)
        first += count

    if paired:
        tile = 512 if cols % 512 == 0 else cols
        tiles = cols // tile
        widths = [2, 2, 1] if tiles == 5 else [tiles]
        others = [cross(pages[0])]
        project = functools.partial(make_projection, lay, table, attended, wo, tile)
        send = project(lambda r: (1 - r) * tiles, widths[:1], "send_part", (others[0],))
        if widths[1:]:
            send += project(
                lambda r: (1 - r) * tiles + widths[0], widths[1:], "send_part", (send[0],)
            )
        own = project(lambda r: r * tiles, widths, "own_part", (send[-1],))
        pieces, received, landed, first = [], [], [], 0
        for n, sent in enumerate(send):
            if n:
                sent = after(sent, (received[-1], own, landed[-2:-1]))
            received.append(cross(sent))
            moved = make_sum(
                lay, table, arrived, own[n].reshape(spans, rows, -1),
                received[-1].reshape(spans, rows, -1), first,
            )
            same = [
                shift(x, owners, hop, 0) if hop else x
                for hop, x in zip(hop_order(chips), moved)
            ]
            landed.append(same)
            pieces.append(same)
            first += sent.shape[1]
        others += [cross(after(cut, moved[0])) for cut in pages[1:]]
        low = [jnp.where(tensor_rank == 0, a, b) for a, b in zip(pages, others)]
        high = [jnp.where(tensor_rank == 0, b, a) for a, b in zip(pages, others)]
        cache = jnp.concatenate(low + high, axis=3)
        for n, same in enumerate(pieces):
            flipped = jnp.concatenate([x[1:] for x in same])
            if n == len(pieces) - 2:
                flipped = after(flipped, others)
            pieces[n] = (same, shift(flipped, owners, 0, 1))
        mixed = make_placed(lay, after(table, cache), pieces, cols).reshape(1, span_len, cols)
    else:
        pages = jnp.concatenate(pages, axis=3)
        attended = jnp.concatenate(attended, axis=1)
        if kv_cols < head:
            pages = lax.dynamic_slice_in_dim(
                pages, lax.rem(tensor_rank, head // kv_cols) * kv_cols, kv_cols, 3
            )
        cache = lax.all_gather(pages, "tensor", axis=3, tiled=True)
        partial = jnp.dot(attended, wo, preferred_element_type=jnp.float32)
        summed = lax.psum_scatter(
            partial.astype(jnp.bfloat16), "tensor", scatter_dimension=1, tiled=True
        )
        summed = summed.reshape(spans, rows, cols).astype(jnp.float32)
        x = jnp.concatenate(arrived).reshape(spans, rows, cols).astype(jnp.float32)
        moved = (x + summed).astype(jnp.bfloat16)
        targets = table[lay.target_at : lay.target_at + spans]
        moved = jnp.zeros_like(moved).at[targets].set(moved, unique_indices=True)
        moved = lax.all_to_all(moved, "group", split_axis=0, concat_axis=0, tiled=True)
        mixed = moved.reshape(1, span_len, cols)
    return (mixed, cache)


def solution(mesh):
    in_specs = (
        P(("replica", "group"), None, "tensor"),
        P("tensor"),
        P(None, "tensor"),
        P(None, "tensor"),
        P(None, "tensor"),
        P(),
        P(),
        P("tensor", None),
        P("replica"),
        P("replica"),
        P("replica"),
        P("replica"),
    )
    out_specs = (P(("replica", "group"), None, "tensor"), P(("replica", "group"), None, None, None))
    return jax.shard_map(local, mesh=mesh, in_specs=in_specs, out_specs=out_specs, check_vma=False)
```

```python
import functools
import math

import jax
import jax.numpy as jnp
from jax import lax
from jax.experimental import pallas as pl
from jax.experimental.pallas import tpu as pltpu
from jax.sharding import PartitionSpec as P

PAGE_ROWS = 128
epsilon = 1e-06
rope_base = 1000000.0
very_negative = -1e30
PARTS = 2
CORES = 2
SHARE = 0.02


def params(mebibytes):
    return pltpu.CompilerParams(vmem_limit_bytes=mebibytes * 1024 * 1024)


def in_hbm(x):
    return pltpu.with_memory_space_constraint(x, pltpu.HBM)


def cost(flops, moved, transcendentals=0):
    return pl.CostEstimate(
        flops=int(flops * SHARE),
        bytes_accessed=int(moved * SHARE),
        transcendentals=int(transcendentals * SHARE),
    )


def hop_order(chips):
    return [0, 1, chips - 1] + list(range(2, chips - 1)) if chips > 2 else list(range(chips))


class Layout:
    def __init__(self, spans, pages, owners):
        self.chips = owners // CORES
        self.span_at = 0
        self.earlier_at = self.span_at + spans
        self.target_at = self.earlier_at + spans
        self.sent_as = self.target_at + spans
        self.page = self.sent_as + spans
        self.origin = self.page + pages
        self.group_rank = self.origin + owners * spans
        self.tensor_rank = self.group_rank + 1
        self.length = self.tensor_rank + 1


def tables_kernel(lay, spans, pages, ranks, prompt_spans, source, target, page_slot, out, span_of, start_of):
    chips = lay.chips
    group_rank = ranks[0]
    out[lay.group_rank] = group_rank
    out[lay.tensor_rank] = ranks[1]
    for k in range(spans):
        start = jnp.int32(0)
        begin = jnp.int32(0)
        for p in range(prompt_spans.shape[0]):
            start = jnp.where(begin <= k, begin, start)
            begin = begin + prompt_spans[p]
        start_of[k] = start
        span_of[source[k]] = jnp.int32(k)
    for p in range(pages):
        out[lay.page + page_slot[p]] = jnp.int32(p)
    chip, core = lax.div(group_rank, CORES), lax.rem(group_rank, CORES)
    hops = hop_order(chips)
    for back in range(chips):
        for other in range(CORES):
            at_chip = lax.rem(chip + chips - back, chips)
            at_core = jnp.where(other == 0, core, 1 - core)
            for n, hop in enumerate(hops):
                for flip in range(CORES):
                    from_chip = lax.rem(at_chip + chips - hop, chips)
                    from_core = jnp.where(flip == 0, at_core, 1 - at_core)
                    k = span_of[from_chip * CORES + from_core]
                    place = n * CORES + flip
                    out[lay.origin + (back * CORES + other) * spans + place] = k
                    if back == 0 and other == 0:
                        out[lay.span_at + place] = k
                        out[lay.earlier_at + place] = k - start_of[k]
                        owner = target[k]
                        ahead = lax.rem(lax.div(owner, CORES) + chips - chip, chips)
                        turn = jnp.int32(0)
                        for m, other_hop in enumerate(hops):
                            turn = jnp.where(ahead == other_hop, jnp.int32(m), turn)
                        crossing = jnp.where(lax.rem(owner, CORES) == core, 0, 1)
                        out[lay.target_at + place] = owner
                        out[lay.sent_as + place] = turn * CORES + crossing


def make_tables(lay, spans, pages, ranks, prompt_spans, source, target, page_slot):
    smem = pl.BlockSpec(memory_space=pltpu.SMEM)
    return pl.pallas_call(
        functools.partial(tables_kernel, lay, spans, pages),
        out_shape=jax.ShapeDtypeStruct((lay.length,), jnp.int32),
        in_specs=[smem] * 5,
        out_specs=smem,
        scratch_shapes=[pltpu.SMEM((spans,), jnp.int32)] * 2,
        compiler_params=params(4),
        name="tables",
    )(ranks, prompt_spans, source, target, page_slot)


def head_norm_rope(u, gain, cosine, sine):
    mean_sq = jnp.mean(u * u, axis=-1, keepdims=True)
    u = u * lax.rsqrt(mean_sq + epsilon) * gain
    half = u.shape[-1] // 2
    return u * cosine + pltpu.roll(u, half, 1) * sine


def half_index(lay, sides, side):
    if sides == 1:
        return lambda t: 0
    if side == 0:
        return lambda t: t[lay.tensor_rank]
    return lambda t: 1 - t[lay.tensor_rank]


def summed_dot(lefts, rights):
    total = None
    for left, right in zip(lefts, rights):
        term = jnp.dot(left[...], right[...], preferred_element_type=jnp.float32)
        total = term if total is None else total + term
    return total


def kv_kernel(sides, blocks, table, *refs):
    refs = list(refs)
    take = lambda n: [refs.pop(0) for _ in range(n)]
    xs = [take(blocks) for _ in range(sides)]
    gains, wks, wvs = take(sides), take(sides), take(sides)
    kgain, cosine, sine = take(3)
    normed, (kv,) = take(sides), take(1)
    head = kgain.shape[1]
    width = sum(x[0].shape[1] for x in xs)

    @pl.when(pl.program_id(0) == 0)
    def _():
        at = 0
        for b in range(blocks):
            wide = [x[b][...].astype(jnp.float32) for x in xs]
            total = sum(jnp.sum(w * w, axis=-1, keepdims=True) for w in wide)
            factor = lax.rsqrt(total / width + epsilon)
            rows = xs[0][b].shape[0]
            for w, gain, to in zip(wide, gains, normed):
                to[at : at + rows] = (w * factor * gain[...].astype(jnp.float32)).astype(
                    jnp.bfloat16
                )
            at += rows

    keys = summed_dot(normed, wks).astype(jnp.bfloat16)
    gains = kgain[...].astype(jnp.float32)
    for h in range(keys.shape[1] // head):
        u = keys[:, h * head : (h + 1) * head].astype(jnp.float32)
        kv[0, :, h * head : (h + 1) * head] = head_norm_rope(
            u, gains, cosine[...], sine[...]
        ).astype(jnp.bfloat16)
    kv[1] = summed_dot(normed, wvs).astype(jnp.bfloat16)


def make_kv(lay, table, xs, gains, wk, wv, kgain, cosine, sine, part):
    sides, blocks = len(xs), len(xs[0])
    rows = sum(x.shape[0] for x in xs[0])
    widths = [x[0].shape[1] for x in xs]
    width, cols = wk.shape
    tile = 256 if cols % 256 == 0 else cols
    head = kgain.shape[1]
    fixed = lambda n, t: (0, 0)
    here = lambda n, t: (part, 0)
    weights = []
    for side in range(sides):
        index = half_index(lay, sides, side)
        weights.append(
            pl.BlockSpec((widths[side], tile), lambda n, t, index=index: (index(t), n))
        )
    return pl.pallas_call(
        functools.partial(kv_kernel, sides, blocks),
        grid_spec=pltpu.PrefetchScalarGridSpec(
            num_scalar_prefetch=1,
            grid=(cols // tile,),
            in_specs=[pl.BlockSpec(x.shape, fixed) for side in xs for x in side]
            + [pl.BlockSpec((1, w), fixed) for w in widths]
            + weights
            + weights
            + [
                pl.BlockSpec((1, head), fixed),
                pl.BlockSpec((rows, head), here),
                pl.BlockSpec((rows, head), here),
            ],
            out_specs=[pl.BlockSpec((rows, w), fixed) for w in widths]
            + [pl.BlockSpec((2, rows, tile), lambda n, t: (0, 0, n))],
        ),
        out_shape=[jax.ShapeDtypeStruct((rows, w), jnp.bfloat16) for w in widths]
        + [jax.ShapeDtypeStruct((2, rows, cols), jnp.bfloat16)],
        compiler_params=params(32),
        cost_estimate=cost(4 * rows * width * cols, 4 * width * cols + 4 * rows * width),
        name="keys_values",
    )(
        table, *[x for side in xs for x in side], *gains,
        *[in_hbm(wk)] * sides, *[in_hbm(wv)] * sides,
        kgain, cosine, sine,
    )


def q_kernel(sides, table, *refs):
    normed, wqs = refs[:sides], refs[sides : 2 * sides]
    qgain, cosine, sine, out = refs[2 * sides :]
    head = qgain.shape[1]
    lin = summed_dot(normed, wqs)
    gains = qgain[...].astype(jnp.float32)
    for h in range(lin.shape[1] // head):
        out[:, h * head : (h + 1) * head] = head_norm_rope(
            lin[:, h * head : (h + 1) * head], gains, cosine[...], sine[...]
        ).astype(jnp.bfloat16)


def make_q(lay, table, normed, wq, qgain, cosine, sine, part):
    sides = len(normed)
    rows = normed[0].shape[0]
    width, cols = wq.shape
    tile = 512 if cols % 512 == 0 else cols
    head = qgain.shape[1]
    fixed = lambda n, t: (0, 0)
    here = lambda n, t: (part, 0)
    weights = []
    for side in range(sides):
        index = half_index(lay, sides, side)
        weights.append(
            pl.BlockSpec(
                (normed[side].shape[1], tile), lambda n, t, index=index: (index(t), n)
            )
        )
    return pl.pallas_call(
        functools.partial(q_kernel, sides),
        grid_spec=pltpu.PrefetchScalarGridSpec(
            num_scalar_prefetch=1,
            grid=(cols // tile,),
            in_specs=[pl.BlockSpec(x.shape, fixed) for x in normed]
            + weights
            + [
                pl.BlockSpec((1, head), fixed),
                pl.BlockSpec((rows, head), here),
                pl.BlockSpec((rows, head), here),
            ],
            out_specs=pl.BlockSpec((rows, tile), lambda n, t: (0, n)),
        ),
        out_shape=jax.ShapeDtypeStruct((rows, cols), jnp.bfloat16),
        compiler_params=params(24),
        cost_estimate=cost(2 * rows * width * cols, 2 * width * cols + 2 * rows * (width + cols)),
        name="queries",
    )(table, *normed, *[in_hbm(wq)] * sides, qgain, cosine, sine)


def attention_kernel(lay, spans, most, per_kv, head, beside, owners, pages_each, table, *refs):
    q_refs = refs[:PARTS]
    kv_refs = refs[PARTS : PARTS + owners * PARTS]
    out, pages, keys, values, asked = refs[PARTS + owners * PARTS :]
    chips = lay.chips
    here, rows = kv_refs[0].shape[1], kv_refs[0].shape[2]
    group_rank = table[lay.group_rank]
    chip, core = lax.div(group_rank, CORES), lax.rem(group_rank, CORES)
    heads = range(beside)
    for p in range(PARTS):
        asked[p * here : (p + 1) * here] = q_refs[p][...]
    for o in range(owners):
        back, other = o // CORES, o % CORES
        owner = lax.rem(chip + chips - back, chips) * CORES + (core if other == 0 else 1 - core)
        at = pl.ds(pl.multiple_of(owner * rows, rows), rows)
        for p in range(PARTS):
            for i in range(here):
                k = table[lay.origin + o * spans + p * here + i]
                for h in heads:
                    lanes = slice(h * head, (h + 1) * head)
                    keys[h, k, at] = kv_refs[o * PARTS + p][0, i, :, lanes]
                    values[h, k, at] = kv_refs[o * PARTS + p][1, i, :, lanes]

    for i in range(pages_each):
        page = table[lay.page + group_rank * pages_each + i]
        k = lax.div(page, pages_each)
        at = pl.ds(pl.multiple_of(lax.rem(page, pages_each) * PAGE_ROWS, PAGE_ROWS), PAGE_ROWS)
        for h in heads:
            lanes = slice(h * head, (h + 1) * head)
            pages[i, 0, :, lanes] = keys[h, k, at]
            pages[i, 1, :, lanes] = values[h, k, at]

    scale = (1.0 / math.sqrt(head)) * math.log2(math.e)
    q_rows, k_rows = per_kv * rows, owners * rows
    row = lax.broadcasted_iota(jnp.int32, (q_rows, k_rows), 0)
    col = lax.broadcasted_iota(jnp.int32, (q_rows, k_rows), 1)
    allowed = col <= group_rank * rows + row % rows

    def one_place(place, carry):
        k = table[lay.span_at + place]
        earlier = table[lay.earlier_at + place]

        def with_earlier(count):
            scores = [[] for _ in heads]
            for h in heads:
                queries = jnp.concatenate(
                    [
                        asked[place, :, (h * per_kv + g) * head : (h * per_kv + g + 1) * head]
                        for g in range(per_kv)
                    ],
                    axis=0,
                )
                for back in range(count + 1):
                    s = lax.dot_general(
                        queries, keys[h, k - back], (((1,), (1,)), ((), ())),
                        preferred_element_type=jnp.float32,
                    )
                    if back == 0:
                        s = jnp.where(allowed, s, very_negative)
                    scores[h].append(s)
            for h in heads:
                best = functools.reduce(jnp.maximum, scores[h])
                best = jnp.max(best, axis=-1, keepdims=True)
                shifted = best * scale
                weights = [jnp.exp2(s * scale - shifted) for s in scores[h]]
                total = jnp.sum(
                    functools.reduce(lambda a, b: a + b, weights), axis=-1, keepdims=True
                )
                summed = None
                for back, w in enumerate(weights):
                    term = jnp.dot(
                        w.astype(jnp.bfloat16), values[h, k - back],
                        preferred_element_type=jnp.float32,
                    )
                    summed = term if summed is None else summed + term
                result = (summed / total).astype(jnp.bfloat16)
                for g in range(per_kv):
                    at = (h * per_kv + g) * head
                    out[place, :, at : at + head] = result[g * rows : (g + 1) * rows]

        for count in range(most):
            pl.when(earlier == count)(functools.partial(with_earlier, count))
        return carry

    lax.fori_loop(0, spans, one_place, 0)


def make_attention(lay, most, table, queries, gathered, per_kv, head, pages_each, first, count):
    here, rows, cols = queries[0].shape
    spans = here * PARTS
    owners = len(gathered)
    at = first // count
    q_spec = pl.BlockSpec((here, rows, count * per_kv * head), lambda h, t: (0, 0, at + h))
    kv_spec = pl.BlockSpec((2, here, rows, count * head), lambda h, t: (0, 0, 0, at + h))
    flat = [x for origin in gathered for x in origin]
    all_rows = spans * rows
    pairs = 2.2 * all_rows * owners * rows * per_kv * count
    return pl.pallas_call(
        functools.partial(
            attention_kernel, lay, spans, most, per_kv, head, count, owners, pages_each
        ),
        grid_spec=pltpu.PrefetchScalarGridSpec(
            num_scalar_prefetch=1,
            grid=(1,),
            in_specs=[q_spec] * PARTS + [kv_spec] * len(flat),
            out_specs=[
                pl.BlockSpec((spans, rows, count * per_kv * head), lambda h, t: (0, 0, h)),
                pl.BlockSpec((pages_each, 2, PAGE_ROWS, count * head), lambda h, t: (0, 0, 0, h)),
            ],
            scratch_shapes=[pltpu.VMEM((count, spans, owners * rows, head), jnp.bfloat16)] * 2
            + [pltpu.VMEM((spans, rows, count * per_kv * head), jnp.bfloat16)],
        ),
        out_shape=[
            jax.ShapeDtypeStruct((spans, rows, count * per_kv * head), jnp.bfloat16),
            jax.ShapeDtypeStruct((pages_each, 2, PAGE_ROWS, count * head), jnp.bfloat16),
        ],
        compiler_params=params(32),
        cost_estimate=cost(
            4 * pairs * head, 4 * all_rows * cols + 2 * len(flat) * flat[0].size, pairs
        ),
        name="attention",
    )(table, *queries, *flat)


def project_kernel(pieces, follows, tile, table, *refs):
    attended, wo, outs = refs[:pieces], refs[pieces], refs[pieces + 1 + follows :]
    total, at = None, 0
    for piece in attended:
        depth = piece.shape[1]
        term = jnp.dot(piece[...], wo[at : at + depth], preferred_element_type=jnp.float32)
        total = term if total is None else total + term
        at += depth
    total = total.astype(jnp.bfloat16)
    step = 0
    for out in outs:
        for at in range(0, out.shape[1], tile):

            @pl.when(pl.program_id(0) == step)
            def _(out=out, at=at):
                out[:, at : at + tile] = total

            step += 1


def make_projection(lay, table, attended, wo, tile, first, widths, name, follows=()):
    rows = attended[0].shape[0]
    depth = wo.shape[0]
    count = sum(widths)
    return pl.pallas_call(
        functools.partial(project_kernel, len(attended), len(follows), tile),
        grid_spec=pltpu.PrefetchScalarGridSpec(
            num_scalar_prefetch=1,
            grid=(count,),
            in_specs=[pl.BlockSpec(x.shape, lambda n, t: (0, 0)) for x in attended]
            + [pl.BlockSpec((depth, tile), lambda n, t: (0, first(t[lay.tensor_rank]) + n))]
            + [pl.BlockSpec(memory_space=pl.ANY)] * len(follows),
            out_specs=[pl.BlockSpec((rows, w * tile), lambda n, t: (0, 0)) for w in widths],
        ),
        out_shape=[jax.ShapeDtypeStruct((rows, w * tile), jnp.bfloat16) for w in widths],
        compiler_params=params(20),
        cost_estimate=cost(
            2 * rows * depth * count * tile, 2 * (rows * depth + (rows + depth) * count * tile)
        ),
        name=name,
    )(table, *attended, in_hbm(wo), *follows)


def add_kernel(lay, blocks, table, *refs):
    x_refs, own, received = refs[:blocks], refs[blocks], refs[blocks + 1]
    outs, moved = refs[blocks + 2 : -1], refs[-1]
    rows = moved.shape[1]
    place = 0
    for x in x_refs:
        for at in range(0, x.shape[0], rows):
            summed = own[place].astype(jnp.float32) + received[place].astype(jnp.float32)
            moved[table[lay.sent_as + place]] = (
                x[at : at + rows].astype(jnp.float32) + summed
            ).astype(jnp.bfloat16)
            place += 1
    for n, out in enumerate(outs):
        for flip in range(CORES):
            out[flip] = moved[n * CORES + flip]


def make_sum(lay, table, arrived, own, received, first):
    spans, rows, cols = received.shape
    chunk = first // cols
    whole = lambda n, t: (0, 0, 0)
    return pl.pallas_call(
        functools.partial(add_kernel, lay, len(arrived)),
        grid_spec=pltpu.PrefetchScalarGridSpec(
            num_scalar_prefetch=1,
            grid=(1,),
            in_specs=[pl.BlockSpec((x.shape[0], cols), lambda n, t: (0, chunk)) for x in arrived]
            + [pl.BlockSpec((spans, rows, cols), whole)] * 2,
            out_specs=[pl.BlockSpec((CORES, rows, cols), whole)] * lay.chips,
            scratch_shapes=[pltpu.VMEM((spans, rows, cols), jnp.bfloat16)],
        ),
        out_shape=[jax.ShapeDtypeStruct((CORES, rows, cols), jnp.bfloat16)] * lay.chips,
        compiler_params=params(12),
        cost_estimate=cost(3 * spans * rows * cols, 8 * spans * rows * cols),
        name="residual",
    )(table, *arrived, in_hbm(own), in_hbm(received))


def place_kernel(lay, chunks, table, *refs):
    out = refs[-1]
    chips = lay.chips
    group_rank = table[lay.group_rank]
    chip, core = lax.div(group_rank, CORES), lax.rem(group_rank, CORES)
    first = 0
    for c in range(chunks):
        same, swapped = refs[c * (chips + 1) : (c + 1) * (chips + 1) - 1], refs[(c + 1) * (chips + 1) - 1]
        rows, cols = swapped.shape[1:]
        for n, hop in enumerate(hop_order(chips)):
            owner = lax.rem(chip + chips - hop, chips) * CORES
            for block, at_core in ((same[n][0], core), (swapped[n], 1 - core)):
                at = pl.multiple_of((owner + at_core) * rows, rows)
                out[pl.ds(at, rows), first : first + cols] = block
        first += cols


def make_placed(lay, table, pieces, cols):
    flat = [x for same, swapped in pieces for x in [*same, swapped]]
    chips, rows, _ = pieces[0][1].shape
    shape = (chips * CORES * rows, cols)
    return pl.pallas_call(
        functools.partial(place_kernel, lay, len(pieces)),
        grid_spec=pltpu.PrefetchScalarGridSpec(
            num_scalar_prefetch=1,
            grid=(1,),
            in_specs=[pl.BlockSpec(x.shape, lambda n, t: (0, 0, 0)) for x in flat],
            out_specs=pl.BlockSpec(shape, lambda n, t: (0, 0)),
        ),
        out_shape=jax.ShapeDtypeStruct(shape, jnp.bfloat16),
        compiler_params=params(16),
        cost_estimate=cost(0, 4 * shape[0] * shape[1]),
        name="placed",
    )(table, *flat)


def rope_tables(earlier, span_len, first_row, rows, head):
    half = head // 2
    freqs = jnp.power(
        jnp.float32(rope_base), -jnp.arange(half, dtype=jnp.float32) * 2.0 / head
    )
    at = earlier[:, None] * span_len + first_row + jnp.arange(rows, dtype=jnp.int32)[None, :]
    angles = at.reshape(-1).astype(jnp.float32)[:, None] * freqs[None, :]
    cosine, sine = jnp.cos(angles), jnp.sin(angles)
    return (
        jnp.concatenate([cosine, cosine], axis=1),
        jnp.concatenate([-sine, sine], axis=1),
    )


def after(x, done):
    return lax.optimization_barrier((x, done))[0]


def shift(x, owners, hop, flip):
    chips = owners // CORES
    pairs = [
        (z * CORES + c, (z + hop) % chips * CORES + (c ^ flip))
        for z in range(chips)
        for c in range(CORES)
    ]
    return lax.ppermute(x, "group", pairs)


def local(
    hidden_in, ln_gain, wq, wk, wv, q_gain, key_norm_gain, wo,
    prompt_spans, span_source, span_target, page_slot,
):
    _, span_len, cols = hidden_in.shape
    tensor_size = lax.axis_size("tensor")
    owners = lax.axis_size("group")
    tensor_rank = lax.axis_index("tensor")
    group_rank = lax.axis_index("group")
    chips = owners // CORES
    head = q_gain.shape[0]
    rows = span_len // owners
    pages_each = span_len // PAGE_ROWS
    spans = span_source.shape[0]
    here = spans // PARTS
    most = min(spans - (prompt_spans.shape[0] - 1), spans // 2)
    kv_cols = wk.shape[1]
    paired = tensor_size == 2
    swap = [(0, 1), (1, 0)]
    lay = Layout(spans, spans * pages_each, owners)

    if kv_cols < head:
        share = head // kv_cols
        sets = [list(range(i, i + share)) for i in range(0, tensor_size, share)]
        wk, wv = [
            lax.all_gather(w, "tensor", axis=1, tiled=True, axis_index_groups=sets)
            for w in (wk, wv)
        ]
    per_kv = wq.shape[1] // max(head, wk.shape[1])

    chip, core = group_rank // CORES, group_rank % CORES
    split = hidden_in.reshape(owners, rows, cols)

    def rows_for(hop, flip):
        to = lax.rem(chip + hop, chips) * CORES + lax.rem(core + flip, CORES)
        return lax.dynamic_index_in_dim(split, to, 0, keepdims=False)

    cross = lambda x: lax.ppermute(x, "tensor", swap)

    hops = hop_order(chips)
    paired_hops = hops[2:]
    near = [rows_for(hop, flip) for hop in hops[1:2] for flip in range(CORES)]
    near = [shift(x, owners, hops[1], flip) for flip, x in enumerate(near)]
    swapped = shift(
        jnp.stack([rows_for(hop, 1) for hop in hops[:1] + paired_hops]), owners, 0, 1
    )
    arrived = [rows_for(0, 0), swapped[0]] + near
    moves = []
    for n, hop in enumerate(paired_hops):
        pair = [rows_for(hop, 0), swapped[1 + n]]
        if n < len(paired_hops) - 1:
            moves.append((hop, jnp.concatenate(pair)))
        else:
            moves += [(hop, block) for block in pair]

    ranks = jnp.stack([group_rank, tensor_rank]).astype(jnp.int32)
    table = make_tables(
        lay, spans, spans * pages_each, ranks, prompt_spans, span_source, span_target, page_slot
    )
    earlier = table[lay.earlier_at : lay.earlier_at + spans]
    cosine, sine = rope_tables(earlier, span_len, group_rank * rows, rows, head)

    crossed = [cross(x) for x in arrived] if paired else []
    if paired:
        gain = ln_gain[None]
        gains = [gain, cross(after(gain, swapped))]
    else:
        gains = [lax.all_gather(ln_gain, "tensor", axis=0, tiled=True)[None]]

    kvs, norms = [], []

    def make_part(own_rows, crossed_rows):
        if paired:
            xs = [own_rows, [in_hbm(x) for x in crossed_rows]]
        else:
            xs = [[lax.all_gather(jnp.concatenate(own_rows), "tensor", axis=1, tiled=True)]]
        *normed, kv = make_kv(
            lay, table, xs, gains, wk, wv, key_norm_gain[None], cosine, sine, len(kvs)
        )
        kvs.append([kv.reshape(2, here, rows, kv.shape[2])])
        norms.append(normed)

    def one_back(p, done=()):
        kvs[p].append(shift(after(kvs[p][-1], done), owners, 1, 0))

    begun = 0
    for n in range(len(moves) + 1):
        if n:
            hop, block = moves[n - 1]
            if paired:
                landed = arrived[-1:] if n > 1 else near
                matching = crossed[2 * n - 2 : 2 * n] if n < 3 else crossed[n + 1]
                block = after(block, (landed, matching, gains))
            arrived.append(shift(block, owners, hop, 0))
            if paired:
                block = arrived[-1]
                if n == len(moves) and kvs:
                    block = after(block, kvs[0][0])
                crossed.append(cross(block))
        if sum(x.shape[0] for x in arrived[begun:]) == here * rows:
            make_part(arrived[begun:], crossed[begun:])
            begun = len(arrived)
            for _ in range(min(2, chips - 1) if len(kvs) == 1 else min(1, chips - 1)):
                one_back(len(kvs) - 1)

    queries, done = [], kvs[1][0]
    for p in range(PARTS):
        made = make_q(
            lay, table, norms[p], wq, after(q_gain[None], done), cosine, sine, p
        )
        queries.append(made.reshape(here, rows, made.shape[1]))
        done = queries[-1]
    for p in range(PARTS):
        while len(kvs[p]) < chips:
            one_back(p, queries[p])
    gathered = []
    for back in range(chips):
        gathered.append([kv[back] for kv in kvs])
        gathered.append([shift(kv[back], owners, 0, 1) for kv in kvs])

    own_kv = wk.shape[1] // head
    sets = [own_kv // 2] * 2 if own_kv % 2 == 0 else [1] * own_kv
    attended, pages, first = [], [], 0
    for count in sets:
        made, cut = make_attention(
            lay, most, table, queries, gathered, per_kv, head, pages_each, first, count
        )
        attended.append(made.reshape(spans * rows, -1))
        pages.append(cut)
        first += count

    if paired:
        tile = 512 if cols % 512 == 0 else cols
        tiles = cols // tile
        widths = [2, 2, 1] if tiles == 5 else [tiles]
        others = [cross(pages[0])]
        project = functools.partial(make_projection, lay, table, attended, wo, tile)
        send = project(lambda r: (1 - r) * tiles, widths[:1], "send_part", (others[0],))
        if widths[1:]:
            send += project(
                lambda r: (1 - r) * tiles + widths[0], widths[1:], "send_part", (send[0],)
            )
        own = project(lambda r: r * tiles, widths, "own_part", (send[-1],))
        pieces, received, landed, first = [], [], [], 0
        for n, sent in enumerate(send):
            if n:
                sent = after(sent, (received[-1], own, landed[-2:-1]))
            received.append(cross(sent))
            moved = make_sum(
                lay, table, arrived, own[n].reshape(spans, rows, -1),
                received[-1].reshape(spans, rows, -1), first,
            )
            same = [
                shift(x, owners, hop, 0) if hop else x
                for hop, x in zip(hop_order(chips), moved)
            ]
            landed.append(same)
            pieces.append(same)
            first += sent.shape[1]
        others += [cross(after(cut, moved[0])) for cut in pages[1:]]
        low = [jnp.where(tensor_rank == 0, a, b) for a, b in zip(pages, others)]
        high = [jnp.where(tensor_rank == 0, b, a) for a, b in zip(pages, others)]
        cache = jnp.concatenate(low + high, axis=3)
        for n, same in enumerate(pieces):
            flipped = jnp.concatenate([x[1:] for x in same])
            if n == len(pieces) - 2:
                flipped = after(flipped, others)
            pieces[n] = (same, shift(flipped, owners, 0, 1))
        mixed = make_placed(lay, after(table, cache), pieces, cols).reshape(1, span_len, cols)
    else:
        pages = jnp.concatenate(pages, axis=3)
        attended = jnp.concatenate(attended, axis=1)
        if kv_cols < head:
            pages = lax.dynamic_slice_in_dim(
                pages, lax.rem(tensor_rank, head // kv_cols) * kv_cols, kv_cols, 3
            )
        cache = lax.all_gather(pages, "tensor", axis=3, tiled=True)
        partial = jnp.dot(attended, wo, preferred_element_type=jnp.float32)
        summed = lax.psum_scatter(
            partial.astype(jnp.bfloat16), "tensor", scatter_dimension=1, tiled=True
        )
        summed = summed.reshape(spans, rows, cols).astype(jnp.float32)
        x = jnp.concatenate(arrived).reshape(spans, rows, cols).astype(jnp.float32)
        moved = (x + summed).astype(jnp.bfloat16)
        targets = table[lay.target_at : lay.target_at + spans]
        moved = jnp.zeros_like(moved).at[targets].set(moved, unique_indices=True)
        moved = lax.all_to_all(moved, "group", split_axis=0, concat_axis=0, tiled=True)
        mixed = moved.reshape(1, span_len, cols)
    return (mixed, cache)


def solution(mesh):
    in_specs = (
        P(("replica", "group"), None, "tensor"),
        P("tensor"),
        P(None, "tensor"),
        P(None, "tensor"),
        P(None, "tensor"),
        P(),
        P(),
        P("tensor", None),
        P("replica"),
        P("replica"),
        P("replica"),
        P("replica"),
    )
    out_specs = (P(("replica", "group"), None, "tensor"), P(("replica", "group"), None, None, None))
    return jax.shard_map(local, mesh=mesh, in_specs=in_specs, out_specs=out_specs, check_vma=False)
```
